32 devices in a mesh: dp: 8 (over z, x), expert: 4 (over y, core).
Axes of the slice: x: 2, y: 2, z: 4, core: 2. Of those that a mesh axis runs over, the one named last changes fastest.
Arguments:
- hidden_in: bfloat16 [16, 1024, 1536], P('dp', 'expert'), may hold values from -6 to 6
- cotangent: bfloat16 [16, 1024, 1536], P('dp', 'expert'), may hold values from -6 to 6
- norm_attn: float32 [1536], replicated, may hold values from 0.5 to 1.5
- w_query: bfloat16 [1536, 1536], replicated, may hold values from -0.15625 to 0.15625
- w_key: bfloat16 [1536, 256], replicated, may hold values from -0.15625 to 0.15625
- w_value: bfloat16 [1536, 256], replicated, may hold values from -0.15625 to 0.15625
- w_out: bfloat16 [1536, 1536], replicated, may hold values from -2 to 2
- norm_ffn: float32 [1536], replicated, may hold values from 0.5 to 1.5
- w_router: bfloat16 [1536, 32], replicated, may hold values from -0.078125 to 0.078125
- w_gate: bfloat16 [32, 1536, 768], P('expert'), may hold values from -0.15625 to 0.15625
- w_up: bfloat16 [32, 1536, 768], P('expert'), may hold values from -0.15625 to 0.15625
- w_down: bfloat16 [32, 768, 1536], P('expert'), may hold values from -0.4375 to 0.4375
- expert_ids: int32 [32, 2, 256, 4], P(('dp', 'expert')), may hold values from 0 to 31, all different within a row; in each aligned block of 512 rows (0 to 511, 512 to 1023, ..., all dimensions but the last counted through in order) at most 80 rows name the same one
- priority: int32 [32, 2, 256], P(('dp', 'expert')), may hold values from 0 to 2047, as said below
- prefix: int32 [16], P('dp'), may hold values from 102 to 512
Outputs:
- output: bfloat16 [16, 1024, 1536], P('dp', 'expert')
- d_hidden: float32 [16, 1024, 1536], P('dp', 'expert')
- d_norm_attn: float32 [1536], replicated
- d_w_query: float32 [1536, 1536], P('dp', 'expert')
- d_w_key: float32 [1536, 256], P('dp', 'expert')
- d_w_value: float32 [1536, 256], P('dp', 'expert')
- d_w_out: float32 [1536, 1536], P('dp', 'expert')
- d_norm_ffn: float32 [1536], replicated
- d_w_router: float32 [1536, 32], replicated
- d_w_gate: float32 [32, 1536, 768], P('expert', 'dp')
- d_w_up: float32 [32, 1536, 768], P('expert', 'dp')
- d_w_down: float32 [32, 768, 1536], P('expert', 'dp')
The draws below stay inside these ranges and needn't reach their ends.
Inputs may be any that keep to these rules, and one draw needn't show every extreme that they name: `expert_ids`: each token names 4 different experts; among the rows of one device no expert is named by more than 80 rows, a bound that some block reaches. `priority`: within each group (the 4 blocks of one index of dp) the values are a permutation of 0 to 2047. `prefix`: one per sequence.
All inputs are finite; a program needn't handle non-finite values.
Results may differ from the reference program's by a relative error of at most 0.024.
Values may be sent and summed in bfloat16 or wider, within the bound.
No kernel may reach another device: no remote copies, remote signals or barrier semaphores. Data moves between devices by JAX's collectives and lax.ppermute only.
A program may use at most 384 MiB of HBM per device.

```python
import math
import jax
import jax.numpy as jnp
import numpy as np
from jax import lax

D = 1536
QH = 12
KVH = 2
HD = 128
EXPERTS = 32
FF = 768
TOPK = 4
LEN = 1024
GSEQ = 2
SEQS = 16
SPAN = 256
TOK_DEV = 512
GT = 2048
QD = 1536
KD = 256
SLOTS = 80
CAP = 288
BLOCKS = 32
N_DP = 8
N_EXPERT = 4


def draw_priority(key, part):
    key = jax.random.fold_in(key, 7)
    group_keys = jax.random.split(key, N_DP)
    orders = jax.vmap(lambda k: jax.random.permutation(k, GT))(group_keys)
    return orders.astype(jnp.int32).reshape(N_DP * N_EXPERT, GSEQ, SPAN)


def set_ends(array, key, least, top_value):
    longest = array.shape.index(max(array.shape))
    spots = []
    for shift in (0, 1):
        where = [jax.random.randint(jax.random.fold_in(key, axis), (), 0, length) for axis, length in enumerate(array.shape)]
        where[longest] = (where[longest] + shift) % array.shape[longest]
        spots.append(tuple(where))
    return array.at[spots[0]].set(least).at[spots[1]].set(top_value)


def with_spikes(entries, rng, source, target, parts, factor):
    def block_of(position):
        return (jnp.arange(entries.shape[position]) // (entries.shape[position] // parts)).reshape((-1,) + (1,) * (entries.ndim - 1 - position))

    one_side = jax.random.permutation(rng, parts)[block_of(target)]
    far = (block_of(target) + parts // 2) % parts
    return jnp.where((block_of(source) == one_side) | (block_of(source) == far), factor * entries, entries)


def block_scale(stream_key, shape, cuts, least, largest):
    loudness, own = 1.0, jax.random.fold_in(stream_key, 6)
    for axis_at, shards_of in cuts:
        steps = jnp.exp(jax.random.uniform(jax.random.fold_in(own, axis_at), (shards_of,), jnp.float32, least / len(cuts), largest / len(cuts)))
        loudness = loudness * jnp.repeat(steps, shape[axis_at] // shards_of).reshape([-1 if axis == axis_at else 1 for axis in range(len(shape))])
    return loudness


def routed_block(stream_key, own, number, rows, amount, top, bound, skew):
    order = jax.random.permutation(stream_key, amount)
    packed, usual = load_shares(amount, rows * top, bound, skew, True), load_shares(amount, rows * top, bound, skew, False)
    places = jnp.arange(amount)

    def named(sizes, rotation):
        used = int((sizes > 0).sum())
        fixed = max(1, used // 4)
        moved = fixed + (places - fixed + rotation * (used - fixed)) % max(1, amount - fixed)
        return jnp.zeros((amount,), jnp.int32).at[order[jnp.where(places < fixed, places, moved)]].set(jnp.asarray(sizes, jnp.int32))

    sizes = jnp.where(number % 4 == 0, named(packed, number // 4), named(usual, number - number // 4 - 1))
    mixed = jax.random.permutation(jax.random.fold_in(own, 3), amount)
    source_of, receiver = mixed[0:amount // 2 * 2:2], mixed[1:amount // 2 * 2:2]
    margin = jnp.minimum(sizes[source_of] - 1, bound - sizes[receiver]) // 2
    margin = jnp.where((source_of == order[0]) | (receiver == order[0]) | (sizes[receiver] == 0), 0, jnp.maximum(margin, 0))
    moved = jax.random.randint(jax.random.fold_in(own, 4), (amount // 2,), 0, 1 << 20) % (margin + 1)
    sizes = sizes.at[source_of].add(-moved).at[receiver].add(moved)
    members = jnp.searchsorted(jnp.cumsum(sizes), jnp.arange(rows * top), side="right").astype(jnp.int32)
    grid = members.reshape(top, rows).T
    grid = grid[jax.random.permutation(jax.random.fold_in(own, 1), rows)]
    rotation = jax.random.randint(jax.random.fold_in(own, 2), (rows, 1), 0, top)
    return jnp.take_along_axis(grid, (jnp.arange(top)[None, :] + rotation) % top, axis=1)


def load_shares(number_of, total, limit, skew, full):
    weights = [(1 << 20) // math.isqrt(standing ** skew) + 1 for standing in range(1, number_of + 1)]
    largest = limit if full else min(limit, max(-(-total // number_of), total * weights[0] // sum(weights)))
    least = 1 if total - largest >= number_of - 1 else 0
    counts, surplus = [largest] + [least] * (number_of - 1), total - largest - least * (number_of - 1)
    while surplus > 0:
        free = [i for i in range(1, number_of) if counts[i] < largest] or [i for i in range(1, number_of) if counts[i] < limit]
        whole, left = sum([weights[i] for i in free]), surplus
        for i in free:
            extra = min(limit - counts[i], max(1, left * weights[i] // whole), surplus)
            counts[i] = counts[i] + extra
            surplus = surplus - extra
    return np.array(counts)


def gaussian(own_key, shape, scale, reach, cuts=(), kind=jnp.bfloat16):
    drawn = jax.random.normal(own_key, shape, jnp.float32) * scale
    if len(cuts) > 0:
        drawn = block_scale(own_key, shape, cuts, -0.22, 0.18) * drawn
    return jnp.clip(drawn, min=-reach, max=reach).astype(kind)


def gaussian_with(rng, shape, width, most, cuts, heavy, held_as=jnp.bfloat16):
    values = width * jax.random.normal(rng, shape, jnp.float32)
    if cuts:
        values = values * block_scale(rng, shape, cuts, -0.22, 0.18)
    return jnp.clip(with_spikes(values, jax.random.fold_in(rng, 3), *heavy), -most, most).astype(held_as)


def setup_inputs(seed: int = 0) -> dict:
    key_of = jax.random.split(jax.random.key(seed), 16)
    hidden_in = gaussian(key_of[0], (SEQS, LEN, D), 1.0, 6.0, ((0, 8), (1, 4)))
    cotangent = gaussian_with(key_of[1], (SEQS, LEN, D), 1.0, 6.0, ((0, 8), (1, 4)), (0, 2, 8, 2.0))
    norm_attn = jnp.clip(1.0 + 0.1 * jax.random.normal(key_of[2], (D,), jnp.float32), 0.5, 1.5)
    w_query = gaussian(key_of[3], (D, QD), D ** -0.5, 0.15625)
    w_key = gaussian(key_of[4], (D, KD), D ** -0.5, 0.15625)
    w_value = gaussian(key_of[5], (D, KD), D ** -0.5, 0.15625)
    w_out = gaussian(key_of[6], (QD, D), 8 ** -0.5, 2.0)
    norm_ffn = jnp.clip(1.0 + 0.1 * jax.random.normal(key_of[7], (D,), jnp.float32), 0.5, 1.5)
    w_router = gaussian(key_of[8], (D, EXPERTS), (4 * D) ** -0.5, 0.078125)
    w_gate = gaussian(key_of[9], (EXPERTS, D, FF), D ** -0.5, 0.15625, ((0, 4),))
    w_up = gaussian(key_of[10], (EXPERTS, D, FF), D ** -0.5, 0.15625, ((0, 4),))
    w_down = gaussian(key_of[11], (EXPERTS, FF, D), (FF // 4) ** -0.5, 0.4375, ((0, 4),))
    expert_ids_keys = jax.random.split(jax.random.fold_in(key_of[12], 1), BLOCKS * GSEQ * SPAN // TOK_DEV)
    expert_ids_turns = jax.random.permutation(jax.random.fold_in(key_of[12], 3), BLOCKS * GSEQ * SPAN // TOK_DEV)
    expert_ids = jax.vmap(lambda own, number: routed_block(jax.random.fold_in(key_of[12], 2), own, number, TOK_DEV, EXPERTS, TOPK, SLOTS, 1))(expert_ids_keys, expert_ids_turns).reshape((BLOCKS, GSEQ, SPAN, TOPK))
    priority = draw_priority(jax.random.fold_in(key_of[15], 71), 0)
    prefix = set_ends(jax.random.randint(key_of[14], (SEQS,), LEN // 10, LEN // 2 + 1), jax.random.fold_in(key_of[14], 1), LEN // 10, (LEN // 2 + 1) - 1).astype(jnp.int32)
    return {"hidden_in": hidden_in, "cotangent": cotangent, "norm_attn": norm_attn, "w_query": w_query, "w_key": w_key, "w_value": w_value, "w_out": w_out, "norm_ffn": norm_ffn, "w_router": w_router, "w_gate": w_gate, "w_up": w_up, "w_down": w_down, "expert_ids": expert_ids, "priority": priority, "prefix": prefix}


EPSILON = 1e-06
ROPE_BASE = 10000.0
MASKED = -1e+30
PRECISE = lax.Precision.HIGHEST

@jax.custom_vjp
def low(v):
    return lax.optimization_barrier(v.astype(jnp.bfloat16)).astype(jnp.float32)

@jax.custom_vjp
def low_back(v):
    return v

def low_keep(v):
    return (low(v), None)

def low_pass(kept, grad):
    return (grad,)

def back_keep(v):
    return (v, None)

def back_low(kept, grad):
    return (low(grad),)
low.defvjp(low_keep, low_pass)
low_back.defvjp(back_keep, back_low)

def rms_scale(values):
    return lax.rsqrt(lax.optimization_barrier(jnp.mean(values * values, axis=-1, keepdims=True)) + EPSILON)

def rope_tables(length, offset):
    positions = (offset + jnp.arange(length, dtype=jnp.int32)).astype(jnp.float32)
    frequency = ROPE_BASE ** (-(jnp.arange(HD // 2, dtype=jnp.float32) * 2.0 / HD))
    angles = positions[:, None] * frequency[None, :]
    return (jnp.cos(angles), jnp.sin(angles))

def rotate(values, cos_table, sin_table):
    half_size = values.shape[-1] // 2
    first_half = values[..., :half_size]
    second = values[..., half_size:]
    cos_part = cos_table[:, None, :]
    sin_part = sin_table[:, None, :]
    return jnp.concatenate([first_half * cos_part - second * sin_part, second * cos_part + first_half * sin_part], axis=-1)

def attend_one(pieces):
    queries, key_rows, values, prefix_len = pieces
    group_ratio = QH // KVH
    grouped = queries.reshape(LEN, KVH, group_ratio, HD)
    scores = jnp.einsum('ikrd,jkd->krij', grouped, key_rows, precision=PRECISE) * HD ** (-0.5)
    scores = low_back(scores)
    places = jnp.arange(LEN, dtype=jnp.int32)
    allowed = (places[None, :] <= places[:, None]) | (places[None, :] < prefix_len)
    scores = jnp.where(allowed, scores, MASKED)
    row_max = lax.optimization_barrier(jnp.max(scores, axis=-1, keepdims=True))
    weights = jnp.exp(scores - row_max)
    attn_probs = low(weights / lax.optimization_barrier(jnp.sum(weights, axis=-1, keepdims=True)))
    attn_mix = jnp.einsum('krij,jkd->ikrd', attn_probs, values, precision=PRECISE)
    return attn_mix.reshape(LEN, QH, HD)

def group_slots(routes, order_rank):
    choice_hits = lax.optimization_barrier(jnp.sum((routes[:, :, None] == jnp.arange(EXPERTS, dtype=jnp.int32)).astype(jnp.int32), axis=1))
    ordered = jnp.zeros_like(choice_hits).at[order_rank].set(choice_hits)
    before = jnp.cumsum(ordered, axis=0) - ordered
    return jnp.take_along_axis(before[order_rank], routes, axis=1)

def group_forward(weights_all, hidden_group, routes, slot_index, starts):
    norm_attn, w_query, w_key, w_value, w_out, norm_ffn, w_router, w_gate, w_up, w_down = weights_all
    tokens = hidden_group.reshape(GT, D)
    normed = low(tokens * rms_scale(tokens) * norm_attn)
    cos_table, sin_table = rope_tables(LEN, 0)
    queries = low_back(jnp.dot(normed, w_query, precision=PRECISE)).reshape(GSEQ, LEN, QH, HD)
    key_rows = low_back(jnp.dot(normed, w_key, precision=PRECISE)).reshape(GSEQ, LEN, KVH, HD)
    values = low(low_back(jnp.dot(normed, w_value, precision=PRECISE))).reshape(GSEQ, LEN, KVH, HD)
    queries = low(rotate(queries, cos_table, sin_table))
    key_rows = low(rotate(key_rows, cos_table, sin_table))
    attn_mix = lax.map(jax.checkpoint(attend_one), (queries, key_rows, values, starts))
    attn_mix = low(low_back(attn_mix.reshape(GT, QD)))
    branch = low_back(jnp.dot(attn_mix, w_out, precision=PRECISE))
    residual = tokens + branch
    routed_in = low(residual * rms_scale(residual) * norm_ffn)
    logits = low_back(jnp.dot(routed_in, w_router, precision=PRECISE))
    chosen = jnp.take_along_axis(logits, routes, axis=1)
    exp_terms = jnp.exp(chosen - lax.optimization_barrier(jnp.max(chosen, axis=1, keepdims=True)))
    gate_probs = exp_terms / lax.optimization_barrier(jnp.sum(exp_terms, axis=1, keepdims=True))
    kept_mask = slot_index < CAP
    target = jnp.where(kept_mask, routes * CAP + slot_index, EXPERTS * CAP).reshape(-1).astype(jnp.int32)
    copies = low_back(jnp.repeat(routed_in, TOPK, axis=0))
    buffer = jnp.zeros((EXPERTS * CAP + 1, D), routed_in.dtype).at[target].add(copies)
    buffer = buffer[:-1].reshape(EXPERTS, CAP, D)
    gate_act = low_back(jnp.einsum('ecd,edf->ecf', buffer, w_gate, precision=PRECISE))
    up_act = low_back(jnp.einsum('ecd,edf->ecf', buffer, w_up, precision=PRECISE))
    hidden_act = low(jax.nn.gelu(gate_act, approximate=False) * up_act)
    result = low(low_back(jnp.einsum('ecf,efd->ecd', hidden_act, w_down, precision=PRECISE)))
    returned = jnp.concatenate([result.reshape(EXPERTS * CAP, D), jnp.zeros((1, D), result.dtype)], axis=0)
    picked = jnp.take(returned, target, axis=0).reshape(GT, TOPK, D)
    expert_sum = lax.optimization_barrier(jnp.sum(gate_probs[:, :, None] * picked, axis=1))
    return (residual + expert_sum).reshape(GSEQ, LEN, D)

def reference(hidden_in, cotangent, norm_attn, w_query, w_key, w_value, w_out, norm_ffn, w_router, w_gate, w_up, w_down, expert_ids, priority, prefix):
    weights_all = tuple((w.astype(jnp.float32) for w in (norm_attn, w_query, w_key, w_value, w_out, norm_ffn, w_router, w_gate, w_up, w_down)))
    routes_all = expert_ids.reshape(N_DP, N_EXPERT, GSEQ, SPAN, TOPK).transpose(0, 2, 1, 3, 4).reshape(N_DP, GT, TOPK).astype(jnp.int32)
    order_all = priority.reshape(N_DP, N_EXPERT, GSEQ, SPAN).transpose(0, 2, 1, 3).reshape(N_DP, GT).astype(jnp.int32)
    hidden_all = hidden_in.astype(jnp.float32).reshape(N_DP, GSEQ, LEN, D)
    upstream_all = cotangent.astype(jnp.float32).reshape(N_DP, GSEQ, LEN, D)
    starts_all = prefix.reshape(N_DP, GSEQ).astype(jnp.int32)

    def group_step(grad_total, pieces):
        hidden_group, upstream, routes, order_rank, starts = pieces
        slot_index = group_slots(routes, order_rank)

        def forward(hidden_value, weight_value):
            return group_forward(weight_value, hidden_value, routes, slot_index, starts)
        output, pullback = jax.vjp(forward, hidden_group, weights_all)
        d_hidden, d_weights = pullback(upstream)
        grad_total = jax.tree.map(lambda a, b: a + b, grad_total, d_weights)
        return (grad_total, (output, d_hidden))
    zero_grads = tuple((jnp.zeros_like(w) for w in weights_all))
    grad_total, (outputs, d_inputs) = lax.scan(group_step, zero_grads, (hidden_all, upstream_all, routes_all, order_all, starts_all))
    output = outputs.reshape(SEQS, LEN, D).astype(jnp.bfloat16)
    d_hidden = d_inputs.reshape(SEQS, LEN, D)
    return (output, d_hidden, grad_total[0], grad_total[1], grad_total[2], grad_total[3], grad_total[4], grad_total[5], grad_total[6], grad_total[7], grad_total[8], grad_total[9])
```

```python
import functools

import jax
import jax.numpy as jnp
from jax import lax
from jax.experimental import pallas as pl
from jax.experimental.pallas import tpu as pltpu
from jax.sharding import PartitionSpec as P

HD = 128
EPSILON = 1e-06
ROPE_BASE = 10000.0
MASKED = -1e30
EXTRA = 16
TEAM_BIT = 2
VMEM_LIMIT = 60 * 1024 * 1024

BF16 = jnp.bfloat16
F32 = jnp.float32


def dot(a, b):
    return jnp.dot(a, b, preferred_element_type=F32)


def dot_nt(a, b):
    return lax.dot_general(a, b, (((1,), (1,)), ((), ())), preferred_element_type=F32)


def dot_tn(a, b):
    return lax.dot_general(a, b, (((0,), (0,)), ((), ())), preferred_element_type=F32)


def bits_of(size):
    return [1 << i for i in reversed(range(size.bit_length() - 1))]


def swap(values, axis_name, bit):
    count = lax.axis_size(axis_name)
    return lax.ppermute(values, axis_name, [(i, i ^ bit) for i in range(count)])


def gather_pieces(values, steps):
    pieces = [values]
    for axis_name, bit in steps:
        pieces = pieces + [swap(piece, axis_name, bit) for piece in pieces]
    return pieces


def add_pair(a, b):
    return (a.astype(F32) + b.astype(F32)).astype(BF16)


def scatter_pieces(pieces, steps):
    for axis_name, bit in reversed(steps):
        half = len(pieces) // 2
        pieces = [
            add_pair(a, swap(b, axis_name, bit))
            for a, b in zip(pieces[:half], pieces[half:], strict=True)
        ]
    return pieces[0]


def all_sum(values, axes):
    for axis_name in axes:
        for bit in reversed(bits_of(lax.axis_size(axis_name))):
            values = values + swap(values, axis_name, bit)
    return values


ANYWHERE = pl.BlockSpec(memory_space=pl.ANY)


TIME_SCALE = 1.0


def kernel_call(us, body, grid, ins, outs, scalars=(), scratch=(), after=(), aliases=None):
    after = list(after)
    lead, held = len(scalars), len(ins)

    def run(*refs):
        body(*refs[: lead + held], *refs[lead + held + len(after) :])

    grid_spec = pltpu.PrefetchScalarGridSpec(
        num_scalar_prefetch=lead,
        grid=grid,
        in_specs=[spec for _, spec in ins] + [ANYWHERE] * len(after),
        out_specs=[spec for _, spec in outs],
        scratch_shapes=list(scratch),
    )
    return pl.pallas_call(
        run,
        grid_spec=grid_spec,
        out_shape=[shape for shape, _ in outs],
        input_output_aliases=aliases or {},
        compiler_params=pltpu.CompilerParams(vmem_limit_bytes=VMEM_LIMIT),
        cost_estimate=pl.CostEstimate(
            flops=int(us * TIME_SCALE * 1e9),
            bytes_accessed=int(us * TIME_SCALE * 3.3e6),
            transcendentals=0,
        ),
    )(*scalars, *[a for a, _ in ins], *after)


def shaped(shape, dtype):
    return jax.ShapeDtypeStruct(tuple(shape), dtype)


def whole(array):
    zeros = (0,) * len(array.shape)
    return pl.BlockSpec(tuple(array.shape), lambda *_: zeros)


def rms_of(values):
    return lax.rsqrt(jnp.mean(values * values, axis=-1, keepdims=True) + EPSILON)


def turn(values, cos_wide, sin_wide):
    return values * cos_wide + pltpu.roll(values, HD // 2, 1) * sin_wide


def column(width, tile):
    return pl.ds(pl.multiple_of(width * tile, tile), tile)


def hold_body(value_ref, out_ref):
    pass


def hold(value, after):
    return kernel_call(
        0.5, hold_body, (1,), [(value, ANYWHERE)], [(shaped(value.shape, value.dtype), ANYWHERE)],
        after=after, aliases={0: 0},
    )[0]


def key_value_body(x_ref, gain, wk, wv, cos_ref, sin_ref, cot_ref, normed_ref, kv_ref, same_ref):
    x = x_ref[...].astype(F32)
    normed = (x * rms_of(x) * gain[...]).astype(BF16)
    normed_ref[...] = normed
    keys = dot(normed, wk[...])
    for h in range(keys.shape[1] // HD):
        cols = slice(h * HD, (h + 1) * HD)
        kv_ref[:, cols] = turn(keys[:, cols], cos_ref[...], sin_ref[...]).astype(BF16)
    kv_ref[:, keys.shape[1] :] = dot(normed, wv[...]).astype(BF16)


def query_body(normed_ref, wq, cos_ref, sin_ref, q_ref):
    queries = dot(normed_ref[...], wq[...])
    for h in range(queries.shape[1] // HD):
        cols = slice(h * HD, (h + 1) * HD)
        q_ref[:, cols] = turn(queries[:, cols], cos_ref[...], sin_ref[...]).astype(BF16)


def project_inputs(x, gain, wq, wk, wv, cos_wide, sin_wide, cot):
    rows, width = x.shape
    kd = wk.shape[1]
    normed, kv, cot = kernel_call(
        4.2,
        key_value_body,
        (1,),
        [(a, whole(a)) for a in (x, gain, wk, wv, cos_wide, sin_wide)] + [(cot, ANYWHERE)],
        [(s, whole(s)) for s in (shaped((rows, width), BF16), shaped((rows, 2 * kd), BF16))]
        + [(shaped(cot.shape, BF16), ANYWHERE)],
        aliases={6: 2},
    )
    tile = 256

    def queries(after):
        return kernel_call(
            8,
            query_body,
            (wq.shape[1] // tile,),
            [
                (normed, whole(normed)),
                (wq, pl.BlockSpec((width, tile), lambda i: (0, i))),
                (cos_wide, whole(cos_wide)),
                (sin_wide, whole(sin_wide)),
            ],
            [(shaped((rows, wq.shape[1]), BF16), pl.BlockSpec((rows, tile), lambda i: (0, i)))],
            after=after,
        )[0]

    return normed, kv, queries, cot


def attention_bias(prefix, source, offset, span, members):
    rows = offset + lax.broadcasted_iota(jnp.int32, (span, span), 0)
    cols = lax.broadcasted_iota(jnp.int32, (span, span), 1)
    parts = []
    for p in range(members):
        keys = source[p] * span + cols
        parts.append(jnp.where((keys <= rows) | (keys < prefix), 0.0, MASKED))
    return jnp.concatenate(parts, axis=1)


def attention_body(members, kvh, ratio, prefix, source, q_ref, *refs):
    pieces, (mix_ref, lse_ref, bias) = refs[:members], refs[members:]
    span = q_ref.shape[1]
    scale = HD ** (-0.5)
    bias[...] = attention_bias(prefix[pl.program_id(0)], source, source[members], span, members)
    columns = []
    for k in range(kvh):
        keys = jnp.concatenate([p[0, :, k * HD : (k + 1) * HD] for p in pieces], axis=0)
        start = (kvh + k) * HD
        values = jnp.concatenate([p[0, :, start : start + HD] for p in pieces], axis=0)
        for r in range(ratio):
            cols = slice((k * ratio + r) * HD, (k * ratio + r + 1) * HD)
            scores = dot_nt(q_ref[0, :, cols], keys) + bias[...]
            top = jnp.max(scores, axis=1, keepdims=True)
            terms = jnp.exp((scores - top) * scale)
            total = jnp.sum(terms, axis=1, keepdims=True)
            mixed = dot(terms.astype(BF16), values)
            mix_ref[0, :, cols] = (mixed / total).astype(BF16)
            columns.append(top * scale + jnp.log(total))
    lse_ref[0] = jnp.concatenate(columns, axis=1)


def attention_back_body(
    members, kvh, ratio, prefix, source, q_ref, do_ref, lse_ref, cos_ref, sin_ref, *refs
):
    pieces, dq_ref = refs[:members], refs[members]
    outs, (bias, dk, dv) = refs[members + 1 : 2 * members + 1], refs[2 * members + 1 :]
    span = q_ref.shape[1]
    scale = HD ** (-0.5)
    bias[...] = attention_bias(prefix[pl.program_id(0)], source, source[members], span, members)
    for k in range(kvh):
        keys = jnp.concatenate([p[0, :, k * HD : (k + 1) * HD] for p in pieces], axis=0)
        start = (kvh + k) * HD
        values = jnp.concatenate([p[0, :, start : start + HD] for p in pieces], axis=0)
        for r in range(ratio):
            h = k * ratio + r
            cols = slice(h * HD, (h + 1) * HD)
            query, upstream = q_ref[0, :, cols], do_ref[0, :, cols]
            scores = dot_nt(query, keys) + bias[...]
            probs = jnp.exp(scores * scale - lse_ref[0, :, h : h + 1])
            d_probs = dot_nt(upstream, values)
            mean = jnp.sum(probs * d_probs, axis=1, keepdims=True)
            d_scores = (probs * (d_probs - mean)).astype(BF16)
            d_query = dot(d_scores, keys) * scale
            dq_ref[0, :, cols] = turn(d_query, cos_ref[...], -sin_ref[...]).astype(BF16)
            part_k = dot_tn(d_scores, query)
            part_v = dot_tn(probs.astype(BF16), upstream)
            if r == 0:
                dk[...] = part_k
                dv[...] = part_v
            else:
                dk[...] += part_k
                dv[...] += part_v
        for p, out in enumerate(outs):
            rows = slice(p * span, (p + 1) * span)
            out[0, :, k * HD : (k + 1) * HD] = (dk[rows, :] * scale).astype(BF16)
            out[0, :, start : start + HD] = dv[rows, :].astype(BF16)


def attend(q, kv, prefix, source):
    groups, span, qd = q.shape
    members, kvh = len(kv), kv[0].shape[2] // (2 * HD)
    heads = qd // HD
    block = lambda n: pl.BlockSpec((1, span, n), lambda g, *_: (g, 0, 0))
    return kernel_call(
        15.7,
        functools.partial(attention_body, members, kvh, heads // kvh),
        (groups,),
        [(q, block(qd))] + [(p, block(p.shape[2])) for p in kv],
        [
            (shaped(q.shape, BF16), block(qd)),
            (shaped((groups, span, heads), F32), block(heads)),
        ],
        scalars=(prefix, source),
        scratch=[pltpu.VMEM((span, span * members), F32)],
    )


def attend_back(q, do, lse, kv, prefix, source, cos_wide, sin_wide, after=()):
    groups, span, qd = q.shape
    members, kvh = len(kv), kv[0].shape[2] // (2 * HD)
    heads = qd // HD
    block = lambda n: pl.BlockSpec((1, span, n), lambda g, *_: (g, 0, 0))
    outs = kernel_call(
        28.6,
        functools.partial(attention_back_body, members, kvh, heads // kvh),
        (groups,),
        [(q, block(qd)), (do, block(qd)), (lse, block(heads))]
        + [(cos_wide, whole(cos_wide)), (sin_wide, whole(sin_wide))]
        + [(p, block(p.shape[2])) for p in kv],
        [(shaped(q.shape, BF16), block(qd))]
        + [(shaped(p.shape, BF16), block(p.shape[2])) for p in kv],
        scalars=(prefix, source),
        scratch=[
            pltpu.VMEM((span, span * members), F32),
            pltpu.VMEM((span * members, HD), F32),
            pltpu.VMEM((span * members, HD), F32),
        ],
        after=after,
    )
    return outs[0], outs[1:]


def branch_body(steps, x_ref, mix_ref, wo, gain, router, hit_ref,
                residual_ref, message_ref, gates_ref):
    i = pl.program_id(0)
    tile = wo.shape[1]
    cols = column(i, tile)
    residual_ref[:, cols] = x_ref[:, cols].astype(F32) + dot(mix_ref[...], wo[...])

    @pl.when(i == steps - 1)
    def _():
        rows = residual_ref.shape[0]
        experts = hit_ref.shape[0]
        h1 = residual_ref[...]
        a2 = (h1 * rms_of(h1) * gain[...]).astype(BF16)
        message_ref[:rows, :] = a2
        hit = hit_ref[...] > 0.0
        logits = jnp.where(hit, dot_nt(router[...], a2), MASKED)
        terms = jnp.exp(logits - jnp.max(logits, axis=0, keepdims=True))
        terms = jnp.where(hit, terms, 0.0)
        gates = terms / jnp.sum(terms, axis=0, keepdims=True)
        gates_ref[...] = gates
        high = gates.astype(BF16)
        rest = gates - high.astype(F32)
        middle = rest.astype(BF16)
        low = (rest - middle.astype(F32)).astype(BF16)
        message_ref[rows:, :rows] = high
        message_ref[rows:, rows : 2 * rows] = middle
        message_ref[rows:, 2 * rows : 3 * rows] = low
        if message_ref.shape[1] > 3 * rows:
            message_ref[rows:, 3 * rows :] = jnp.zeros(
                (experts, message_ref.shape[1] - 3 * rows), BF16
            )


def branch(x, mix, wo, gain, router_t, hit_t):
    rows, width = x.shape
    experts = router_t.shape[0]
    tile = 256
    outs = (
        shaped((rows, width), F32),
        shaped((rows + experts, width), BF16),
        shaped((experts, rows), F32),
    )
    return kernel_call(
        10,
        functools.partial(branch_body, width // tile),
        (width // tile,),
        [(x, whole(x)), (mix, whole(mix))]
        + [(wo, pl.BlockSpec((wo.shape[0], tile), lambda i: (0, i)))]
        + [(a, whole(a)) for a in (gain, router_t, hit_t)],
        [(s, whole(s)) for s in outs],
    )


def slot_masks(places, slot_count):
    experts, tokens = places.shape
    slots = lax.broadcasted_iota(jnp.int32, (slot_count, tokens), 0).astype(F32)
    return [places[e : e + 1, :] == slots for e in range(experts)]


def hot_rows(masks):
    return jnp.concatenate([m.astype(F32) for m in masks], axis=0).astype(BF16)


def pick_experts(table, first, count):
    row = lax.broadcasted_iota(jnp.int32, table.shape, 0)
    picked = [
        jnp.sum(jnp.where(row == first + e, table, 0.0), axis=0, keepdims=True)
        for e in range(count)
    ]
    return jnp.concatenate(picked, axis=0)


def places_body(blocks, count, capacity, first, table_ref, column_ref, out_ref):
    b = pl.program_id(0)
    tokens = table_ref.shape[2]
    top = table_ref.shape[1] - 1
    padded = 8

    def hits(at):
        row = lax.broadcasted_iota(jnp.int32, (padded, tokens), 0)
        expert = jnp.where(row < count, first[0] + row, -1)
        found = table_ref[at, 0:1, :] == expert
        for k in range(1, top):
            found = found | (table_ref[at, k : k + 1, :] == expert)
        return found

    own_order = table_ref[b, top : top + 1, :]
    before = jnp.zeros((padded, tokens), F32)
    for n in range(blocks // 2):
        at = 2 * n + b % 2
        earlier = jnp.where(column_ref[at] < own_order, 1.0, 0.0).astype(BF16)
        before = before + dot(jnp.where(hits(at), 1.0, 0.0).astype(BF16), earlier)
    kept = hits(b) & (before < capacity)
    row = lax.broadcasted_iota(jnp.int32, (tokens, tokens), 0)
    col = lax.broadcasted_iota(jnp.int32, (tokens, tokens), 1)
    ahead = jnp.where(row < col, 1.0, 0.0).astype(BF16)
    slots = dot(jnp.where(kept, 1.0, 0.0).astype(BF16), ahead)
    out_ref[0] = jnp.where(kept, slots, -1.0)[:count]


def find_places(tables, first, count, capacity, after=()):
    blocks, wide, tokens = tables.shape
    columns = tables[:, wide - 1, :, None]
    shape = shaped((blocks, count, tokens), F32)
    return kernel_call(
        4,
        functools.partial(places_body, blocks, count, capacity),
        (blocks,),
        [(tables, whole(tables)), (columns, whole(columns))],
        [(shape, pl.BlockSpec((1, count, tokens), lambda b, *_: (b, 0, 0)))],
        scalars=(first,),
        after=after,
    )[0]


def dispatch_body(parts, with_gates, slot_count, first, *refs):
    segments, refs = refs[:parts], refs[parts:]
    if with_gates:
        extra_ref, places_ref, rows_ref, gate_ref = refs
    else:
        places_ref, rows_ref = refs
    _, count, tokens = places_ref.shape
    masks = slot_masks(places_ref[0], slot_count)
    hot = hot_rows(masks)
    if with_gates:
        extra = extra_ref[...].astype(F32)
        table = extra[:, :tokens] + extra[:, tokens : 2 * tokens]
        gates = pick_experts(table + extra[:, 2 * tokens : 3 * tokens], first[0], count)
        for e in range(count):
            gate = jnp.sum(jnp.where(masks[e], gates[e : e + 1, :], 0.0), axis=1, keepdims=True)
            gate_ref[e] = jnp.broadcast_to(gate, (slot_count, 128))
    total, start = 0.0, 0
    for segment in segments:
        stop = min(start + segment.shape[0], tokens)
        total = total + dot(hot[:, start:stop], segment[: stop - start, :])
        start = stop
    total = total.astype(BF16)
    for e in range(count):
        rows_ref[e] = total[e * slot_count : (e + 1) * slot_count]


def dispatch(segments, at, places, first, slot_count, with_gates, after=()):
    width = segments[0].shape[1]
    _, count, tokens = places.shape
    ins = [(a, whole(a)) for a in segments]
    outs = [shaped((count, slot_count, width), BF16)]
    if with_gates:
        last = segments[-1]
        extra = last.shape[0] - (tokens - sum(a.shape[0] for a in segments[:-1]))
        spot = last.shape[0] // extra - 1
        ins.append((last, pl.BlockSpec((extra, width), lambda *_: (spot, 0))))
        outs.append(shaped((count, slot_count, 128), F32))
    ins.append((places, pl.BlockSpec((1, count, tokens), lambda *_: (at, 0, 0))))
    return kernel_call(
        1.5,
        functools.partial(dispatch_body, len(segments), with_gates, slot_count),
        (1,),
        ins,
        [(o, whole(o)) for o in outs],
        scalars=(first,),
        after=after,
    )


def combine_body(experts, with_extra, starts, cut, first, *refs):
    refs = list(refs)
    rows = [refs.pop(0) for _ in range(experts)]
    places_ref = refs.pop(0)
    slopes = [refs.pop(0) for _ in range(experts)] if with_extra else None
    added = [refs.pop(0) for _ in starts]
    outs = refs
    slot_count = rows[0].shape[1]
    tokens = places_ref.shape[2]
    masks = slot_masks(places_ref[0], slot_count)
    values = jnp.concatenate([r[0] for r in rows], axis=0)
    total = dot_tn(hot_rows(masks), values)
    last = outs[-1]
    width = last.shape[1]
    for other, start in zip(added, starts, strict=True):
        count = min(other.shape[0], tokens - start)
        parts = [total[start : start + count] + other[:count, :].astype(F32)]
        if start > 0:
            parts = [total[:start]] + parts
        if start + count < tokens:
            parts.append(total[start + count :])
        total = parts[0] if len(parts) == 1 else jnp.concatenate(parts, axis=0)
    total = total.astype(BF16)
    if cut:
        outs[0][...] = total[:cut]
    last[: tokens - cut, :] = total[cut:]
    if with_extra:
        count = last.shape[0] - (tokens - cut)
        row = lax.broadcasted_iota(jnp.int32, (count, tokens), 0)
        table = jnp.zeros((count, tokens), F32)
        for e in range(experts):
            slope = jnp.sum(jnp.where(masks[e], slopes[e][0, :, :1], 0.0), axis=0, keepdims=True)
            table = jnp.where(row == first[0] + e, slope, table)
        high = table.astype(BF16).astype(F32)
        for side, value in enumerate((high, table - high)):
            cols = slice(side * tokens, (side + 1) * tokens)
            for other, start in zip(added, starts, strict=True):
                if start + other.shape[0] > tokens:
                    value = value + other[tokens - start :, cols].astype(F32)
            last[tokens - cut :, cols] = value.astype(BF16)
        last[tokens - cut :, 2 * tokens :] = jnp.zeros((count, width - 2 * tokens), BF16)


def combine(rows, at, places, slopes, first, added, cut, extra, after=()):
    experts = len(rows)
    _, slot_count, width = rows[0].shape
    _, count, tokens = places.shape
    block = lambda n: pl.BlockSpec((1, slot_count, n), lambda *_: (at, 0, 0))
    ins = [(r, block(width)) for r in rows]
    ins.append((places, pl.BlockSpec((1, count, tokens), lambda *_: (at, 0, 0))))
    if slopes is not None:
        ins += [(s, block(128)) for s in slopes]
    ins += [(a, whole(a)) for a, _ in added]
    long = tokens + (extra if slopes is not None else 0)
    outs = [shaped((cut, width), BF16)] if cut else []
    outs.append(shaped((long - cut, width), BF16))
    starts = tuple(start for _, start in added)
    return kernel_call(
        1.2,
        functools.partial(combine_body, experts, slopes is not None, starts, cut),
        (1,),
        ins,
        [(s, whole(s)) for s in outs],
        scalars=(first,),
        after=after,
    )


def expert_body(index, blocks, joint, n_dp, order, expert_ref, me_ref, *refs):
    refs = list(refs)
    u_hbm = [refs.pop(0) for _ in range(blocks)]
    dz_hbm = [refs.pop(0) for _ in range(blocks)]
    gate_hbm = [refs.pop(0) for _ in range(blocks)]
    wg_hbm, wu_hbm, wd_hbm, yg_hbm, du_hbm, slope_ref = refs[:6]
    grads_hbm, refs = (refs[6:7], refs[7:]) if joint else (refs[6:8], refs[8:])
    (
        u_ref, dz_ref, gate_ref, wg, wu, wd, ha, side_gate, side_up, dy, dga, dua, yg, du, stage,
        row_sems, sems,
    ) = refs
    _, slot_count, width = u_ref.shape
    rows = blocks * slot_count
    ff = ha.shape[1]
    expert, me = expert_ref[0], me_ref[0]

    def loads(sources, target, at):
        return [
            pltpu.make_async_copy(s.at[index], target.at[b], row_sems.at[at, b])
            for b, s in enumerate(sources)
        ]

    u_loads, dz_loads, gate_loads = (
        loads(u_hbm, u_ref, 0), loads(dz_hbm, dz_ref, 1), loads(gate_hbm, gate_ref, 2)
    )
    w_loads = [
        pltpu.make_async_copy(source.at[expert], target, sems.at[at])
        for at, (source, target) in enumerate(((wg_hbm, wg), (wu_hbm, wu), (wd_hbm, wd)))
    ]
    first, second = u_loads + w_loads[:2], w_loads[2:] + gate_loads + dz_loads
    for load in first + second:
        load.start()
    for load in first:
        load.wait()
    tile = 256

    @pl.loop(0, ff // tile)
    def _(t):
        cols = column(t, tile)
        u = u_ref[...].reshape(rows, width)
        a = dot(u, wg[:, cols])
        b = dot(u, wu[:, cols])
        cdf = 0.5 * (1.0 + lax.erf(a * 0.7071067811865476))
        pdf = jnp.exp(-0.5 * a * a) * 0.3989422804014327
        glu = a * cdf
        ha[:, cols] = (glu * b).astype(BF16)
        side_gate[:, cols] = b * (cdf + a * pdf)
        side_up[:, cols] = glu

    for load in second:
        load.wait()
    slope_ref[...] = jnp.zeros_like(slope_ref)

    @pl.loop(0, width // tile)
    def _(t):
        cols = column(t, tile)
        gate = gate_ref[...].reshape(rows, 128)[:, :1]
        y = dot(ha[...], wd[:, cols]).astype(BF16).astype(F32)
        dz = dz_ref[:, :, cols].reshape(rows, tile).astype(F32)
        part = jnp.sum(dz * y, axis=1, keepdims=True)
        slope_ref[...] += jnp.broadcast_to(part, (rows, 128)).reshape(blocks, slot_count, 128)
        yg[:, :, cols] = (gate * y).astype(BF16).reshape(blocks, slot_count, tile)
        dy[:, cols] = (gate * dz).astype(BF16)

    out_yg = pltpu.make_async_copy(yg, yg_hbm, sems.at[3])
    out_yg.start()

    @pl.loop(0, ff // tile)
    def _(t):
        cols = column(t, tile)
        dha = dot_nt(dy[...], wd[cols, :])
        dga[:, cols] = (dha * side_gate[:, cols]).astype(BF16)
        dua[:, cols] = (dha * side_up[:, cols]).astype(BF16)

    wide = 384
    deep = width // n_dp
    flat = ff // n_dp

    def spot(block):
        if not joint:
            return place_of(block ^ me, order, n_dp)
        rank = block % TEAM_BIT + (block // (2 * TEAM_BIT)) * TEAM_BIT
        return 2 * rank + (block // TEAM_BIT + me // TEAM_BIT) % 2

    @pl.loop(0, width // wide)
    def _(t):
        cols = column(t, wide)
        ut = u_ref[:, :, cols].reshape(rows, wide)
        for which, grad in ((0, dga), (1, dua)):
            d_weight = dot_tn(ut, grad[...]).astype(BF16)
            for i in range(wide // deep):
                at = spot(t * (wide // deep) + i)
                stage[which, at] = d_weight[i * deep : (i + 1) * deep]

    @pl.loop(0, ff // wide)
    def _(t):
        cols = column(t, wide)
        d_weight = dot_tn(ha[:, cols], dy[...]).astype(BF16)
        for i in range(wide // flat):
            at = spot(t * (wide // flat) + i)
            part = d_weight[i * flat : (i + 1) * flat]
            stage[2, at, :flat] = part[:, :ff]
            stage[2, at, flat:] = part[:, ff:]

    if joint:
        out_grads = [
            pltpu.make_async_copy(stage.at[m], grads_hbm[0].at[:, m], sems.at[5 + m])
            for m in range(3)
        ]
    else:
        out_grads = [
            pltpu.make_async_copy(
                stage.at[:, pl.ds(side * (n_dp // 2), n_dp // 2)], grads_hbm[side], sems.at[5 + side]
            )
            for side in range(2)
        ]
    for copy in out_grads:
        copy.start()

    @pl.loop(0, width // tile)
    def _(t):
        cols = column(t, tile)
        back = dot_nt(dga[...], wg[cols, :]) + dot_nt(dua[...], wu[cols, :])
        du[:, :, cols] = back.astype(BF16).reshape(blocks, slot_count, tile)

    out_du = pltpu.make_async_copy(du, du_hbm, sems.at[4])
    out_du.start()
    out_yg.wait()
    for copy in out_grads:
        copy.wait()
    out_du.wait()


def place_of(index, order, count):
    place = 0
    for at, bit in enumerate(order):
        place = place + ((index // bit) % 2) * (count >> (at + 1))
    return place


def expert_pass(index, expert, me, u, dz, gates, wg, wu, wd, n_dp, order, joint, after=()):
    blocks = len(u)
    _, slot_count, width = u[0].shape
    ff = wg.shape[2]
    rows = blocks * slot_count
    deep = width // n_dp
    if joint:
        packed = [shaped((n_dp, 3, deep, ff), BF16)]
    else:
        packed = [shaped((3, n_dp // 2, deep, ff), BF16)] * 2
    row_shape = shaped((blocks, slot_count, width), BF16)
    slope_shape = shaped((blocks, slot_count, 128), F32)
    return kernel_call(
        26.5,
        functools.partial(expert_body, index, blocks, joint, n_dp, order),
        (1,),
        [(a, ANYWHERE) for a in list(u) + list(dz) + list(gates) + [wg, wu, wd]],
        [
            (row_shape, ANYWHERE),
            (row_shape, ANYWHERE),
            (slope_shape, whole(slope_shape)),
        ]
        + [(p, ANYWHERE) for p in packed],
        scalars=(expert, me),
        scratch=[
            pltpu.VMEM((blocks, slot_count, width), BF16),
            pltpu.VMEM((blocks, slot_count, width), BF16),
            pltpu.VMEM((blocks, slot_count, 128), F32),
            pltpu.VMEM((width, ff), BF16),
            pltpu.VMEM((width, ff), BF16),
            pltpu.VMEM((ff, width), BF16),
            pltpu.VMEM((rows, ff), BF16),
            pltpu.VMEM((rows, ff), F32),
            pltpu.VMEM((rows, ff), F32),
            pltpu.VMEM((rows, width), BF16),
            pltpu.VMEM((rows, ff), BF16),
            pltpu.VMEM((rows, ff), BF16),
            pltpu.VMEM((blocks, slot_count, width), BF16),
            pltpu.VMEM((blocks, slot_count, width), BF16),
            pltpu.VMEM((3, n_dp, width // n_dp, ff), BF16),
            pltpu.SemaphoreType.DMA((3, blocks)),
            pltpu.SemaphoreType.DMA((8,)),
        ],
        after=after,
    )


def add_split_body(a_ref, b_ref, c_ref, d_ref, keep_ref, send_ref):
    keep_ref[...] = (a_ref[...].astype(F32) + b_ref[...].astype(F32)).astype(keep_ref.dtype)
    send_ref[...] = (c_ref[...].astype(F32) + d_ref[...].astype(F32)).astype(BF16)


def add_split(held, arrived, axis, last=False, after=()):
    half = held.shape[axis] // 2
    shape = list(held.shape)
    shape[axis] = half
    block = [1 if at == axis else size for at, size in enumerate(held.shape)]
    spot = lambda shift: lambda i: tuple(i + shift if at == axis else 0 for at in range(len(block)))
    low, high = pl.BlockSpec(tuple(block), spot(0)), pl.BlockSpec(tuple(block), spot(half))
    return kernel_call(
        4.5,
        add_split_body,
        (half,),
        [(held, low), (arrived, low), (held, high), (arrived, high)],
        [(shaped(shape, F32 if last else BF16), low), (shaped(shape, BF16), low)],
        after=after,
    )


def settle_body(slots, own_ref, other_ref, *refs):
    outs = refs[-3:]

    def write(part):
        for m, out in enumerate(outs):
            value = part[m].astype(F32)
            if m == 2:
                flat = out.shape[1]
                value = jnp.concatenate([value[:flat], value[flat:]], axis=1)
            out[0] = value

    @pl.when(pl.program_id(0) == 0)
    def _():
        write(own_ref)

    @pl.when(pl.program_id(0) == 1)
    def _():
        write(other_ref)


def settle(own, other, slots, local_count, totals, after=()):
    _, deep, ff = own.shape
    shapes = [
        shaped((local_count, deep, ff), F32),
        shaped((local_count, deep, ff), F32),
        shaped((local_count, deep // 2, 2 * ff), F32),
    ]
    out_spec = lambda s: pl.BlockSpec((1, *s.shape[1:]), lambda i, slots: (slots[i], 0, 0))
    ins = [(own, whole(own)), (other, whole(other))] + [(t, ANYWHERE) for t in totals]
    return kernel_call(
        4.3,
        settle_body,
        (2,),
        ins,
        [(s, out_spec(s)) for s in shapes],
        scalars=(slots,),
        aliases={3 + i: i for i in range(len(totals))},
        after=after,
    )


def weight_grad_body(half, wide, order, n_dp, places, left_ref, right_ref, *refs):
    keep_ref, send_ref = refs[-2:]
    q = pl.program_id(0)
    width = left_ref.shape[1]
    deep = width // n_dp

    def fill(out_ref):
        right = right_ref[...].reshape(left_ref.shape[0], right_ref.shape[-1])
        for t in range(width // wide):
            part = dot_tn(left_ref[:, t * wide : (t + 1) * wide], right).astype(BF16)
            for i in range(wide // deep):
                at = place_of((t * (wide // deep) + i) ^ places[2 * half], order, n_dp)
                out_ref[0, at] = part[i * deep : (i + 1) * deep]

    @pl.when(q < half)
    def _():
        fill(keep_ref)

    @pl.when(q >= half)
    def _():
        fill(send_ref)


def weight_grad(left, right, places, n_dp, members, order, total_cols, start, buffers, after=()):
    rows, width = left.shape
    cols = right.shape[1] // members
    half = members // 2
    deep = width // n_dp
    if cols % 128 == 0:
        right_in = (right, pl.BlockSpec((rows, cols), lambda q, places: (0, places[q])))
    else:
        right = jnp.swapaxes(right.reshape(rows, members, cols), 0, 1)
        right_in = (right, pl.BlockSpec((1, rows, cols), lambda q, places: (places[q], 0, 0)))
        total_cols, start, buffers = cols, 0, []
    block = (1, n_dp, deep, cols)
    shape = shaped((half, n_dp, deep, total_cols), BF16)
    at = start // cols
    ins = [(left, whole(left)), right_in] + [(b, ANYWHERE) for b in buffers]
    return kernel_call(
        7,
        functools.partial(weight_grad_body, half, 384, order, n_dp),
        (members,),
        ins,
        [
            (shape, pl.BlockSpec(block, lambda q, places: (jnp.minimum(q, half - 1), 0, 0, at))),
            (shape, pl.BlockSpec(block, lambda q, places: (jnp.maximum(q - half, 0), 0, 0, at))),
        ],
        scalars=(places,),
        aliases={3 + i: i for i in range(len(buffers))},
        after=after,
    )


def reduce_grad(keep, send, steps):
    outer = keep.shape[0].bit_length()
    arrived = swap(send, *steps[0])
    for at in range(1, len(steps)):
        if at == outer:
            keep, arrived = keep[0], arrived[0]
        keep, send = add_split(keep, arrived, 0)
        arrived = swap(send, *steps[at])
    return keep[0].astype(F32) + arrived[0].astype(F32)


def norm_back(inputs, gain, upstream):
    scale = rms_of(inputs)
    weighted = gain * upstream
    middle = jnp.mean(inputs * weighted, axis=1, keepdims=True)
    grad = scale * weighted - inputs * (scale * scale * scale) * middle
    return grad, jnp.sum(upstream * inputs * scale, axis=0, keepdims=True)


def back_body(terms, *refs):
    refs = list(refs)
    parts = [refs.pop(0) for _ in range(terms)]
    (
        residual_ref, cot_ref, gain, gates_ref, router, message_ref, wo,
        d_res_ref, d_branch_ref, d_mix_ref, small_ref, total,
    ) = refs
    rows = residual_ref.shape[0]
    experts = gates_ref.shape[0]

    @pl.when(pl.program_id(0) == 0)
    def _():
        value = parts[0][...].astype(F32)
        for part in parts[1:]:
            value = value + part[...].astype(F32)
        total[...] = value
        slopes = total[rows:, :rows] + total[rows:, rows : 2 * rows]
        gates = gates_ref[...]
        mean = jnp.sum(gates * slopes, axis=0, keepdims=True)
        d_logits = (gates * (slopes - mean)).astype(BF16)
        d_routed = total[:rows, :] + dot_tn(d_logits, router[...])
        grad, d_gain = norm_back(residual_ref[...], gain[...], d_routed)
        d_residual = cot_ref[...].astype(F32) + grad
        d_res_ref[...] = d_residual
        d_branch_ref[...] = d_residual.astype(BF16)
        small_ref[:experts, :] = dot(d_logits, message_ref[:rows, :])
        small_ref[experts:, :] = jnp.broadcast_to(d_gain, (8, d_gain.shape[1]))

    d_mix_ref[...] = dot_nt(d_branch_ref[...], wo[...]).astype(BF16)


def back_through_branch(terms, residual, cot, gain, gates_t, router_t, message, wo, after=()):
    rows, width = residual.shape
    experts = gates_t.shape[0]
    tile = 256
    outs = (
        shaped((rows, width), F32),
        shaped((rows, width), BF16),
        shaped((experts + 8, width), F32),
    )
    d_mix = shaped((rows, wo.shape[0]), BF16)
    d_residual, d_branch, d_mix, small = kernel_call(
        13.8,
        functools.partial(back_body, len(terms)),
        (wo.shape[0] // tile,),
        [(a, whole(a)) for a in terms]
        + [(a, whole(a)) for a in (residual, cot, gain, gates_t, router_t, message)]
        + [(wo, pl.BlockSpec((tile, width), lambda i: (i, 0)))],
        [(s, whole(s)) for s in outs[:2]]
        + [(d_mix, pl.BlockSpec((rows, tile), lambda i: (0, i))), (outs[2], whole(outs[2]))],
        scratch=[pltpu.VMEM((rows + experts, width), F32)],
        after=after,
    )
    return d_residual, d_branch, d_mix, small


def output_body(residual_ref, *refs):
    total = residual_ref[...]
    for part in refs[:-1]:
        total = total + part[...].astype(F32)
    refs[-1][...] = total.astype(BF16)


def layer_output(residual, terms):
    out = shaped(residual.shape, BF16)
    return kernel_call(
        5,
        output_body, (1,), [(a, whole(a)) for a in [residual, *terms]], [(out, whole(out))]
    )[0]


def key_value_back_body(members, held_ref, arrived_ref, cos_ref, sin_ref, own_ref, joined_ref):
    total = held_ref[...].astype(F32) + arrived_ref[...].astype(F32)
    kd = total.shape[1] // 2
    keys = [
        turn(total[:, h * HD : (h + 1) * HD], cos_ref[...], -sin_ref[...])
        for h in range(kd // HD)
    ]
    keys, values = jnp.concatenate(keys, axis=1), total[:, kd:]
    own_ref[:, :kd] = keys.astype(BF16)
    own_ref[:, kd:] = values.astype(BF16)
    part = kd // members
    joined = []
    for c in range(members):
        cols = slice(c * part, (c + 1) * part)
        joined += [keys[:, cols], values[:, cols]]
    joined_ref[...] = jnp.concatenate(joined, axis=1).astype(BF16)


def key_value_back(held, arrived, cos_wide, sin_wide, members):
    return kernel_call(
        2.6,
        functools.partial(key_value_back_body, members),
        (1,),
        [(a, whole(a)) for a in (held, arrived, cos_wide, sin_wide)],
        [(s, whole(s)) for s in [shaped(held.shape, BF16)] * 2],
    )


def finish_body(steps, dq_ref, dkv_ref, wq, wk, wv, x_ref, d_res_ref, gain, small_ref,
                d_hidden_ref, sums_ref, total):
    i = pl.program_id(0)
    kd = wk.shape[1]
    part = dot_nt(dq_ref[...], wq[...])
    part = part + dot_nt(dkv_ref[:, :kd], wk[...]) + dot_nt(dkv_ref[:, kd:], wv[...])
    total[:, column(i, part.shape[1])] = part

    @pl.when(i == steps - 1)
    def _():
        x = x_ref[...].astype(F32)
        grad, d_gain = norm_back(x, gain[...], total[...])
        d_hidden_ref[...] = d_res_ref[...] + grad
        lead = small_ref.shape[0] - 8
        sums_ref[:lead, :] = small_ref[:lead, :]
        row = lax.broadcasted_iota(jnp.int32, (8, 1), 0)
        sums_ref[lead:, :] = jnp.where(row == 1, d_gain, small_ref[lead:, :])


def finish(dq, dkv, wq, wk, wv, x, d_residual, gain, small, after=()):
    rows, width = x.shape
    tile = 256
    by_rows = lambda w: (w, pl.BlockSpec((tile, w.shape[1]), lambda i: (i, 0)))
    outs = (shaped((rows, width), F32), shaped(small.shape, F32))
    return kernel_call(
        13,
        functools.partial(finish_body, width // tile),
        (width // tile,),
        [(dq, whole(dq)), (dkv, whole(dkv)), by_rows(wq), by_rows(wk), by_rows(wv)]
        + [(a, whole(a)) for a in (x, d_residual, gain, small)],
        [(s, whole(s)) for s in outs],
        scratch=[pltpu.VMEM((rows, width), F32)],
        after=after,
    )


def per_device(
    hidden_in, cotangent, norm_attn, w_query, w_key, w_value, w_out, norm_ffn, w_router,
    w_gate, w_up, w_down, expert_ids, priority, prefix,
):
    group_count, span_len, width = hidden_in.shape
    row_count = group_count * span_len
    q_width, kv_width = w_query.shape[1], w_key.shape[1]
    kv_heads = kv_width // HD
    members, n_dp = lax.axis_size("expert"), lax.axis_size("dp")
    expert_count = w_router.shape[1]
    local_count = w_gate.shape[0]
    team_count = local_count // 2
    top_count = expert_ids.shape[3]
    slot_count = row_count * top_count * 5 // (expert_count * 4)
    capacity = 9 * row_count * members * top_count // (8 * expert_count)
    e_index, d_index = lax.axis_index("expert"), lax.axis_index("dp")
    parity = (d_index // TEAM_BIT) % 2
    first_local = parity * team_count
    first_expert = (e_index * local_count + first_local).reshape(1).astype(jnp.int32)
    e_steps = [("expert", bit) for bit in bits_of(members)]
    team = ("dp", TEAM_BIT)
    gain_one, gain_two = norm_attn.reshape(1, width), norm_ffn.reshape(1, width)
    router_t = w_router.T

    expert_range = jnp.arange(expert_count, dtype=jnp.int32)
    routes_t = expert_ids.reshape(row_count, top_count).T
    hit_t = jnp.any(routes_t[:, None, :] == expert_range[None, :, None], axis=0)
    tables = jnp.concatenate([routes_t, priority.reshape(1, row_count)], axis=0)[None]
    for axis_name, bit in [team] + e_steps:
        tables = jnp.concatenate([tables, swap(tables, axis_name, bit)], axis=0)

    offset = e_index * span_len
    positions = (offset + jnp.arange(span_len, dtype=jnp.int32)).astype(F32)
    frequency = ROPE_BASE ** (-(jnp.arange(HD // 2, dtype=F32) * 2.0 / HD))
    angles = positions[:, None] * frequency[None, :]
    cos_table, sin_table = jnp.cos(angles), jnp.sin(angles)
    cos_span = jnp.concatenate([cos_table, cos_table], axis=1)
    sin_span = jnp.concatenate([-sin_table, sin_table], axis=1)
    cos_wide, sin_wide = jnp.tile(cos_span, (group_count, 1)), jnp.tile(sin_span, (group_count, 1))
    x = hidden_in.reshape(row_count, width)
    cot = cotangent.reshape(row_count, width)
    normed, kv_own, queries, cot_later = project_inputs(
        x, gain_one, w_query, w_key, w_value, cos_wide, sin_wide, cot
    )
    kv = gather_pieces(kv_own.reshape(group_count, span_len, 2 * kv_width), e_steps)
    q = queries([tables])
    source = e_index ^ sum(
        ((jnp.arange(members) >> at) & 1) * bit for at, (_, bit) in enumerate(e_steps)
    )
    source = jnp.concatenate([source, offset.reshape(1)]).astype(jnp.int32)

    cut = row_count // 2

    far, near = ("expert", 2), ("expert", 1)

    def corner_of(over_z, over_y):
        return swap(over_z[:cut], *far), swap(over_y[cut:], *team)

    def over_near(piece):
        return tuple(swap(s, *near) for s in piece)

    def scatter_team(make):
        if members != 4:
            pieces = [make(at, [], 0)[0] for at in range(2 * members)]
            return [scatter_pieces(pieces, [team] + e_steps)]
        sent = {at: swap(make(at + 4, [], 0)[0], "expert", 1) for at in (3, 1, 2, 0)}
        low, high = make(3, [(sent[3], 0)], cut)
        from_y, from_z = swap(low, *far), swap(high, *team)
        own = make(0, [(sent[0], 0)], 0)[0]
        over_z = swap(make(1, [(sent[1], 0), (from_y, 0)], 0)[0], *team)
        over_y = swap(make(2, [(sent[2], 0), (from_z, cut)], 0)[0], *far)
        return [own, over_z, over_y]

    split = members == 4
    if split:
        over_z, over_y = swap(cot, *team), swap(cot_later, *far)
        cots = [(cot,), (over_z,), (over_y,)]
    else:
        cots = [(piece,) for piece in gather_pieces(cot, [team] + e_steps)]

    q = q.reshape(group_count, span_len, q_width)
    mix, lse = attend(q, kv, prefix, source)
    mix = mix.reshape(row_count, q_width)
    residual, message, gates_t = branch(x, mix, w_out, gain_two, router_t, hit_t.astype(F32))

    u_rows, gate_rows = {}, {}

    def send_rows(at, piece, after):
        u_rows[at], gate_rows[at] = dispatch(
            piece, at, places, first_expert, slot_count, True, after
        )

    if split:
        over_z, over_y = swap(message, *team), swap(message, *far)
    else:
        pieces = gather_pieces(message, [team] + e_steps)
    places = find_places(tables, first_expert, team_count, capacity, [message])
    if split:
        cots.append(corner_of(hold(cots[1][0], [places]), hold(cots[2][0], [places])))
        cots += [over_near(piece) for piece in cots]
    dz_rows = []
    for at, piece in enumerate(cots):
        dz_rows.append(
            dispatch(piece, at, places, first_expert, slot_count, False, dz_rows[-1:])[0]
        )
    if split:
        send_rows(0, (message,), dz_rows[-1:])
        send_rows(4, over_near((message,)), [u_rows[0]])
        over_z, over_y = hold(over_z, [u_rows[4]]), hold(over_y, [u_rows[4]])
        corner = corner_of(over_z, over_y)
        for at, piece in ((1, (over_z,)), (2, (over_y,))):
            send_rows(at, piece, [])
            send_rows(4 + at, over_near(piece), [])
        last = [u_rows[5], u_rows[6]]
        corner = tuple(hold(part, last) for part in corner)
        send_rows(3, corner, [])
        send_rows(7, over_near(corner), [])
    else:
        for at, piece in enumerate(pieces):
            send_rows(at, (piece,), dz_rows[-1:])
    u_rows, gate_rows = ([rows[at] for at in range(2 * members)] for rows in (u_rows, gate_rows))
    d_order = [bit for bit in reversed(bits_of(n_dp)) if bit != TEAM_BIT] + [TEAM_BIT]
    me = d_index.reshape(1).astype(jnp.int32)
    outs, backs, slopes, chains = [], [], [], []
    chunk = 8
    for e in range(team_count):
        expert = (first_local + e).reshape(1).astype(jnp.int32)
        parts = []
        for start in range(0, len(u_rows), chunk):
            span = slice(start, start + chunk)
            parts.append(
                expert_pass(
                    e, expert, me, u_rows[span], dz_rows[span], gate_rows[span],
                    w_gate, w_up, w_down, n_dp, d_order, False, slopes[-1:],
                )
            )
        if len(parts) == 1:
            out, back, slope, *grads = parts[0]
        else:
            out, back, slope = (jnp.concatenate([p[i] for p in parts], axis=0) for i in range(3))
            grads = [
                sum(p[i].astype(F32) for p in parts).astype(BF16) for i in range(3, len(parts[0]))
            ]
        outs.append(out)
        backs.append(back)
        slopes.append(slope)
        chains.append((grads[0], swap(grads[1], "dp", d_order[0])))
    done = [0] * team_count
    ppermuted = team_count

    def advance(e, after):
        if e >= ppermuted or done[e] >= len(d_order) - 1:
            return list(after)
        done[e] += 1
        step = done[e]
        keep, arrived = chains[e]
        keep, send = add_split(keep, arrived, 1, step == len(d_order) - 1, after)
        if step == len(d_order) - 1:
            chains[e] = (keep[:, 0], swap(send[:, 0], "dp", d_order[step]))
        else:
            chains[e] = (keep, swap(send, "dp", d_order[step]))
        return [keep]

    extra = expert_count

    first_marks = advance(0, slopes[-1:])

    def make_back(at, added, cut_at):
        return combine(
            backs, at, places, slopes, first_expert, added, cut_at, extra,
            first_marks if at >= members else (),
        )

    back_terms = scatter_team(make_back)
    marks = advance(0, advance(1, back_terms[:1]))
    d_residual, d_branch, d_mix, small = back_through_branch(
        back_terms, residual, cot, gain_two, gates_t, router_t, message, w_out, marks
    )

    member_order = [bit for _, bit in reversed(e_steps)]
    member_places = [
        sum(((q >> (len(member_order) - 1 - at)) & 1) * bit for at, bit in enumerate(member_order))
        for q in range(members)
    ]
    grad_places = jnp.concatenate(
        [e_index ^ jnp.array(member_places, jnp.int32), d_index.reshape(1)]
    ).astype(jnp.int32)
    w_order = list(reversed(bits_of(n_dp)))
    w_steps = [("expert", bit) for bit in member_order] + [("dp", bit) for bit in w_order]
    q_part, kv_part = q_width // members, kv_width // members
    w_parts = []

    def add_weight(left, right, start, after):
        buffers = w_parts[-1] if w_parts else []
        w_parts.append(
            weight_grad(
                left, right, grad_places, n_dp, members, w_order,
                2 * q_part + 2 * kv_part, start, buffers, after,
            )
        )

    dq, d_kv = attend_back(
        q, d_mix.reshape(group_count, span_len, q_width), lse, kv, prefix, source,
        cos_span, sin_span,
    )
    dq = dq.reshape(row_count, q_width)
    add_weight(mix, d_branch, 0, [dq])
    add_weight(normed, dq, q_part, [])
    last_step = e_steps[0]
    halves = [scatter_pieces(d_kv[at::2], e_steps[1:]) for at in range(2)]
    held, sent = (h.reshape(row_count, 2 * kv_width) for h in halves)
    arrived = hold(swap(sent, *last_step), w_parts[-1][:1])
    d_kv_own, joined = key_value_back(held, arrived, cos_wide, sin_wide, members)
    add_weight(normed, joined, 2 * q_part, [])
    d_hidden, sums = finish(
        dq, d_kv_own, w_query, w_key, w_value, x, d_residual, gain_one, small, w_parts[-1][:1]
    )
    if q_part % 128 == 0 and kv_part % 64 == 0:
        w_keep, w_send = w_parts[-1]
    else:
        w_keep, w_send = (jnp.concatenate([p[i] for p in w_parts], axis=3) for i in range(2))
    marks = advance(1, advance(2, [d_hidden]))

    def make_out(at, added, cut_at):
        return combine(outs, at, places, None, first_expert, added, cut_at, 0, marks)

    output = layer_output(residual, scatter_team(make_out))
    sums = all_sum(sums, ("expert", "dp"))
    w_total = reduce_grad(w_keep, w_send, w_steps)

    totals = []
    for e in range(team_count):
        while e < ppermuted and done[e] < len(d_order) - 1:
            advance(e, [output])
        own, other = chains[e]
        slots = jnp.stack([first_local + e, team_count - first_local + e]).astype(jnp.int32)
        totals = settle(own, other, slots, local_count, totals, [output])
    grad_gate, grad_up, grad_down = totals
    return (
        output.reshape(group_count, span_len, width),
        d_hidden.reshape(group_count, span_len, width),
        sums[expert_count + 1],
        w_total[:, q_part : 2 * q_part],
        w_total[:, 2 * q_part : 2 * q_part + kv_part],
        w_total[:, 2 * q_part + kv_part :],
        w_total[:, :q_part],
        sums[expert_count],
        sums[:expert_count].T,
        grad_gate,
        grad_up,
        grad_down,
    )


def solution(mesh):
    in_specs = (
        P("dp", "expert", None),
        P("dp", "expert", None),
        P(),
        P(),
        P(),
        P(),
        P(),
        P(),
        P(),
        P("expert", None, None),
        P("expert", None, None),
        P("expert", None, None),
        P(("dp", "expert"), None, None, None),
        P(("dp", "expert"), None, None),
        P("dp"),
    )
    out_specs = (
        P("dp", "expert", None),
        P("dp", "expert", None),
        P(),
        P("dp", "expert"),
        P("dp", "expert"),
        P("dp", "expert"),
        P("dp", "expert"),
        P(),
        P(),
        P("expert", "dp", None),
        P("expert", "dp", None),
        P("expert", "dp", None),
    )
    return jax.shard_map(
        per_device, mesh=mesh, in_specs=in_specs, out_specs=out_specs, check_vma=False
    )
```

```python
import functools

import jax
import jax.numpy as jnp
from jax import lax
from jax.experimental import pallas as pl
from jax.experimental.pallas import tpu as pltpu
from jax.sharding import PartitionSpec as P

HD = 128
EPSILON = 1e-06
ROPE_BASE = 10000.0
MASKED = -1e30
EXTRA = 16
TEAM_BIT = 2
VMEM_LIMIT = 60 * 1024 * 1024

BF16 = jnp.bfloat16
F32 = jnp.float32


def dot(a, b):
    return jnp.dot(a, b, preferred_element_type=F32)


def dot_nt(a, b):
    return lax.dot_general(a, b, (((1,), (1,)), ((), ())), preferred_element_type=F32)


def dot_tn(a, b):
    return lax.dot_general(a, b, (((0,), (0,)), ((), ())), preferred_element_type=F32)


def bits_of(size):
    return [1 << i for i in reversed(range(size.bit_length() - 1))]


def swap(values, axis_name, bit):
    count = lax.axis_size(axis_name)
    return lax.ppermute(values, axis_name, [(i, i ^ bit) for i in range(count)])


def gather_pieces(values, steps):
    pieces = [values]
    for axis_name, bit in steps:
        pieces = pieces + [swap(piece, axis_name, bit) for piece in pieces]
    return pieces


def add_pair(a, b):
    return (a.astype(F32) + b.astype(F32)).astype(BF16)


def scatter_pieces(pieces, steps):
    for axis_name, bit in reversed(steps):
        half = len(pieces) // 2
        pieces = [
            add_pair(a, swap(b, axis_name, bit))
            for a, b in zip(pieces[:half], pieces[half:], strict=True)
        ]
    return pieces[0]


def all_sum(values, axes):
    for axis_name in axes:
        for bit in reversed(bits_of(lax.axis_size(axis_name))):
            values = values + swap(values, axis_name, bit)
    return values


ANYWHERE = pl.BlockSpec(memory_space=pl.ANY)


TIME_SCALE = 0.01


def kernel_call(us, body, grid, ins, outs, scalars=(), scratch=(), after=(), aliases=None):
    after = list(after)
    lead, held = len(scalars), len(ins)

    def run(*refs):
        body(*refs[: lead + held], *refs[lead + held + len(after) :])

    grid_spec = pltpu.PrefetchScalarGridSpec(
        num_scalar_prefetch=lead,
        grid=grid,
        in_specs=[spec for _, spec in ins] + [ANYWHERE] * len(after),
        out_specs=[spec for _, spec in outs],
        scratch_shapes=list(scratch),
    )
    return pl.pallas_call(
        run,
        grid_spec=grid_spec,
        out_shape=[shape for shape, _ in outs],
        input_output_aliases=aliases or {},
        compiler_params=pltpu.CompilerParams(vmem_limit_bytes=VMEM_LIMIT),
        cost_estimate=pl.CostEstimate(
            flops=int(us * TIME_SCALE * 1e9),
            bytes_accessed=int(us * TIME_SCALE * 3.3e6),
            transcendentals=0,
        ),
    )(*scalars, *[a for a, _ in ins], *after)


def shaped(shape, dtype):
    return jax.ShapeDtypeStruct(tuple(shape), dtype)


def whole(array):
    zeros = (0,) * len(array.shape)
    return pl.BlockSpec(tuple(array.shape), lambda *_: zeros)


def rms_of(values):
    return lax.rsqrt(jnp.mean(values * values, axis=-1, keepdims=True) + EPSILON)


def turn(values, cos_wide, sin_wide):
    return values * cos_wide + pltpu.roll(values, HD // 2, 1) * sin_wide


def column(width, tile):
    return pl.ds(pl.multiple_of(width * tile, tile), tile)


def hold_body(value_ref, out_ref):
    pass


def hold(value, after):
    return kernel_call(
        0.5, hold_body, (1,), [(value, ANYWHERE)], [(shaped(value.shape, value.dtype), ANYWHERE)],
        after=after, aliases={0: 0},
    )[0]


def key_value_body(x_ref, gain, wk, wv, cos_ref, sin_ref, cot_ref, normed_ref, kv_ref, same_ref):
    x = x_ref[...].astype(F32)
    normed = (x * rms_of(x) * gain[...]).astype(BF16)
    normed_ref[...] = normed
    keys = dot(normed, wk[...])
    for h in range(keys.shape[1] // HD):
        cols = slice(h * HD, (h + 1) * HD)
        kv_ref[:, cols] = turn(keys[:, cols], cos_ref[...], sin_ref[...]).astype(BF16)
    kv_ref[:, keys.shape[1] :] = dot(normed, wv[...]).astype(BF16)


def query_body(normed_ref, wq, cos_ref, sin_ref, q_ref):
    queries = dot(normed_ref[...], wq[...])
    for h in range(queries.shape[1] // HD):
        cols = slice(h * HD, (h + 1) * HD)
        q_ref[:, cols] = turn(queries[:, cols], cos_ref[...], sin_ref[...]).astype(BF16)


def project_inputs(x, gain, wq, wk, wv, cos_wide, sin_wide, cot):
    rows, width = x.shape
    kd = wk.shape[1]
    normed, kv, cot = kernel_call(
        4.2,
        key_value_body,
        (1,),
        [(a, whole(a)) for a in (x, gain, wk, wv, cos_wide, sin_wide)] + [(cot, ANYWHERE)],
        [(s, whole(s)) for s in (shaped((rows, width), BF16), shaped((rows, 2 * kd), BF16))]
        + [(shaped(cot.shape, BF16), ANYWHERE)],
        aliases={6: 2},
    )
    tile = 256

    def queries(after):
        return kernel_call(
            8,
            query_body,
            (wq.shape[1] // tile,),
            [
                (normed, whole(normed)),
                (wq, pl.BlockSpec((width, tile), lambda i: (0, i))),
                (cos_wide, whole(cos_wide)),
                (sin_wide, whole(sin_wide)),
            ],
            [(shaped((rows, wq.shape[1]), BF16), pl.BlockSpec((rows, tile), lambda i: (0, i)))],
            after=after,
        )[0]

    return normed, kv, queries, cot


def attention_bias(prefix, source, offset, span, members):
    rows = offset + lax.broadcasted_iota(jnp.int32, (span, span), 0)
    cols = lax.broadcasted_iota(jnp.int32, (span, span), 1)
    parts = []
    for p in range(members):
        keys = source[p] * span + cols
        parts.append(jnp.where((keys <= rows) | (keys < prefix), 0.0, MASKED))
    return jnp.concatenate(parts, axis=1)


def attention_body(members, kvh, ratio, prefix, source, q_ref, *refs):
    pieces, (mix_ref, lse_ref, bias) = refs[:members], refs[members:]
    span = q_ref.shape[1]
    scale = HD ** (-0.5)
    bias[...] = attention_bias(prefix[pl.program_id(0)], source, source[members], span, members)
    columns = []
    for k in range(kvh):
        keys = jnp.concatenate([p[0, :, k * HD : (k + 1) * HD] for p in pieces], axis=0)
        start = (kvh + k) * HD
        values = jnp.concatenate([p[0, :, start : start + HD] for p in pieces], axis=0)
        for r in range(ratio):
            cols = slice((k * ratio + r) * HD, (k * ratio + r + 1) * HD)
            scores = dot_nt(q_ref[0, :, cols], keys) + bias[...]
            top = jnp.max(scores, axis=1, keepdims=True)
            terms = jnp.exp((scores - top) * scale)
            total = jnp.sum(terms, axis=1, keepdims=True)
            mixed = dot(terms.astype(BF16), values)
            mix_ref[0, :, cols] = (mixed / total).astype(BF16)
            columns.append(top * scale + jnp.log(total))
    lse_ref[0] = jnp.concatenate(columns, axis=1)


def attention_back_body(
    members, kvh, ratio, prefix, source, q_ref, do_ref, lse_ref, cos_ref, sin_ref, *refs
):
    pieces, dq_ref = refs[:members], refs[members]
    outs, (bias, dk, dv) = refs[members + 1 : 2 * members + 1], refs[2 * members + 1 :]
    span = q_ref.shape[1]
    scale = HD ** (-0.5)
    bias[...] = attention_bias(prefix[pl.program_id(0)], source, source[members], span, members)
    for k in range(kvh):
        keys = jnp.concatenate([p[0, :, k * HD : (k + 1) * HD] for p in pieces], axis=0)
        start = (kvh + k) * HD
        values = jnp.concatenate([p[0, :, start : start + HD] for p in pieces], axis=0)
        for r in range(ratio):
            h = k * ratio + r
            cols = slice(h * HD, (h + 1) * HD)
            query, upstream = q_ref[0, :, cols], do_ref[0, :, cols]
            scores = dot_nt(query, keys) + bias[...]
            probs = jnp.exp(scores * scale - lse_ref[0, :, h : h + 1])
            d_probs = dot_nt(upstream, values)
            mean = jnp.sum(probs * d_probs, axis=1, keepdims=True)
            d_scores = (probs * (d_probs - mean)).astype(BF16)
            d_query = dot(d_scores, keys) * scale
            dq_ref[0, :, cols] = turn(d_query, cos_ref[...], -sin_ref[...]).astype(BF16)
            part_k = dot_tn(d_scores, query)
            part_v = dot_tn(probs.astype(BF16), upstream)
            if r == 0:
                dk[...] = part_k
                dv[...] = part_v
            else:
                dk[...] += part_k
                dv[...] += part_v
        for p, out in enumerate(outs):
            rows = slice(p * span, (p + 1) * span)
            out[0, :, k * HD : (k + 1) * HD] = (dk[rows, :] * scale).astype(BF16)
            out[0, :, start : start + HD] = dv[rows, :].astype(BF16)


def attend(q, kv, prefix, source):
    groups, span, qd = q.shape
    members, kvh = len(kv), kv[0].shape[2] // (2 * HD)
    heads = qd // HD
    block = lambda n: pl.BlockSpec((1, span, n), lambda g, *_: (g, 0, 0))
    return kernel_call(
        15.7,
        functools.partial(attention_body, members, kvh, heads // kvh),
        (groups,),
        [(q, block(qd))] + [(p, block(p.shape[2])) for p in kv],
        [
            (shaped(q.shape, BF16), block(qd)),
            (shaped((groups, span, heads), F32), block(heads)),
        ],
        scalars=(prefix, source),
        scratch=[pltpu.VMEM((span, span * members), F32)],
    )


def attend_back(q, do, lse, kv, prefix, source, cos_wide, sin_wide, after=()):
    groups, span, qd = q.shape
    members, kvh = len(kv), kv[0].shape[2] // (2 * HD)
    heads = qd // HD
    block = lambda n: pl.BlockSpec((1, span, n), lambda g, *_: (g, 0, 0))
    outs = kernel_call(
        28.6,
        functools.partial(attention_back_body, members, kvh, heads // kvh),
        (groups,),
        [(q, block(qd)), (do, block(qd)), (lse, block(heads))]
        + [(cos_wide, whole(cos_wide)), (sin_wide, whole(sin_wide))]
        + [(p, block(p.shape[2])) for p in kv],
        [(shaped(q.shape, BF16), block(qd))]
        + [(shaped(p.shape, BF16), block(p.shape[2])) for p in kv],
        scalars=(prefix, source),
        scratch=[
            pltpu.VMEM((span, span * members), F32),
            pltpu.VMEM((span * members, HD), F32),
            pltpu.VMEM((span * members, HD), F32),
        ],
        after=after,
    )
    return outs[0], outs[1:]


def branch_body(steps, x_ref, mix_ref, wo, gain, router, hit_ref,
                residual_ref, message_ref, gates_ref):
    i = pl.program_id(0)
    tile = wo.shape[1]
    cols = column(i, tile)
    residual_ref[:, cols] = x_ref[:, cols].astype(F32) + dot(mix_ref[...], wo[...])

    @pl.when(i == steps - 1)
    def _():
        rows = residual_ref.shape[0]
        experts = hit_ref.shape[0]
        h1 = residual_ref[...]
        a2 = (h1 * rms_of(h1) * gain[...]).astype(BF16)
        message_ref[:rows, :] = a2
        hit = hit_ref[...] > 0.0
        logits = jnp.where(hit, dot_nt(router[...], a2), MASKED)
        terms = jnp.exp(logits - jnp.max(logits, axis=0, keepdims=True))
        terms = jnp.where(hit, terms, 0.0)
        gates = terms / jnp.sum(terms, axis=0, keepdims=True)
        gates_ref[...] = gates
        high = gates.astype(BF16)
        rest = gates - high.astype(F32)
        middle = rest.astype(BF16)
        low = (rest - middle.astype(F32)).astype(BF16)
        message_ref[rows:, :rows] = high
        message_ref[rows:, rows : 2 * rows] = middle
        message_ref[rows:, 2 * rows : 3 * rows] = low
        if message_ref.shape[1] > 3 * rows:
            message_ref[rows:, 3 * rows :] = jnp.zeros(
                (experts, message_ref.shape[1] - 3 * rows), BF16
            )


def branch(x, mix, wo, gain, router_t, hit_t, after=()):
    rows, width = x.shape
    experts = router_t.shape[0]
    tile = 256
    outs = (
        shaped((rows, width), F32),
        shaped((rows + experts, width), BF16),
        shaped((experts, rows), F32),
    )
    return kernel_call(
        10,
        functools.partial(branch_body, width // tile),
        (width // tile,),
        [(x, whole(x)), (mix, whole(mix))]
        + [(wo, pl.BlockSpec((wo.shape[0], tile), lambda i: (0, i)))]
        + [(a, whole(a)) for a in (gain, router_t, hit_t)],
        [(s, whole(s)) for s in outs],
        after=after,
    )


def slot_masks(places, slot_count):
    experts, tokens = places.shape
    slots = lax.broadcasted_iota(jnp.int32, (slot_count, tokens), 0).astype(F32)
    return [places[e : e + 1, :] == slots for e in range(experts)]


def hot_rows(masks):
    return jnp.concatenate([m.astype(F32) for m in masks], axis=0).astype(BF16)


def pick_experts(table, first, count):
    row = lax.broadcasted_iota(jnp.int32, table.shape, 0)
    picked = [
        jnp.sum(jnp.where(row == first + e, table, 0.0), axis=0, keepdims=True)
        for e in range(count)
    ]
    return jnp.concatenate(picked, axis=0)


def places_body(blocks, count, capacity, first, table_ref, column_ref, out_ref):
    b = pl.program_id(0)
    tokens = table_ref.shape[2]
    top = table_ref.shape[1] - 1
    padded = 8

    def hits(at):
        row = lax.broadcasted_iota(jnp.int32, (padded, tokens), 0)
        expert = jnp.where(row < count, first[0] + row, -1)
        found = table_ref[at, 0:1, :] == expert
        for k in range(1, top):
            found = found | (table_ref[at, k : k + 1, :] == expert)
        return found

    own_order = table_ref[b, top : top + 1, :]
    before = jnp.zeros((padded, tokens), F32)
    for n in range(blocks // 2):
        at = 2 * n + b % 2
        earlier = jnp.where(column_ref[at] < own_order, 1.0, 0.0).astype(BF16)
        before = before + dot(jnp.where(hits(at), 1.0, 0.0).astype(BF16), earlier)
    kept = hits(b) & (before < capacity)
    row = lax.broadcasted_iota(jnp.int32, (tokens, tokens), 0)
    col = lax.broadcasted_iota(jnp.int32, (tokens, tokens), 1)
    ahead = jnp.where(row < col, 1.0, 0.0).astype(BF16)
    slots = dot(jnp.where(kept, 1.0, 0.0).astype(BF16), ahead)
    out_ref[0] = jnp.where(kept, slots, -1.0)[:count]


def find_places(tables, first, count, capacity, after=()):
    blocks, wide, tokens = tables.shape
    columns = tables[:, wide - 1, :, None]
    shape = shaped((blocks, count, tokens), F32)
    return kernel_call(
        4,
        functools.partial(places_body, blocks, count, capacity),
        (blocks,),
        [(tables, whole(tables)), (columns, whole(columns))],
        [(shape, pl.BlockSpec((1, count, tokens), lambda b, *_: (b, 0, 0)))],
        scalars=(first,),
        after=after,
    )[0]


def dispatch_body(parts, with_gates, slot_count, first, *refs):
    segments, refs = refs[:parts], refs[parts:]
    if with_gates:
        extra_ref, places_ref, rows_ref, gate_ref = refs
    else:
        places_ref, rows_ref = refs
    _, count, tokens = places_ref.shape
    masks = slot_masks(places_ref[0], slot_count)
    hot = hot_rows(masks)
    if with_gates:
        extra = extra_ref[...].astype(F32)
        table = extra[:, :tokens] + extra[:, tokens : 2 * tokens]
        gates = pick_experts(table + extra[:, 2 * tokens : 3 * tokens], first[0], count)
        for e in range(count):
            gate = jnp.sum(jnp.where(masks[e], gates[e : e + 1, :], 0.0), axis=1, keepdims=True)
            gate_ref[e] = jnp.broadcast_to(gate, (slot_count, 128))
    total, start = 0.0, 0
    for segment in segments:
        stop = min(start + segment.shape[0], tokens)
        total = total + dot(hot[:, start:stop], segment[: stop - start, :])
        start = stop
    total = total.astype(BF16)
    for e in range(count):
        rows_ref[e] = total[e * slot_count : (e + 1) * slot_count]


def dispatch(segments, at, places, first, slot_count, with_gates, after=()):
    width = segments[0].shape[1]
    _, count, tokens = places.shape
    ins = [(a, whole(a)) for a in segments]
    outs = [shaped((count, slot_count, width), BF16)]
    if with_gates:
        last = segments[-1]
        extra = last.shape[0] - (tokens - sum(a.shape[0] for a in segments[:-1]))
        spot = last.shape[0] // extra - 1
        ins.append((last, pl.BlockSpec((extra, width), lambda *_: (spot, 0))))
        outs.append(shaped((count, slot_count, 128), F32))
    ins.append((places, pl.BlockSpec((1, count, tokens), lambda *_: (at, 0, 0))))
    return kernel_call(
        1.5,
        functools.partial(dispatch_body, len(segments), with_gates, slot_count),
        (1,),
        ins,
        [(o, whole(o)) for o in outs],
        scalars=(first,),
        after=after,
    )


def combine_body(experts, with_extra, starts, cut, first, *refs):
    refs = list(refs)
    rows = [refs.pop(0) for _ in range(experts)]
    places_ref = refs.pop(0)
    slopes = [refs.pop(0) for _ in range(experts)] if with_extra else None
    added = [refs.pop(0) for _ in starts]
    outs = refs
    slot_count = rows[0].shape[1]
    tokens = places_ref.shape[2]
    masks = slot_masks(places_ref[0], slot_count)
    values = jnp.concatenate([r[0] for r in rows], axis=0)
    total = dot_tn(hot_rows(masks), values)
    last = outs[-1]
    width = last.shape[1]
    for other, start in zip(added, starts, strict=True):
        count = min(other.shape[0], tokens - start)
        parts = [total[start : start + count] + other[:count, :].astype(F32)]
        if start > 0:
            parts = [total[:start]] + parts
        if start + count < tokens:
            parts.append(total[start + count :])
        total = parts[0] if len(parts) == 1 else jnp.concatenate(parts, axis=0)
    total = total.astype(BF16)
    if cut:
        outs[0][...] = total[:cut]
    last[: tokens - cut, :] = total[cut:]
    if with_extra:
        count = last.shape[0] - (tokens - cut)
        row = lax.broadcasted_iota(jnp.int32, (count, tokens), 0)
        table = jnp.zeros((count, tokens), F32)
        for e in range(experts):
            slope = jnp.sum(jnp.where(masks[e], slopes[e][0, :, :1], 0.0), axis=0, keepdims=True)
            table = jnp.where(row == first[0] + e, slope, table)
        high = table.astype(BF16).astype(F32)
        for side, value in enumerate((high, table - high)):
            cols = slice(side * tokens, (side + 1) * tokens)
            for other, start in zip(added, starts, strict=True):
                if start + other.shape[0] > tokens:
                    value = value + other[tokens - start :, cols].astype(F32)
            last[tokens - cut :, cols] = value.astype(BF16)
        last[tokens - cut :, 2 * tokens :] = jnp.zeros((count, width - 2 * tokens), BF16)


def combine(rows, at, places, slopes, first, added, cut, extra, after=()):
    experts = len(rows)
    _, slot_count, width = rows[0].shape
    _, count, tokens = places.shape
    block = lambda n: pl.BlockSpec((1, slot_count, n), lambda *_: (at, 0, 0))
    ins = [(r, block(width)) for r in rows]
    ins.append((places, pl.BlockSpec((1, count, tokens), lambda *_: (at, 0, 0))))
    if slopes is not None:
        ins += [(s, block(128)) for s in slopes]
    ins += [(a, whole(a)) for a, _ in added]
    long = tokens + (extra if slopes is not None else 0)
    outs = [shaped((cut, width), BF16)] if cut else []
    outs.append(shaped((long - cut, width), BF16))
    starts = tuple(start for _, start in added)
    return kernel_call(
        1.2,
        functools.partial(combine_body, experts, slopes is not None, starts, cut),
        (1,),
        ins,
        [(s, whole(s)) for s in outs],
        scalars=(first,),
        after=after,
    )


def expert_body(index, blocks, joint, n_dp, order, expert_ref, me_ref, *refs):
    refs = list(refs)
    u_hbm = [refs.pop(0) for _ in range(blocks)]
    dz_hbm = [refs.pop(0) for _ in range(blocks)]
    gate_hbm = [refs.pop(0) for _ in range(blocks)]
    wg_hbm, wu_hbm, wd_hbm, yg_hbm, du_hbm, slope_ref = refs[:6]
    grads_hbm, refs = refs[6 : 8 - joint], refs[8 - joint :]
    (
        u_ref, dz_ref, gate_ref, wg, wu, wd, ha, side_gate, side_up, dy, dga, dua, yg, du, stage,
        row_sems, sems,
    ) = refs
    _, slot_count, width = u_ref.shape
    rows = blocks * slot_count
    ff = ha.shape[1]
    expert, me = expert_ref[0], me_ref[0]

    def loads(sources, target, at):
        return [
            pltpu.make_async_copy(s.at[index], target.at[b], row_sems.at[at, b])
            for b, s in enumerate(sources)
        ]

    u_loads, dz_loads, gate_loads = (
        loads(u_hbm, u_ref, 0), loads(dz_hbm, dz_ref, 1), loads(gate_hbm, gate_ref, 2)
    )
    w_loads = [
        pltpu.make_async_copy(source.at[expert], target, sems.at[at])
        for at, (source, target) in enumerate(((wg_hbm, wg), (wu_hbm, wu), (wd_hbm, wd)))
    ]
    first, second = u_loads + w_loads[:2], w_loads[2:] + gate_loads + dz_loads
    for load in first + second:
        load.start()
    for load in first:
        load.wait()
    tile = 256

    @pl.loop(0, ff // tile)
    def _(t):
        cols = column(t, tile)
        u = u_ref[...].reshape(rows, width)
        a = dot(u, wg[:, cols])
        b = dot(u, wu[:, cols])
        cdf = 0.5 * (1.0 + lax.erf(a * 0.7071067811865476))
        pdf = jnp.exp(-0.5 * a * a) * 0.3989422804014327
        glu = a * cdf
        ha[:, cols] = (glu * b).astype(BF16)
        side_gate[:, cols] = b * (cdf + a * pdf)
        side_up[:, cols] = glu

    for load in second:
        load.wait()
    slope_ref[...] = jnp.zeros_like(slope_ref)

    @pl.loop(0, width // tile)
    def _(t):
        cols = column(t, tile)
        gate = gate_ref[...].reshape(rows, 128)[:, :1]
        y = dot(ha[...], wd[:, cols]).astype(BF16).astype(F32)
        dz = dz_ref[:, :, cols].reshape(rows, tile).astype(F32)
        part = jnp.sum(dz * y, axis=1, keepdims=True)
        slope_ref[...] += jnp.broadcast_to(part, (rows, 128)).reshape(blocks, slot_count, 128)
        yg[:, :, cols] = (gate * y).astype(BF16).reshape(blocks, slot_count, tile)
        dy[:, cols] = (gate * dz).astype(BF16)

    out_yg = pltpu.make_async_copy(yg, yg_hbm, sems.at[3])
    out_yg.start()

    @pl.loop(0, ff // tile)
    def _(t):
        cols = column(t, tile)
        dha = dot_nt(dy[...], wd[cols, :])
        dga[:, cols] = (dha * side_gate[:, cols]).astype(BF16)
        dua[:, cols] = (dha * side_up[:, cols]).astype(BF16)

    wide = 384
    deep = width // n_dp
    flat = ff // n_dp

    def spot(block):
        return place_of(block ^ me, order, n_dp)

    @pl.loop(0, width // wide)
    def _(t):
        cols = column(t, wide)
        ut = u_ref[:, :, cols].reshape(rows, wide)
        for which, grad in ((0, dga), (1, dua)):
            d_weight = dot_tn(ut, grad[...]).astype(BF16)
            for i in range(wide // deep):
                at = spot(t * (wide // deep) + i)
                stage[at, which] = d_weight[i * deep : (i + 1) * deep]

    @pl.loop(0, ff // wide)
    def _(t):
        cols = column(t, wide)
        d_weight = dot_tn(ha[:, cols], dy[...]).astype(BF16)
        for i in range(wide // flat):
            at = spot(t * (wide // flat) + i)
            part = d_weight[i * flat : (i + 1) * flat]
            stage[at, 2, :flat] = part[:, :ff]
            stage[at, 2, flat:] = part[:, ff:]

    part = n_dp // len(grads_hbm)
    out_grads = [
        pltpu.make_async_copy(stage.at[pl.ds(side * part, part)], target, sems.at[5 + side])
        for side, target in enumerate(grads_hbm)
    ]
    for copy in out_grads:
        copy.start()

    @pl.loop(0, width // tile)
    def _(t):
        cols = column(t, tile)
        back = dot_nt(dga[...], wg[cols, :]) + dot_nt(dua[...], wu[cols, :])
        du[:, :, cols] = back.astype(BF16).reshape(blocks, slot_count, tile)

    out_du = pltpu.make_async_copy(du, du_hbm, sems.at[4])
    out_du.start()
    out_yg.wait()
    for copy in out_grads:
        copy.wait()
    out_du.wait()


def place_of(index, order, count):
    place = 0
    for at, bit in enumerate(order):
        place = place + ((index // bit) % 2) * (count >> (at + 1))
    return place


def expert_pass(index, expert, me, u, dz, gates, wg, wu, wd, n_dp, order, joint, after=()):
    blocks = len(u)
    _, slot_count, width = u[0].shape
    ff = wg.shape[2]
    rows = blocks * slot_count
    deep = width // n_dp
    packed = [shaped((n_dp // (2 - joint), 3, deep, ff), BF16)] * (2 - joint)
    row_shape = shaped((blocks, slot_count, width), BF16)
    slope_shape = shaped((blocks, slot_count, 128), F32)
    return kernel_call(
        26.5,
        functools.partial(expert_body, index, blocks, joint, n_dp, order),
        (1,),
        [(a, ANYWHERE) for a in list(u) + list(dz) + list(gates) + [wg, wu, wd]],
        [
            (row_shape, ANYWHERE),
            (row_shape, ANYWHERE),
            (slope_shape, whole(slope_shape)),
        ]
        + [(p, ANYWHERE) for p in packed],
        scalars=(expert, me),
        scratch=[
            pltpu.VMEM((blocks, slot_count, width), BF16),
            pltpu.VMEM((blocks, slot_count, width), BF16),
            pltpu.VMEM((blocks, slot_count, 128), F32),
            pltpu.VMEM((width, ff), BF16),
            pltpu.VMEM((width, ff), BF16),
            pltpu.VMEM((ff, width), BF16),
            pltpu.VMEM((rows, ff), BF16),
            pltpu.VMEM((rows, ff), F32),
            pltpu.VMEM((rows, ff), F32),
            pltpu.VMEM((rows, width), BF16),
            pltpu.VMEM((rows, ff), BF16),
            pltpu.VMEM((rows, ff), BF16),
            pltpu.VMEM((blocks, slot_count, width), BF16),
            pltpu.VMEM((blocks, slot_count, width), BF16),
            pltpu.VMEM((n_dp, 3, width // n_dp, ff), BF16),
            pltpu.SemaphoreType.DMA((3, blocks)),
            pltpu.SemaphoreType.DMA((8,)),
        ],
        after=after,
    )


def add_split_body(a_ref, b_ref, c_ref, d_ref, keep_ref, send_ref):
    keep_ref[...] = (a_ref[...].astype(F32) + b_ref[...].astype(F32)).astype(keep_ref.dtype)
    send_ref[...] = (c_ref[...].astype(F32) + d_ref[...].astype(F32)).astype(BF16)


def add_split(held, arrived, axis, last=False, after=()):
    half = held.shape[axis] // 2
    shape = list(held.shape)
    shape[axis] = half
    block = [1 if at == axis else size for at, size in enumerate(held.shape)]
    spot = lambda shift: lambda i: tuple(i + shift if at == axis else 0 for at in range(len(block)))
    low, high = pl.BlockSpec(tuple(block), spot(0)), pl.BlockSpec(tuple(block), spot(half))
    return kernel_call(
        4.5,
        add_split_body,
        (half,),
        [(held, low), (arrived, low), (held, high), (arrived, high)],
        [(shaped(shape, F32 if last else BF16), low), (shaped(shape, BF16), low)],
        after=after,
    )


def add_body(a_ref, b_ref, out_ref):
    out_ref[...] = (a_ref[...].astype(F32) + b_ref[...].astype(F32)).astype(BF16)


def add_blocks(held, arrived, after):
    block = pl.BlockSpec((1, *held.shape[1:]), lambda i: (i, 0, 0, 0))
    return kernel_call(
        4.5, add_body, held.shape[:1], [(held, block), (arrived, block)],
        [(shaped(held.shape, BF16), block)], after=after,
    )[0]


def settle_body(slots, own_ref, other_ref, *refs):
    outs = refs[-3:]

    def write(part):
        for m, out in enumerate(outs):
            value = part[m].astype(F32)
            if m == 2:
                flat = out.shape[1]
                value = jnp.concatenate([value[:flat], value[flat:]], axis=1)
            out[0] = value

    @pl.when(pl.program_id(0) == 0)
    def _():
        write(own_ref)

    @pl.when(pl.program_id(0) == 1)
    def _():
        write(other_ref)


def settle(own, other, slots, local_count, totals, after=()):
    _, deep, ff = own.shape
    shapes = [
        shaped((local_count, deep, ff), F32),
        shaped((local_count, deep, ff), F32),
        shaped((local_count, deep // 2, 2 * ff), F32),
    ]
    out_spec = lambda s: pl.BlockSpec((1, *s.shape[1:]), lambda i, slots: (slots[i], 0, 0))
    ins = [(own, whole(own)), (other, whole(other))] + [(t, ANYWHERE) for t in totals]
    return kernel_call(
        4.3,
        settle_body,
        (2,),
        ins,
        [(s, out_spec(s)) for s in shapes],
        scalars=(slots,),
        aliases={3 + i: i for i in range(len(totals))},
        after=after,
    )


def weight_grad_body(half, wide, order, n_dp, places, left_ref, right_ref, *refs):
    keep_ref, send_ref = refs[-2:]
    q = pl.program_id(0)
    width = left_ref.shape[1]
    deep = width // n_dp

    def fill(out_ref):
        right = right_ref[...].reshape(left_ref.shape[0], right_ref.shape[-1])
        for t in range(width // wide):
            part = dot_tn(left_ref[:, t * wide : (t + 1) * wide], right).astype(BF16)
            for i in range(wide // deep):
                at = place_of((t * (wide // deep) + i) ^ places[2 * half], order, n_dp)
                out_ref[0, at] = part[i * deep : (i + 1) * deep]

    @pl.when(q < half)
    def _():
        fill(keep_ref)

    @pl.when(q >= half)
    def _():
        fill(send_ref)


def weight_grad(left, right, places, n_dp, members, order, total_cols, start, buffers, after=()):
    rows, width = left.shape
    cols = right.shape[1] // members
    half = members // 2
    deep = width // n_dp
    if cols % 128 == 0:
        right_in = (right, pl.BlockSpec((rows, cols), lambda q, places: (0, places[q])))
    else:
        right = jnp.swapaxes(right.reshape(rows, members, cols), 0, 1)
        right_in = (right, pl.BlockSpec((1, rows, cols), lambda q, places: (places[q], 0, 0)))
        total_cols, start, buffers = cols, 0, []
    block = (1, n_dp, deep, cols)
    shape = shaped((half, n_dp, deep, total_cols), BF16)
    at = start // cols
    ins = [(left, whole(left)), right_in] + [(b, ANYWHERE) for b in buffers]
    return kernel_call(
        7,
        functools.partial(weight_grad_body, half, 384, order, n_dp),
        (members,),
        ins,
        [
            (shape, pl.BlockSpec(block, lambda q, places: (jnp.minimum(q, half - 1), 0, 0, at))),
            (shape, pl.BlockSpec(block, lambda q, places: (jnp.maximum(q - half, 0), 0, 0, at))),
        ],
        scalars=(places,),
        aliases={3 + i: i for i in range(len(buffers))},
        after=after,
    )


def reduce_grad(keep, send, steps, after=(), marks=None):
    outer = keep.shape[0].bit_length()
    arrived = swap(send, *steps[0])
    for at in range(1, len(steps)):
        if at == outer:
            keep, arrived = keep[0], arrived[0]
        keep, send = add_split(keep, arrived, 0, False, after if at == 1 else ())
        if marks is not None:
            marks.append(keep)
        arrived = swap(send, *steps[at])
    return keep[0].astype(F32) + arrived[0].astype(F32)


def norm_back(inputs, gain, upstream):
    scale = rms_of(inputs)
    weighted = gain * upstream
    middle = jnp.mean(inputs * weighted, axis=1, keepdims=True)
    grad = scale * weighted - inputs * (scale * scale * scale) * middle
    return grad, jnp.sum(upstream * inputs * scale, axis=0, keepdims=True)


def back_body(terms, *refs):
    refs = list(refs)
    parts = [refs.pop(0) for _ in range(terms)]
    (
        residual_ref, cot_ref, gain, gates_ref, router, message_ref, wo,
        d_res_ref, d_branch_ref, d_mix_ref, small_ref, total,
    ) = refs
    rows = residual_ref.shape[0]
    experts = gates_ref.shape[0]

    @pl.when(pl.program_id(0) == 0)
    def _():
        value = parts[0][...].astype(F32)
        for part in parts[1:]:
            value = value + part[...].astype(F32)
        total[...] = value
        slopes = total[rows:, :rows] + total[rows:, rows : 2 * rows]
        gates = gates_ref[...]
        mean = jnp.sum(gates * slopes, axis=0, keepdims=True)
        d_logits = (gates * (slopes - mean)).astype(BF16)
        d_routed = total[:rows, :] + dot_tn(d_logits, router[...])
        grad, d_gain = norm_back(residual_ref[...], gain[...], d_routed)
        d_residual = cot_ref[...].astype(F32) + grad
        d_res_ref[...] = d_residual
        d_branch_ref[...] = d_residual.astype(BF16)
        small_ref[:experts, :] = dot(d_logits, message_ref[:rows, :])
        small_ref[experts:, :] = jnp.broadcast_to(d_gain, (8, d_gain.shape[1]))

    d_mix_ref[...] = dot_nt(d_branch_ref[...], wo[...]).astype(BF16)


def back_through_branch(terms, residual, cot, gain, gates_t, router_t, message, wo, after=()):
    rows, width = residual.shape
    experts = gates_t.shape[0]
    tile = 256
    outs = (
        shaped((rows, width), F32),
        shaped((rows, width), BF16),
        shaped((experts + 8, width), F32),
    )
    d_mix = shaped((rows, wo.shape[0]), BF16)
    d_residual, d_branch, d_mix, small = kernel_call(
        13.8,
        functools.partial(back_body, len(terms)),
        (wo.shape[0] // tile,),
        [(a, whole(a)) for a in terms]
        + [(a, whole(a)) for a in (residual, cot, gain, gates_t, router_t, message)]
        + [(wo, pl.BlockSpec((tile, width), lambda i: (i, 0)))],
        [(s, whole(s)) for s in outs[:2]]
        + [(d_mix, pl.BlockSpec((rows, tile), lambda i: (0, i))), (outs[2], whole(outs[2]))],
        scratch=[pltpu.VMEM((rows + experts, width), F32)],
        after=after,
    )
    return d_residual, d_branch, d_mix, small


def output_body(starts, residual_ref, *refs):
    parts, out_ref = refs[:-1], refs[-1]
    cuts = sorted({0, residual_ref.shape[0], *starts})
    for low, high in zip(cuts[:-1], cuts[1:], strict=True):
        total = residual_ref[low:high, :]
        for part, start in zip(parts, starts, strict=True):
            if start <= low and high <= start + part.shape[0]:
                total = total + part[low - start : high - start, :].astype(F32)
        out_ref[low:high, :] = total.astype(BF16)


def layer_output(residual, terms):
    out = shaped(residual.shape, BF16)
    return kernel_call(
        5,
        functools.partial(output_body, tuple(start for _, start in terms)),
        (1,),
        [(a, whole(a)) for a in [residual] + [t for t, _ in terms]],
        [(out, whole(out))],
    )[0]


def key_value_back_body(members, held_ref, arrived_ref, cos_ref, sin_ref, own_ref, joined_ref):
    total = held_ref[...].astype(F32) + arrived_ref[...].astype(F32)
    kd = total.shape[1] // 2
    keys = [
        turn(total[:, h * HD : (h + 1) * HD], cos_ref[...], -sin_ref[...])
        for h in range(kd // HD)
    ]
    keys, values = jnp.concatenate(keys, axis=1), total[:, kd:]
    own_ref[:, :kd] = keys.astype(BF16)
    own_ref[:, kd:] = values.astype(BF16)
    part = kd // members
    joined = []
    for c in range(members):
        cols = slice(c * part, (c + 1) * part)
        joined += [keys[:, cols], values[:, cols]]
    joined_ref[...] = jnp.concatenate(joined, axis=1).astype(BF16)


def key_value_back(held, arrived, cos_wide, sin_wide, members):
    return kernel_call(
        2.6,
        functools.partial(key_value_back_body, members),
        (1,),
        [(a, whole(a)) for a in (held, arrived, cos_wide, sin_wide)],
        [(s, whole(s)) for s in [shaped(held.shape, BF16)] * 2],
    )


def finish_body(steps, dq_ref, dkv_ref, wq, wk, wv, x_ref, d_res_ref, gain, small_ref,
                d_hidden_ref, sums_ref, total):
    i = pl.program_id(0)
    kd = wk.shape[1]
    part = dot_nt(dq_ref[...], wq[...])
    part = part + dot_nt(dkv_ref[:, :kd], wk[...]) + dot_nt(dkv_ref[:, kd:], wv[...])
    total[:, column(i, part.shape[1])] = part

    @pl.when(i == steps - 1)
    def _():
        x = x_ref[...].astype(F32)
        grad, d_gain = norm_back(x, gain[...], total[...])
        d_hidden_ref[...] = d_res_ref[...] + grad
        lead = small_ref.shape[0] - 8
        sums_ref[:lead, :] = small_ref[:lead, :]
        row = lax.broadcasted_iota(jnp.int32, (8, 1), 0)
        sums_ref[lead:, :] = jnp.where(row == 1, d_gain, small_ref[lead:, :])


def finish(dq, dkv, wq, wk, wv, x, d_residual, gain, small, after=()):
    rows, width = x.shape
    tile = 256
    by_rows = lambda w: (w, pl.BlockSpec((tile, w.shape[1]), lambda i: (i, 0)))
    outs = (shaped((rows, width), F32), shaped(small.shape, F32))
    return kernel_call(
        13,
        functools.partial(finish_body, width // tile),
        (width // tile,),
        [(dq, whole(dq)), (dkv, whole(dkv)), by_rows(wq), by_rows(wk), by_rows(wv)]
        + [(a, whole(a)) for a in (x, d_residual, gain, small)],
        [(s, whole(s)) for s in outs],
        scratch=[pltpu.VMEM((rows, width), F32)],
        after=after,
    )


def per_device(
    hidden_in, cotangent, norm_attn, w_query, w_key, w_value, w_out, norm_ffn, w_router,
    w_gate, w_up, w_down, expert_ids, priority, prefix,
):
    group_count, span_len, width = hidden_in.shape
    row_count = group_count * span_len
    q_width, kv_width = w_query.shape[1], w_key.shape[1]
    kv_heads = kv_width // HD
    members, n_dp = lax.axis_size("expert"), lax.axis_size("dp")
    expert_count = w_router.shape[1]
    local_count = w_gate.shape[0]
    team_count = local_count // 2
    top_count = expert_ids.shape[3]
    slot_count = row_count * top_count * 5 // (expert_count * 4)
    capacity = 9 * row_count * members * top_count // (8 * expert_count)
    e_index, d_index = lax.axis_index("expert"), lax.axis_index("dp")
    parity = (d_index // TEAM_BIT) % 2
    first_local = parity * team_count
    first_expert = (e_index * local_count + first_local).reshape(1).astype(jnp.int32)
    e_steps = [("expert", bit) for bit in bits_of(members)]
    team = ("dp", TEAM_BIT)
    gain_one, gain_two = norm_attn.reshape(1, width), norm_ffn.reshape(1, width)
    router_t = w_router.T

    expert_range = jnp.arange(expert_count, dtype=jnp.int32)
    routes_t = expert_ids.reshape(row_count, top_count).T
    hit_t = jnp.any(routes_t[:, None, :] == expert_range[None, :, None], axis=0)
    tables = jnp.concatenate([routes_t, priority.reshape(1, row_count)], axis=0)[None]
    for axis_name, bit in [team] + e_steps:
        tables = jnp.concatenate([tables, swap(tables, axis_name, bit)], axis=0)

    offset = e_index * span_len
    positions = (offset + jnp.arange(span_len, dtype=jnp.int32)).astype(F32)
    frequency = ROPE_BASE ** (-(jnp.arange(HD // 2, dtype=F32) * 2.0 / HD))
    angles = positions[:, None] * frequency[None, :]
    cos_table, sin_table = jnp.cos(angles), jnp.sin(angles)
    cos_span = jnp.concatenate([cos_table, cos_table], axis=1)
    sin_span = jnp.concatenate([-sin_table, sin_table], axis=1)
    cos_wide, sin_wide = jnp.tile(cos_span, (group_count, 1)), jnp.tile(sin_span, (group_count, 1))
    x = hidden_in.reshape(row_count, width)
    cot = cotangent.reshape(row_count, width)
    normed, kv_own, queries, cot_later = project_inputs(
        x, gain_one, w_query, w_key, w_value, cos_wide, sin_wide, cot
    )
    kv = [kv_own.reshape(group_count, span_len, 2 * kv_width)]
    q = queries([tables])
    for number, (axis_name, bit) in enumerate(e_steps):
        arrived = [swap(piece, axis_name, bit) for piece in kv]
        kv = kv + arrived
    source = e_index ^ sum(
        ((jnp.arange(members) >> at) & 1) * bit for at, (_, bit) in enumerate(e_steps)
    )
    source = jnp.concatenate([source, offset.reshape(1)]).astype(jnp.int32)

    cut = row_count // 2

    far, near = ("expert", 2), ("expert", 1)

    def corner_of(over_z, over_y):
        return swap(over_z[:cut], *far), swap(over_y[cut:], *team)

    def over_near(piece):
        return tuple(swap(s, *near) for s in piece)

    def scatter_team(make):
        if members != 4:
            pieces = [make(at, [], 0)[0] for at in range(2 * members)]
            return [(scatter_pieces(pieces, [team] + e_steps), 0)]
        sent = {at: swap(make(at + 4, [], 0)[0], "expert", 1) for at in (3, 1, 2, 0)}
        low, high = make(3, [(sent[3], 0)], cut)
        from_y, from_z = swap(low, *far), swap(high, *team)
        own = make(0, [(sent[0], 0)], 0)[0]
        over_z = swap(make(1, [(sent[1], 0), (from_y, 0)], 0)[0], *team)
        over_y = swap(make(2, [(sent[2], 0), (from_z, cut)], 0)[0], *far)
        return [(own, 0), (over_z, 0), (over_y, 0)]

    split = members == 4
    if split:
        over_z = swap(hold(cot, [tables]), *team)
        cot_later = hold(cot_later, [tables, kv[1]])
        over_y = swap(cot_later, *far)
        near_own = over_near((cot,))
        cots = [(cot,), (over_z,), (over_y,)]
    else:
        cots = [(piece,) for piece in gather_pieces(cot, [team] + e_steps)]

    q = q.reshape(group_count, span_len, q_width)
    mix, lse = attend(q, kv, prefix, source)
    mix = mix.reshape(row_count, q_width)
    places = find_places(tables, first_expert, team_count, capacity, [mix])
    residual, message, gates_t = branch(
        x, mix, w_out, gain_two, router_t, hit_t.astype(F32), [over_z, over_y, places] if split else [places]
    )

    u_rows, gate_rows = {}, {}

    def send_rows(at, piece, after):
        u_rows[at], gate_rows[at] = dispatch(
            piece, at, places, first_expert, slot_count, True, after
        )

    if split:
        over_z, over_y = swap(message, *team), swap(message, *far)
        near_rows = over_near((message,))
    else:
        pieces = gather_pieces(message, [team] + e_steps)
    dz_rows = {}

    def own_rows(at, piece, after):
        dz_rows[at] = dispatch(piece, at, places, first_expert, slot_count, False, after)[0]
        return [dz_rows[at]]

    if split:
        over_cot_z, over_cot_y = (hold(cots[n][0], [places]) for n in (1, 2))
        corner = corner_of(over_cot_z, over_cot_y)
        near_z, near_y = over_near((over_cot_z,)), over_near((over_cot_y,))
        last = own_rows(0, cots[0], [places])
        last = own_rows(4, near_own, last)
        last = own_rows(1, (over_cot_z,), last)
        last = own_rows(2, (over_cot_y,), last)
        last = own_rows(5, near_z, last)
        last = own_rows(6, near_y, last)
        send_rows(0, (message,), last)
        send_rows(4, near_rows, [u_rows[0]])
        over_z, over_y = hold(over_z, [u_rows[4]]), hold(over_y, [u_rows[4]])
        corner_rows = corner_of(over_z, over_y)
        near_rows_z, near_rows_y = over_near((over_z,)), over_near((over_y,))
        send_rows(1, (over_z,), [])
        send_rows(2, (over_y,), [u_rows[1]])
        send_rows(5, near_rows_z, [u_rows[2]])
        send_rows(6, near_rows_y, [u_rows[5]])
        corner = tuple(hold(part, [u_rows[6]]) for part in corner)
        near_corner = over_near(corner)
        last = own_rows(3, corner, [u_rows[6]])
        corner_rows = tuple(hold(part, last) for part in corner_rows)
        near_corner_rows = over_near(corner_rows)
        last = own_rows(7, near_corner, last)
        send_rows(3, corner_rows, last)
        send_rows(7, near_corner_rows, [u_rows[3]])
    else:
        last = []
        for at, piece in enumerate(cots):
            last = own_rows(at, piece, last)
        for at, piece in enumerate(pieces):
            send_rows(at, (piece,), last)
    dz_rows = [dz_rows[at] for at in range(2 * members)]
    u_rows, gate_rows = ([rows[at] for at in range(2 * members)] for rows in (u_rows, gate_rows))
    d_order = [bit for bit in reversed(bits_of(n_dp)) if bit != TEAM_BIT] + [TEAM_BIT]
    kept_bits = sum(d_order[1:-1])
    me = (d_index - (d_index & kept_bits)).reshape(1).astype(jnp.int32)
    team_place = (d_index & TEAM_BIT).reshape(1).astype(jnp.int32)
    outs, backs, slopes, chains = [], [], [], []
    chunk = 8
    for e in range(team_count):
        expert = (first_local + e).reshape(1).astype(jnp.int32)
        joint = int(e == 3)
        parts = []
        for start in range(0, len(u_rows), chunk):
            span = slice(start, start + chunk)
            parts.append(
                expert_pass(
                    e, expert, team_place if joint else me, u_rows[span], dz_rows[span], gate_rows[span],
                    w_gate, w_up, w_down, n_dp, d_order, joint, slopes[-1:],
                )
            )
        if len(parts) == 1:
            out, back, slope, *grads = parts[0]
        else:
            out, back, slope = (jnp.concatenate([p[i] for p in parts], axis=0) for i in range(3))
            grads = [
                sum(p[i].astype(F32) for p in parts).astype(BF16) for i in range(3, len(parts[0]))
            ]
        outs.append(out)
        backs.append(back)
        slopes.append(slope)
        chains.append(grads[0] if joint else (grads[0], swap(grads[1], "dp", d_order[0])))
    pairs = {
        bit: [[d, d + bit] for d in range(n_dp) if (d // bit) % 2 == 0] for bit in d_order[1:-1]
    }

    def advance(e, after):
        if e >= team_count:
            return list(after)
        if e == 3:
            ranks = [
                sum(bit for at, bit in enumerate(d_order[:-1]) if (n_dp // 4 >> at) & r)
                for r in range(n_dp // 2)
            ]
            groups = [[side * TEAM_BIT + r for r in ranks] for side in range(2)]
            chains[e] = lax.psum_scatter(
                hold(chains[e], after), "dp", scatter_dimension=0, tiled=True,
                axis_index_groups=groups,
            )
            return list(after)
        total = mark = add_blocks(*chains[e], after)
        for bit in d_order[1:-1]:
            total = lax.psum_scatter(
                total, "dp", scatter_dimension=0, tiled=True, axis_index_groups=pairs[bit]
            )
        chains[e] = total
        return [mark]

    extra = expert_count

    first_marks, marked = advance(0, slopes[-1:]), []

    def make_back(at, added, cut_at):
        parts = combine(
            backs, at, places, slopes, first_expert, added, cut_at, extra,
            first_marks if at >= members else (),
        )
        marked.append(parts[0])
        return parts

    back_terms = [term for term, _ in scatter_team(make_back)]
    marks = advance(1, marked[-3:])
    d_residual, d_branch, d_mix, small = back_through_branch(
        back_terms, residual, cot, gain_two, gates_t, router_t, message, w_out, marks
    )

    member_order = [bit for _, bit in reversed(e_steps)]
    member_places = [
        sum(((q >> (len(member_order) - 1 - at)) & 1) * bit for at, bit in enumerate(member_order))
        for q in range(members)
    ]
    grad_places = jnp.concatenate(
        [e_index ^ jnp.array(member_places, jnp.int32), d_index.reshape(1)]
    ).astype(jnp.int32)
    w_order = list(reversed(bits_of(n_dp)))
    w_steps = [("expert", bit) for bit in member_order] + [("dp", bit) for bit in w_order]
    q_part, kv_part = q_width // members, kv_width // members
    w_parts = []

    def add_weight(left, right, total_cols, start, after):
        buffers = w_parts[-1] if start else []
        w_parts.append(
            weight_grad(
                left, right, grad_places, n_dp, members, w_order,
                total_cols, start, buffers, after,
            )
        )

    marks = advance(3, advance(2, [d_mix]))

    def out_rows(at, added, cut_at, after):
        return combine(outs, at, places, None, first_expert, added, cut_at, 0, after)

    if split:
        nears = {at: out_rows(at + 4, [], 0, marks)[0] for at in (3, 1, 2, 0)}
        sent = {at: swap(rows, *near) for at, rows in nears.items()}
        marks = list(nears.values())
    dq, d_kv = attend_back(
        q, d_mix.reshape(group_count, span_len, q_width), lse, kv, prefix, source,
        cos_span, sin_span, marks,
    )
    dq = dq.reshape(row_count, q_width)
    settled = []

    def settle_expert(e, held, after):
        result = hold(chains[e], held)
        slots = jnp.stack([first_local + e, team_count - first_local + e]).astype(jnp.int32)
        totals = settled[-1] if settled else []
        other = swap(result[1], *team)
        settled.append(settle(result[0], other, slots, local_count, totals, after))

    marks = [dq]
    if split:
        low, high = out_rows(3, [(sent[3], 0)], cut, marks)
        from_y, from_z = swap(low, *far), swap(high, *team)
        marks = [low]
    add_weight(mix, d_branch, 2 * q_part, 0, marks)
    add_weight(normed, dq, 2 * q_part, q_part, [])
    marks = w_parts[-1][:1]
    if split:
        own = out_rows(0, [(sent[0], 0)], 0, marks)[0]
        over_z = out_rows(1, [(sent[1], 0), (from_y, 0)], 0, marks)[0]
        over_y = out_rows(2, [(sent[2], 0), (from_z, cut)], 0, marks)[0]
        out_terms = [(own, 0), (swap(over_z, *team), 0), (swap(over_y, *far), 0)]
        marks = [own, over_z, over_y]
    else:
        out_terms = scatter_team(lambda at, added, cut_at: out_rows(at, added, cut_at, marks))
    last_step = e_steps[0]
    halves = [scatter_pieces(d_kv[at::2], e_steps[1:]) for at in range(2)]
    held, far_half = (h.reshape(row_count, 2 * kv_width) for h in halves)
    arrived = hold(swap(far_half, *last_step), marks)
    d_kv_own, joined = key_value_back(held, arrived, cos_wide, sin_wide, members)
    if q_part % 128 == 0:
        w_keep, w_send = w_parts[1]
    else:
        w_keep, w_send = (jnp.concatenate([p[i] for p in w_parts], axis=3) for i in range(2))
    w_marks = []
    grads = reduce_grad(w_keep, w_send, w_steps, [d_kv_own], w_marks)
    add_weight(normed, joined, 2 * kv_part, 0, w_marks[:1])
    d_hidden, sums = finish(
        dq, d_kv_own, w_query, w_key, w_value, x, d_residual, gain_one, small, [w_parts[-1][0]]
    )
    later = [d_hidden]
    output = layer_output(residual, out_terms)
    kv_keep, kv_send = w_parts[2]
    kv_grads = reduce_grad(kv_keep, hold(kv_send, later), w_steps)
    sums = all_sum(hold(sums, later), ("expert", "dp"))

    for e in range(len(settled), team_count):
        settle_expert(e, [dq] if e < 2 else [output], [output])
    grad_gate, grad_up, grad_down = settled[-1]
    return (
        output.reshape(group_count, span_len, width),
        d_hidden.reshape(group_count, span_len, width),
        sums[expert_count + 1],
        grads[:, q_part:],
        kv_grads[:, :kv_part],
        kv_grads[:, kv_part:],
        grads[:, :q_part],
        sums[expert_count],
        sums[:expert_count].T,
        grad_gate,
        grad_up,
        grad_down,
    )


def solution(mesh):
    in_specs = (
        P("dp", "expert", None),
        P("dp", "expert", None),
        P(),
        P(),
        P(),
        P(),
        P(),
        P(),
        P(),
        P("expert", None, None),
        P("expert", None, None),
        P("expert", None, None),
        P(("dp", "expert"), None, None, None),
        P(("dp", "expert"), None, None),
        P("dp"),
    )
    out_specs = (
        P("dp", "expert", None),
        P("dp", "expert", None),
        P(),
        P("dp", "expert"),
        P("dp", "expert"),
        P("dp", "expert"),
        P("dp", "expert"),
        P(),
        P(),
        P("expert", "dp", None),
        P("expert", "dp", None),
        P("expert", "dp", None),
    )
    return jax.shard_map(
        per_device, mesh=mesh, in_specs=in_specs, out_specs=out_specs, check_vma=False
    )
```

```python
import functools

import jax
import jax.numpy as jnp
from jax import lax
from jax.experimental import pallas as pl
from jax.experimental.pallas import tpu as pltpu
from jax.sharding import PartitionSpec as P

HD = 128
EPSILON = 1e-06
ROPE_BASE = 10000.0
MASKED = -1e30
EXTRA = 16
TEAM_BIT = 2
VMEM_LIMIT = 60 * 1024 * 1024

BF16 = jnp.bfloat16
F32 = jnp.float32


def dot(a, b):
    return jnp.dot(a, b, preferred_element_type=F32)


def dot_nt(a, b):
    return lax.dot_general(a, b, (((1,), (1,)), ((), ())), preferred_element_type=F32)


def dot_tn(a, b):
    return lax.dot_general(a, b, (((0,), (0,)), ((), ())), preferred_element_type=F32)


def bits_of(size):
    return [1 << i for i in reversed(range(size.bit_length() - 1))]


def swap(values, axis_name, bit):
    count = lax.axis_size(axis_name)
    return lax.ppermute(values, axis_name, [(i, i ^ bit) for i in range(count)])


def gather_pieces(values, steps):
    pieces = [values]
    for axis_name, bit in steps:
        pieces = pieces + [swap(piece, axis_name, bit) for piece in pieces]
    return pieces


def add_pair(a, b):
    return (a.astype(F32) + b.astype(F32)).astype(BF16)


def scatter_pieces(pieces, steps):
    for axis_name, bit in reversed(steps):
        half = len(pieces) // 2
        pieces = [
            add_pair(a, swap(b, axis_name, bit))
            for a, b in zip(pieces[:half], pieces[half:], strict=True)
        ]
    return pieces[0]


def all_sum(values, axes):
    for axis_name in axes:
        for bit in reversed(bits_of(lax.axis_size(axis_name))):
            values = values + swap(values, axis_name, bit)
    return values


ANYWHERE = pl.BlockSpec(memory_space=pl.ANY)


TIME_SCALE = 0.01


def kernel_call(us, body, grid, ins, outs, scalars=(), scratch=(), after=(), aliases=None):
    after = list(after)
    lead, held = len(scalars), len(ins)

    def run(*refs):
        body(*refs[: lead + held], *refs[lead + held + len(after) :])

    grid_spec = pltpu.PrefetchScalarGridSpec(
        num_scalar_prefetch=lead,
        grid=grid,
        in_specs=[spec for _, spec in ins] + [ANYWHERE] * len(after),
        out_specs=[spec for _, spec in outs],
        scratch_shapes=list(scratch),
    )
    return pl.pallas_call(
        run,
        grid_spec=grid_spec,
        out_shape=[shape for shape, _ in outs],
        input_output_aliases=aliases or {},
        compiler_params=pltpu.CompilerParams(vmem_limit_bytes=VMEM_LIMIT),
        cost_estimate=pl.CostEstimate(
            flops=int(us * TIME_SCALE * 1e9),
            bytes_accessed=int(us * TIME_SCALE * 3.3e6),
            transcendentals=0,
        ),
    )(*scalars, *[a for a, _ in ins], *after)


def shaped(shape, dtype):
    return jax.ShapeDtypeStruct(tuple(shape), dtype)


def whole(array):
    zeros = (0,) * len(array.shape)
    return pl.BlockSpec(tuple(array.shape), lambda *_: zeros)


def rms_of(values):
    return lax.rsqrt(jnp.mean(values * values, axis=-1, keepdims=True) + EPSILON)


def turn(values, cos_wide, sin_wide):
    return values * cos_wide + pltpu.roll(values, HD // 2, 1) * sin_wide


def column(width, tile):
    return pl.ds(pl.multiple_of(width * tile, tile), tile)


def hold_body(value_ref, out_ref):
    pass


def hold(value, after):
    return kernel_call(
        0.5, hold_body, (1,), [(value, ANYWHERE)], [(shaped(value.shape, value.dtype), ANYWHERE)],
        after=after, aliases={0: 0},
    )[0]


def key_value_body(x_ref, gain, wk, wv, cos_ref, sin_ref, cot_ref, normed_ref, kv_ref, same_ref):
    x = x_ref[...].astype(F32)
    normed = (x * rms_of(x) * gain[...]).astype(BF16)
    normed_ref[...] = normed
    keys = dot(normed, wk[...])
    for h in range(keys.shape[1] // HD):
        cols = slice(h * HD, (h + 1) * HD)
        kv_ref[:, cols] = turn(keys[:, cols], cos_ref[...], sin_ref[...]).astype(BF16)
    kv_ref[:, keys.shape[1] :] = dot(normed, wv[...]).astype(BF16)


def query_body(normed_ref, wq, cos_ref, sin_ref, q_ref):
    queries = dot(normed_ref[...], wq[...])
    for h in range(queries.shape[1] // HD):
        cols = slice(h * HD, (h + 1) * HD)
        q_ref[:, cols] = turn(queries[:, cols], cos_ref[...], sin_ref[...]).astype(BF16)


def project_inputs(x, gain, wq, wk, wv, cos_wide, sin_wide, cot):
    rows, width = x.shape
    kd = wk.shape[1]
    normed, kv, cot = kernel_call(
        4.2,
        key_value_body,
        (1,),
        [(a, whole(a)) for a in (x, gain, wk, wv, cos_wide, sin_wide)] + [(cot, ANYWHERE)],
        [(s, whole(s)) for s in (shaped((rows, width), BF16), shaped((rows, 2 * kd), BF16))]
        + [(shaped(cot.shape, BF16), ANYWHERE)],
        aliases={6: 2},
    )
    tile = 256

    def queries(after):
        return kernel_call(
            8,
            query_body,
            (wq.shape[1] // tile,),
            [
                (normed, whole(normed)),
                (wq, pl.BlockSpec((width, tile), lambda i: (0, i))),
                (cos_wide, whole(cos_wide)),
                (sin_wide, whole(sin_wide)),
            ],
            [(shaped((rows, wq.shape[1]), BF16), pl.BlockSpec((rows, tile), lambda i: (0, i)))],
            after=after,
        )[0]

    return normed, kv, queries, cot


def attention_bias(prefix, source, offset, span, members):
    rows = offset + lax.broadcasted_iota(jnp.int32, (span, span), 0)
    cols = lax.broadcasted_iota(jnp.int32, (span, span), 1)
    parts = []
    for p in range(members):
        keys = source[p] * span + cols
        parts.append(jnp.where((keys <= rows) | (keys < prefix), 0.0, MASKED))
    return jnp.concatenate(parts, axis=1)


def attention_body(members, kvh, ratio, prefix, source, q_ref, *refs):
    pieces, (mix_ref, lse_ref, bias) = refs[:members], refs[members:]
    span = q_ref.shape[1]
    scale = HD ** (-0.5)
    bias[...] = attention_bias(prefix[pl.program_id(0)], source, source[members], span, members)
    columns = []
    for k in range(kvh):
        keys = jnp.concatenate([p[0, :, k * HD : (k + 1) * HD] for p in pieces], axis=0)
        start = (kvh + k) * HD
        values = jnp.concatenate([p[0, :, start : start + HD] for p in pieces], axis=0)
        for r in range(ratio):
            cols = slice((k * ratio + r) * HD, (k * ratio + r + 1) * HD)
            scores = dot_nt(q_ref[0, :, cols], keys) + bias[...]
            top = jnp.max(scores, axis=1, keepdims=True)
            terms = jnp.exp((scores - top) * scale)
            total = jnp.sum(terms, axis=1, keepdims=True)
            mixed = dot(terms.astype(BF16), values)
            mix_ref[0, :, cols] = (mixed / total).astype(BF16)
            columns.append(top * scale + jnp.log(total))
    lse_ref[0] = jnp.concatenate(columns, axis=1)


def attention_back_body(
    members, kvh, ratio, prefix, source, q_ref, do_ref, lse_ref, cos_ref, sin_ref, *refs
):
    pieces, dq_ref = refs[:members], refs[members]
    outs, (bias, dk, dv) = refs[members + 1 : 2 * members + 1], refs[2 * members + 1 :]
    span = q_ref.shape[1]
    scale = HD ** (-0.5)
    bias[...] = attention_bias(prefix[pl.program_id(0)], source, source[members], span, members)
    for k in range(kvh):
        keys = jnp.concatenate([p[0, :, k * HD : (k + 1) * HD] for p in pieces], axis=0)
        start = (kvh + k) * HD
        values = jnp.concatenate([p[0, :, start : start + HD] for p in pieces], axis=0)
        for r in range(ratio):
            h = k * ratio + r
            cols = slice(h * HD, (h + 1) * HD)
            query, upstream = q_ref[0, :, cols], do_ref[0, :, cols]
            scores = dot_nt(query, keys) + bias[...]
            probs = jnp.exp(scores * scale - lse_ref[0, :, h : h + 1])
            d_probs = dot_nt(upstream, values)
            mean = jnp.sum(probs * d_probs, axis=1, keepdims=True)
            d_scores = (probs * (d_probs - mean)).astype(BF16)
            d_query = dot(d_scores, keys) * scale
            dq_ref[0, :, cols] = turn(d_query, cos_ref[...], -sin_ref[...]).astype(BF16)
            part_k = dot_tn(d_scores, query)
            part_v = dot_tn(probs.astype(BF16), upstream)
            if r == 0:
                dk[...] = part_k
                dv[...] = part_v
            else:
                dk[...] += part_k
                dv[...] += part_v
        for p, out in enumerate(outs):
            rows = slice(p * span, (p + 1) * span)
            out[0, :, k * HD : (k + 1) * HD] = (dk[rows, :] * scale).astype(BF16)
            out[0, :, start : start + HD] = dv[rows, :].astype(BF16)


def attend(q, kv, prefix, source):
    groups, span, qd = q.shape
    members, kvh = len(kv), kv[0].shape[2] // (2 * HD)
    heads = qd // HD
    block = lambda n: pl.BlockSpec((1, span, n), lambda g, *_: (g, 0, 0))
    return kernel_call(
        15.7,
        functools.partial(attention_body, members, kvh, heads // kvh),
        (groups,),
        [(q, block(qd))] + [(p, block(p.shape[2])) for p in kv],
        [
            (shaped(q.shape, BF16), block(qd)),
            (shaped((groups, span, heads), F32), block(heads)),
        ],
        scalars=(prefix, source),
        scratch=[pltpu.VMEM((span, span * members), F32)],
    )


def attend_back(q, do, lse, kv, prefix, source, cos_wide, sin_wide, after=()):
    groups, span, qd = q.shape
    members, kvh = len(kv), kv[0].shape[2] // (2 * HD)
    heads = qd // HD
    block = lambda n: pl.BlockSpec((1, span, n), lambda g, *_: (g, 0, 0))
    outs = kernel_call(
        28.6,
        functools.partial(attention_back_body, members, kvh, heads // kvh),
        (groups,),
        [(q, block(qd)), (do, block(qd)), (lse, block(heads))]
        + [(cos_wide, whole(cos_wide)), (sin_wide, whole(sin_wide))]
        + [(p, block(p.shape[2])) for p in kv],
        [(shaped(q.shape, BF16), block(qd))]
        + [(shaped(p.shape, BF16), block(p.shape[2])) for p in kv],
        scalars=(prefix, source),
        scratch=[
            pltpu.VMEM((span, span * members), F32),
            pltpu.VMEM((span * members, HD), F32),
            pltpu.VMEM((span * members, HD), F32),
        ],
        after=after,
    )
    return outs[0], outs[1:]


def branch_body(steps, x_ref, mix_ref, wo, gain, router, hit_ref,
                residual_ref, message_ref, gates_ref):
    i = pl.program_id(0)
    tile = wo.shape[1]
    cols = column(i, tile)
    residual_ref[:, cols] = x_ref[:, cols].astype(F32) + dot(mix_ref[...], wo[...])

    @pl.when(i == steps - 1)
    def _():
        rows = residual_ref.shape[0]
        experts = hit_ref.shape[0]
        h1 = residual_ref[...]
        a2 = (h1 * rms_of(h1) * gain[...]).astype(BF16)
        message_ref[:rows, :] = a2
        hit = hit_ref[...] > 0.0
        logits = jnp.where(hit, dot_nt(router[...], a2), MASKED)
        terms = jnp.exp(logits - jnp.max(logits, axis=0, keepdims=True))
        terms = jnp.where(hit, terms, 0.0)
        gates = terms / jnp.sum(terms, axis=0, keepdims=True)
        gates_ref[...] = gates
        high = gates.astype(BF16)
        rest = gates - high.astype(F32)
        middle = rest.astype(BF16)
        low = (rest - middle.astype(F32)).astype(BF16)
        message_ref[rows:, :rows] = high
        message_ref[rows:, rows : 2 * rows] = middle
        message_ref[rows:, 2 * rows : 3 * rows] = low
        if message_ref.shape[1] > 3 * rows:
            message_ref[rows:, 3 * rows :] = jnp.zeros(
                (experts, message_ref.shape[1] - 3 * rows), BF16
            )


def branch(x, mix, wo, gain, router_t, hit_t, after=()):
    rows, width = x.shape
    experts = router_t.shape[0]
    tile = 256
    outs = (
        shaped((rows, width), F32),
        shaped((rows + experts, width), BF16),
        shaped((experts, rows), F32),
    )
    return kernel_call(
        10,
        functools.partial(branch_body, width // tile),
        (width // tile,),
        [(x, whole(x)), (mix, whole(mix))]
        + [(wo, pl.BlockSpec((wo.shape[0], tile), lambda i: (0, i)))]
        + [(a, whole(a)) for a in (gain, router_t, hit_t)],
        [(s, whole(s)) for s in outs],
        after=after,
    )


def slot_masks(places, slot_count):
    experts, tokens = places.shape
    slots = lax.broadcasted_iota(jnp.int32, (slot_count, tokens), 0).astype(F32)
    return [places[e : e + 1, :] == slots for e in range(experts)]


def hot_rows(masks):
    return jnp.concatenate([m.astype(F32) for m in masks], axis=0).astype(BF16)


def pick_experts(table, first, count):
    row = lax.broadcasted_iota(jnp.int32, table.shape, 0)
    picked = [
        jnp.sum(jnp.where(row == first + e, table, 0.0), axis=0, keepdims=True)
        for e in range(count)
    ]
    return jnp.concatenate(picked, axis=0)


def places_body(blocks, count, capacity, first, table_ref, column_ref, out_ref):
    b = pl.program_id(0)
    tokens = table_ref.shape[2]
    top = table_ref.shape[1] - 1
    padded = 8

    def hits(at):
        row = lax.broadcasted_iota(jnp.int32, (padded, tokens), 0)
        expert = jnp.where(row < count, first[0] + row, -1)
        found = table_ref[at, 0:1, :] == expert
        for k in range(1, top):
            found = found | (table_ref[at, k : k + 1, :] == expert)
        return found

    own_order = table_ref[b, top : top + 1, :]
    before = jnp.zeros((padded, tokens), F32)
    for n in range(blocks // 2):
        at = 2 * n + b % 2
        earlier = jnp.where(column_ref[at] < own_order, 1.0, 0.0).astype(BF16)
        before = before + dot(jnp.where(hits(at), 1.0, 0.0).astype(BF16), earlier)
    kept = hits(b) & (before < capacity)
    row = lax.broadcasted_iota(jnp.int32, (tokens, tokens), 0)
    col = lax.broadcasted_iota(jnp.int32, (tokens, tokens), 1)
    ahead = jnp.where(row < col, 1.0, 0.0).astype(BF16)
    slots = dot(jnp.where(kept, 1.0, 0.0).astype(BF16), ahead)
    out_ref[0] = jnp.where(kept, slots, -1.0)[:count]


def find_places(tables, first, count, capacity, after=()):
    blocks, wide, tokens = tables.shape
    columns = tables[:, wide - 1, :, None]
    shape = shaped((blocks, count, tokens), F32)
    return kernel_call(
        4,
        functools.partial(places_body, blocks, count, capacity),
        (blocks,),
        [(tables, whole(tables)), (columns, whole(columns))],
        [(shape, pl.BlockSpec((1, count, tokens), lambda b, *_: (b, 0, 0)))],
        scalars=(first,),
        after=after,
    )[0]


def dispatch_body(parts, with_gates, slot_count, first, *refs):
    segments, refs = refs[:parts], refs[parts:]
    if with_gates:
        extra_ref, places_ref, rows_ref, gate_ref = refs
    else:
        places_ref, rows_ref = refs
    _, count, tokens = places_ref.shape
    masks = slot_masks(places_ref[0], slot_count)
    hot = hot_rows(masks)
    if with_gates:
        extra = extra_ref[...].astype(F32)
        table = extra[:, :tokens] + extra[:, tokens : 2 * tokens]
        gates = pick_experts(table + extra[:, 2 * tokens : 3 * tokens], first[0], count)
        for e in range(count):
            gate = jnp.sum(jnp.where(masks[e], gates[e : e + 1, :], 0.0), axis=1, keepdims=True)
            gate_ref[e] = jnp.broadcast_to(gate, (slot_count, 128))
    total, start = 0.0, 0
    for segment in segments:
        stop = min(start + segment.shape[0], tokens)
        total = total + dot(hot[:, start:stop], segment[: stop - start, :])
        start = stop
    total = total.astype(BF16)
    for e in range(count):
        rows_ref[e] = total[e * slot_count : (e + 1) * slot_count]


def dispatch(segments, at, places, first, slot_count, with_gates, after=()):
    width = segments[0].shape[1]
    _, count, tokens = places.shape
    ins = [(a, whole(a)) for a in segments]
    outs = [shaped((count, slot_count, width), BF16)]
    if with_gates:
        last = segments[-1]
        extra = last.shape[0] - (tokens - sum(a.shape[0] for a in segments[:-1]))
        spot = last.shape[0] // extra - 1
        ins.append((last, pl.BlockSpec((extra, width), lambda *_: (spot, 0))))
        outs.append(shaped((count, slot_count, 128), F32))
    ins.append((places, pl.BlockSpec((1, count, tokens), lambda *_: (at, 0, 0))))
    return kernel_call(
        1.5,
        functools.partial(dispatch_body, len(segments), with_gates, slot_count),
        (1,),
        ins,
        [(o, whole(o)) for o in outs],
        scalars=(first,),
        after=after,
    )


def combine_body(experts, with_extra, starts, cut, first, *refs):
    refs = list(refs)
    rows = [refs.pop(0) for _ in range(experts)]
    places_ref = refs.pop(0)
    slopes = [refs.pop(0) for _ in range(experts)] if with_extra else None
    added = [refs.pop(0) for _ in starts]
    outs = refs
    slot_count = rows[0].shape[1]
    tokens = places_ref.shape[2]
    masks = slot_masks(places_ref[0], slot_count)
    values = jnp.concatenate([r[0] for r in rows], axis=0)
    total = dot_tn(hot_rows(masks), values)
    last = outs[-1]
    width = last.shape[1]
    for other, start in zip(added, starts, strict=True):
        count = min(other.shape[0], tokens - start)
        parts = [total[start : start + count] + other[:count, :].astype(F32)]
        if start > 0:
            parts = [total[:start]] + parts
        if start + count < tokens:
            parts.append(total[start + count :])
        total = parts[0] if len(parts) == 1 else jnp.concatenate(parts, axis=0)
    total = total.astype(BF16)
    if cut:
        outs[0][...] = total[:cut]
    last[: tokens - cut, :] = total[cut:]
    if with_extra:
        count = last.shape[0] - (tokens - cut)
        row = lax.broadcasted_iota(jnp.int32, (count, tokens), 0)
        table = jnp.zeros((count, tokens), F32)
        for e in range(experts):
            slope = jnp.sum(jnp.where(masks[e], slopes[e][0, :, :1], 0.0), axis=0, keepdims=True)
            table = jnp.where(row == first[0] + e, slope, table)
        high = table.astype(BF16).astype(F32)
        for side, value in enumerate((high, table - high)):
            cols = slice(side * tokens, (side + 1) * tokens)
            for other, start in zip(added, starts, strict=True):
                if start + other.shape[0] > tokens:
                    value = value + other[tokens - start :, cols].astype(F32)
            last[tokens - cut :, cols] = value.astype(BF16)
        last[tokens - cut :, 2 * tokens :] = jnp.zeros((count, width - 2 * tokens), BF16)


def combine(rows, at, places, slopes, first, added, cut, extra, after=()):
    experts = len(rows)
    _, slot_count, width = rows[0].shape
    _, count, tokens = places.shape
    block = lambda n: pl.BlockSpec((1, slot_count, n), lambda *_: (at, 0, 0))
    ins = [(r, block(width)) for r in rows]
    ins.append((places, pl.BlockSpec((1, count, tokens), lambda *_: (at, 0, 0))))
    if slopes is not None:
        ins += [(s, block(128)) for s in slopes]
    ins += [(a, whole(a)) for a, _ in added]
    long = tokens + (extra if slopes is not None else 0)
    outs = [shaped((cut, width), BF16)] if cut else []
    outs.append(shaped((long - cut, width), BF16))
    starts = tuple(start for _, start in added)
    return kernel_call(
        1.2,
        functools.partial(combine_body, experts, slopes is not None, starts, cut),
        (1,),
        ins,
        [(s, whole(s)) for s in outs],
        scalars=(first,),
        after=after,
    )


def expert_body(index, blocks, joint, n_dp, order, expert_ref, me_ref, *refs):
    refs = list(refs)
    u_hbm = [refs.pop(0) for _ in range(blocks)]
    dz_hbm = [refs.pop(0) for _ in range(blocks)]
    gate_hbm = [refs.pop(0) for _ in range(blocks)]
    wg_hbm, wu_hbm, wd_hbm, yg_hbm, du_hbm, slope_ref = refs[:6]
    grads_hbm, refs = refs[6 : 8 - joint], refs[8 - joint :]
    (
        u_ref, dz_ref, gate_ref, wg, wu, wd, ha, side_gate, side_up, dy, dga, dua, yg, du, stage,
        row_sems, sems,
    ) = refs
    _, slot_count, width = u_ref.shape
    rows = blocks * slot_count
    ff = ha.shape[1]
    expert, me = expert_ref[0], me_ref[0]

    def loads(sources, target, at):
        return [
            pltpu.make_async_copy(s.at[index], target.at[b], row_sems.at[at, b])
            for b, s in enumerate(sources)
        ]

    u_loads, dz_loads, gate_loads = (
        loads(u_hbm, u_ref, 0), loads(dz_hbm, dz_ref, 1), loads(gate_hbm, gate_ref, 2)
    )
    w_loads = [
        pltpu.make_async_copy(source.at[expert], target, sems.at[at])
        for at, (source, target) in enumerate(((wg_hbm, wg), (wu_hbm, wu), (wd_hbm, wd)))
    ]
    first, second = u_loads + w_loads[:2], w_loads[2:] + gate_loads + dz_loads
    for load in first + second:
        load.start()
    for load in first:
        load.wait()
    tile = 256

    @pl.loop(0, ff // tile)
    def _(t):
        cols = column(t, tile)
        u = u_ref[...].reshape(rows, width)
        a = dot(u, wg[:, cols])
        b = dot(u, wu[:, cols])
        cdf = 0.5 * (1.0 + lax.erf(a * 0.7071067811865476))
        pdf = jnp.exp(-0.5 * a * a) * 0.3989422804014327
        glu = a * cdf
        ha[:, cols] = (glu * b).astype(BF16)
        side_gate[:, cols] = b * (cdf + a * pdf)
        side_up[:, cols] = glu

    for load in second:
        load.wait()
    slope_ref[...] = jnp.zeros_like(slope_ref)

    @pl.loop(0, width // tile)
    def _(t):
        cols = column(t, tile)
        gate = gate_ref[...].reshape(rows, 128)[:, :1]
        y = dot(ha[...], wd[:, cols]).astype(BF16).astype(F32)
        dz = dz_ref[:, :, cols].reshape(rows, tile).astype(F32)
        part = jnp.sum(dz * y, axis=1, keepdims=True)
        slope_ref[...] += jnp.broadcast_to(part, (rows, 128)).reshape(blocks, slot_count, 128)
        yg[:, :, cols] = (gate * y).astype(BF16).reshape(blocks, slot_count, tile)
        dy[:, cols] = (gate * dz).astype(BF16)

    out_yg = pltpu.make_async_copy(yg, yg_hbm, sems.at[3])
    out_yg.start()

    @pl.loop(0, ff // tile)
    def _(t):
        cols = column(t, tile)
        dha = dot_nt(dy[...], wd[cols, :])
        dga[:, cols] = (dha * side_gate[:, cols]).astype(BF16)
        dua[:, cols] = (dha * side_up[:, cols]).astype(BF16)

    wide = 384
    deep = width // n_dp
    flat = ff // n_dp

    def spot(block):
        return place_of(block ^ me, order, n_dp)

    @pl.loop(0, width // wide)
    def _(t):
        cols = column(t, wide)
        ut = u_ref[:, :, cols].reshape(rows, wide)
        for which, grad in ((0, dga), (1, dua)):
            d_weight = dot_tn(ut, grad[...]).astype(BF16)
            for i in range(wide // deep):
                at = spot(t * (wide // deep) + i)
                stage[at, which] = d_weight[i * deep : (i + 1) * deep]

    @pl.loop(0, ff // wide)
    def _(t):
        cols = column(t, wide)
        d_weight = dot_tn(ha[:, cols], dy[...]).astype(BF16)
        for i in range(wide // flat):
            at = spot(t * (wide // flat) + i)
            part = d_weight[i * flat : (i + 1) * flat]
            stage[at, 2, :flat] = part[:, :ff]
            stage[at, 2, flat:] = part[:, ff:]

    part = n_dp // len(grads_hbm)
    out_grads = [
        pltpu.make_async_copy(stage.at[pl.ds(side * part, part)], target, sems.at[5 + side])
        for side, target in enumerate(grads_hbm)
    ]
    for copy in out_grads:
        copy.start()

    @pl.loop(0, width // tile)
    def _(t):
        cols = column(t, tile)
        back = dot_nt(dga[...], wg[cols, :]) + dot_nt(dua[...], wu[cols, :])
        du[:, :, cols] = back.astype(BF16).reshape(blocks, slot_count, tile)

    out_du = pltpu.make_async_copy(du, du_hbm, sems.at[4])
    out_du.start()
    out_yg.wait()
    for copy in out_grads:
        copy.wait()
    out_du.wait()


def place_of(index, order, count):
    place = 0
    for at, bit in enumerate(order):
        place = place + ((index // bit) % 2) * (count >> (at + 1))
    return place


def expert_pass(index, expert, me, u, dz, gates, wg, wu, wd, n_dp, order, joint, after=()):
    blocks = len(u)
    _, slot_count, width = u[0].shape
    ff = wg.shape[2]
    rows = blocks * slot_count
    deep = width // n_dp
    packed = [shaped((n_dp // (2 - joint), 3, deep, ff), BF16)] * (2 - joint)
    row_shape = shaped((blocks, slot_count, width), BF16)
    slope_shape = shaped((blocks, slot_count, 128), F32)
    return kernel_call(
        26.5,
        functools.partial(expert_body, index, blocks, joint, n_dp, order),
        (1,),
        [(a, ANYWHERE) for a in list(u) + list(dz) + list(gates) + [wg, wu, wd]],
        [
            (row_shape, ANYWHERE),
            (row_shape, ANYWHERE),
            (slope_shape, whole(slope_shape)),
        ]
        + [(p, ANYWHERE) for p in packed],
        scalars=(expert, me),
        scratch=[
            pltpu.VMEM((blocks, slot_count, width), BF16),
            pltpu.VMEM((blocks, slot_count, width), BF16),
            pltpu.VMEM((blocks, slot_count, 128), F32),
            pltpu.VMEM((width, ff), BF16),
            pltpu.VMEM((width, ff), BF16),
            pltpu.VMEM((ff, width), BF16),
            pltpu.VMEM((rows, ff), BF16),
            pltpu.VMEM((rows, ff), F32),
            pltpu.VMEM((rows, ff), F32),
            pltpu.VMEM((rows, width), BF16),
            pltpu.VMEM((rows, ff), BF16),
            pltpu.VMEM((rows, ff), BF16),
            pltpu.VMEM((blocks, slot_count, width), BF16),
            pltpu.VMEM((blocks, slot_count, width), BF16),
            pltpu.VMEM((n_dp, 3, width // n_dp, ff), BF16),
            pltpu.SemaphoreType.DMA((3, blocks)),
            pltpu.SemaphoreType.DMA((8,)),
        ],
        after=after,
    )


def add_split_body(a_ref, b_ref, c_ref, d_ref, keep_ref, send_ref):
    keep_ref[...] = (a_ref[...].astype(F32) + b_ref[...].astype(F32)).astype(keep_ref.dtype)
    send_ref[...] = (c_ref[...].astype(F32) + d_ref[...].astype(F32)).astype(BF16)


def add_split(held, arrived, axis, last=False, after=()):
    half = held.shape[axis] // 2
    shape = list(held.shape)
    shape[axis] = half
    block = [1 if at == axis else size for at, size in enumerate(held.shape)]
    spot = lambda shift: lambda i: tuple(i + shift if at == axis else 0 for at in range(len(block)))
    low, high = pl.BlockSpec(tuple(block), spot(0)), pl.BlockSpec(tuple(block), spot(half))
    return kernel_call(
        4.5,
        add_split_body,
        (half,),
        [(held, low), (arrived, low), (held, high), (arrived, high)],
        [(shaped(shape, F32 if last else BF16), low), (shaped(shape, BF16), low)],
        after=after,
    )


def add_body(a_ref, b_ref, out_ref):
    out_ref[...] = (a_ref[...].astype(F32) + b_ref[...].astype(F32)).astype(BF16)


def add_blocks(held, arrived, after):
    block = pl.BlockSpec((1, *held.shape[1:]), lambda i: (i, 0, 0, 0))
    return kernel_call(
        4.5, add_body, held.shape[:1], [(held, block), (arrived, block)],
        [(shaped(held.shape, BF16), block)], after=after,
    )[0]


def settle_body(slots, own_ref, other_ref, *refs):
    outs = refs[-3:]

    def write(part):
        for m, out in enumerate(outs):
            value = part[m].astype(F32)
            if m == 2:
                flat = out.shape[1]
                value = jnp.concatenate([value[:flat], value[flat:]], axis=1)
            out[0] = value

    @pl.when(pl.program_id(0) == 0)
    def _():
        write(own_ref)

    @pl.when(pl.program_id(0) == 1)
    def _():
        write(other_ref)


def settle(own, other, slots, local_count, totals, after=()):
    _, deep, ff = own.shape
    shapes = [
        shaped((local_count, deep, ff), F32),
        shaped((local_count, deep, ff), F32),
        shaped((local_count, deep // 2, 2 * ff), F32),
    ]
    out_spec = lambda s: pl.BlockSpec((1, *s.shape[1:]), lambda i, slots: (slots[i], 0, 0))
    ins = [(own, whole(own)), (other, whole(other))] + [(t, ANYWHERE) for t in totals]
    return kernel_call(
        4.3,
        settle_body,
        (2,),
        ins,
        [(s, out_spec(s)) for s in shapes],
        scalars=(slots,),
        aliases={3 + i: i for i in range(len(totals))},
        after=after,
    )


def weight_grad_body(half, wide, order, n_dp, places, left_ref, right_ref, *refs):
    keep_ref, send_ref = refs[-2:]
    q = pl.program_id(0)
    width = left_ref.shape[1]
    deep = width // n_dp

    def fill(out_ref):
        right = right_ref[...].reshape(left_ref.shape[0], right_ref.shape[-1])
        for t in range(width // wide):
            part = dot_tn(left_ref[:, t * wide : (t + 1) * wide], right).astype(BF16)
            for i in range(wide // deep):
                at = place_of((t * (wide // deep) + i) ^ places[2 * half], order, n_dp)
                out_ref[0, at] = part[i * deep : (i + 1) * deep]

    @pl.when(q < half)
    def _():
        fill(keep_ref)

    @pl.when(q >= half)
    def _():
        fill(send_ref)


def weight_grad(left, right, places, n_dp, members, order, total_cols, start, buffers, after=()):
    rows, width = left.shape
    cols = right.shape[1] // members
    half = members // 2
    deep = width // n_dp
    if cols % 128 == 0:
        right_in = (right, pl.BlockSpec((rows, cols), lambda q, places: (0, places[q])))
    else:
        right = jnp.swapaxes(right.reshape(rows, members, cols), 0, 1)
        right_in = (right, pl.BlockSpec((1, rows, cols), lambda q, places: (places[q], 0, 0)))
        total_cols, start, buffers = cols, 0, []
    block = (1, n_dp, deep, cols)
    shape = shaped((half, n_dp, deep, total_cols), BF16)
    at = start // cols
    ins = [(left, whole(left)), right_in] + [(b, ANYWHERE) for b in buffers]
    return kernel_call(
        7,
        functools.partial(weight_grad_body, half, 384, order, n_dp),
        (members,),
        ins,
        [
            (shape, pl.BlockSpec(block, lambda q, places: (jnp.minimum(q, half - 1), 0, 0, at))),
            (shape, pl.BlockSpec(block, lambda q, places: (jnp.maximum(q - half, 0), 0, 0, at))),
        ],
        scalars=(places,),
        aliases={3 + i: i for i in range(len(buffers))},
        after=after,
    )


def reduce_grad(keep, send, steps, after=(), marks=None, late=None):
    outer = keep.shape[0].bit_length()
    arrived = swap(send, *steps[0])
    for at in range(1, len(steps)):
        if at == outer:
            keep, arrived = keep[0], arrived[0]
        keep, send = add_split(keep, arrived, 0, False, after if at == 1 else ())
        if marks is not None:
            marks.append(keep)
        if late is not None and steps[at] == ("dp", TEAM_BIT):
            send = hold(send, late(keep))
        arrived = swap(send, *steps[at])
    return keep[0].astype(F32) + arrived[0].astype(F32)


def norm_back(inputs, gain, upstream):
    scale = rms_of(inputs)
    weighted = gain * upstream
    middle = jnp.mean(inputs * weighted, axis=1, keepdims=True)
    grad = scale * weighted - inputs * (scale * scale * scale) * middle
    return grad, jnp.sum(upstream * inputs * scale, axis=0, keepdims=True)


def back_body(terms, *refs):
    refs = list(refs)
    parts = [refs.pop(0) for _ in range(terms)]
    (
        residual_ref, cot_ref, gain, gates_ref, router, message_ref, wo,
        d_res_ref, d_branch_ref, d_mix_ref, small_ref, total,
    ) = refs
    rows = residual_ref.shape[0]
    experts = gates_ref.shape[0]

    @pl.when(pl.program_id(0) == 0)
    def _():
        value = parts[0][...].astype(F32)
        for part in parts[1:]:
            value = value + part[...].astype(F32)
        total[...] = value
        slopes = total[rows:, :rows] + total[rows:, rows : 2 * rows]
        gates = gates_ref[...]
        mean = jnp.sum(gates * slopes, axis=0, keepdims=True)
        d_logits = (gates * (slopes - mean)).astype(BF16)
        d_routed = total[:rows, :] + dot_tn(d_logits, router[...])
        grad, d_gain = norm_back(residual_ref[...], gain[...], d_routed)
        d_residual = cot_ref[...].astype(F32) + grad
        d_res_ref[...] = d_residual
        d_branch_ref[...] = d_residual.astype(BF16)
        small_ref[:experts, :] = dot(d_logits, message_ref[:rows, :])
        small_ref[experts:, :] = jnp.broadcast_to(d_gain, (8, d_gain.shape[1]))

    d_mix_ref[...] = dot_nt(d_branch_ref[...], wo[...]).astype(BF16)


def back_through_branch(terms, residual, cot, gain, gates_t, router_t, message, wo, after=()):
    rows, width = residual.shape
    experts = gates_t.shape[0]
    tile = 256
    outs = (
        shaped((rows, width), F32),
        shaped((rows, width), BF16),
        shaped((experts + 8, width), F32),
    )
    d_mix = shaped((rows, wo.shape[0]), BF16)
    d_residual, d_branch, d_mix, small = kernel_call(
        13.8,
        functools.partial(back_body, len(terms)),
        (wo.shape[0] // tile,),
        [(a, whole(a)) for a in terms]
        + [(a, whole(a)) for a in (residual, cot, gain, gates_t, router_t, message)]
        + [(wo, pl.BlockSpec((tile, width), lambda i: (i, 0)))],
        [(s, whole(s)) for s in outs[:2]]
        + [(d_mix, pl.BlockSpec((rows, tile), lambda i: (0, i))), (outs[2], whole(outs[2]))],
        scratch=[pltpu.VMEM((rows + experts, width), F32)],
        after=after,
    )
    return d_residual, d_branch, d_mix, small


def output_body(starts, residual_ref, *refs):
    parts, out_ref = refs[:-1], refs[-1]
    cuts = sorted({0, residual_ref.shape[0], *starts})
    for low, high in zip(cuts[:-1], cuts[1:], strict=True):
        total = residual_ref[low:high, :]
        for part, start in zip(parts, starts, strict=True):
            if start <= low and high <= start + part.shape[0]:
                total = total + part[low - start : high - start, :].astype(F32)
        out_ref[low:high, :] = total.astype(BF16)


def layer_output(residual, terms, after=()):
    out = shaped(residual.shape, BF16)
    return kernel_call(
        5,
        functools.partial(output_body, tuple(start for _, start in terms)),
        (1,),
        [(a, whole(a)) for a in [residual] + [t for t, _ in terms]],
        [(out, whole(out))],
        after=after,
    )[0]


def key_value_back_body(members, held_ref, arrived_ref, cos_ref, sin_ref, own_ref, joined_ref):
    total = held_ref[...].astype(F32) + arrived_ref[...].astype(F32)
    kd = total.shape[1] // 2
    keys = [
        turn(total[:, h * HD : (h + 1) * HD], cos_ref[...], -sin_ref[...])
        for h in range(kd // HD)
    ]
    keys, values = jnp.concatenate(keys, axis=1), total[:, kd:]
    own_ref[:, :kd] = keys.astype(BF16)
    own_ref[:, kd:] = values.astype(BF16)
    part = kd // members
    joined = []
    for c in range(members):
        cols = slice(c * part, (c + 1) * part)
        joined += [keys[:, cols], values[:, cols]]
    joined_ref[...] = jnp.concatenate(joined, axis=1).astype(BF16)


def key_value_back(held, arrived, cos_wide, sin_wide, members):
    return kernel_call(
        2.6,
        functools.partial(key_value_back_body, members),
        (1,),
        [(a, whole(a)) for a in (held, arrived, cos_wide, sin_wide)],
        [(s, whole(s)) for s in [shaped(held.shape, BF16)] * 2],
    )


def finish_body(steps, dq_ref, dkv_ref, wq, wk, wv, x_ref, d_res_ref, gain, small_ref,
                d_hidden_ref, sums_ref, total):
    i = pl.program_id(0)
    kd = wk.shape[1]
    part = dot_nt(dq_ref[...], wq[...])
    part = part + dot_nt(dkv_ref[:, :kd], wk[...]) + dot_nt(dkv_ref[:, kd:], wv[...])
    total[:, column(i, part.shape[1])] = part

    @pl.when(i == steps - 1)
    def _():
        x = x_ref[...].astype(F32)
        grad, d_gain = norm_back(x, gain[...], total[...])
        d_hidden_ref[...] = d_res_ref[...] + grad
        lead = small_ref.shape[0] - 8
        sums_ref[:lead, :] = small_ref[:lead, :]
        row = lax.broadcasted_iota(jnp.int32, (8, 1), 0)
        sums_ref[lead:, :] = jnp.where(row == 1, d_gain, small_ref[lead:, :])


def finish(dq, dkv, wq, wk, wv, x, d_residual, gain, small, after=()):
    rows, width = x.shape
    tile = 256
    by_rows = lambda w: (w, pl.BlockSpec((tile, w.shape[1]), lambda i: (i, 0)))
    outs = (shaped((rows, width), F32), shaped(small.shape, F32))
    return kernel_call(
        13,
        functools.partial(finish_body, width // tile),
        (width // tile,),
        [(dq, whole(dq)), (dkv, whole(dkv)), by_rows(wq), by_rows(wk), by_rows(wv)]
        + [(a, whole(a)) for a in (x, d_residual, gain, small)],
        [(s, whole(s)) for s in outs],
        scratch=[pltpu.VMEM((rows, width), F32)],
        after=after,
    )


def per_device(
    hidden_in, cotangent, norm_attn, w_query, w_key, w_value, w_out, norm_ffn, w_router,
    w_gate, w_up, w_down, expert_ids, priority, prefix,
):
    group_count, span_len, width = hidden_in.shape
    row_count = group_count * span_len
    q_width, kv_width = w_query.shape[1], w_key.shape[1]
    kv_heads = kv_width // HD
    members, n_dp = lax.axis_size("expert"), lax.axis_size("dp")
    expert_count = w_router.shape[1]
    local_count = w_gate.shape[0]
    team_count = local_count // 2
    top_count = expert_ids.shape[3]
    slot_count = row_count * top_count * 5 // (expert_count * 4)
    capacity = 9 * row_count * members * top_count // (8 * expert_count)
    e_index, d_index = lax.axis_index("expert"), lax.axis_index("dp")
    parity = (d_index // TEAM_BIT) % 2
    first_local = parity * team_count
    first_expert = (e_index * local_count + first_local).reshape(1).astype(jnp.int32)
    e_steps = [("expert", bit) for bit in bits_of(members)]
    team = ("dp", TEAM_BIT)
    gain_one, gain_two = norm_attn.reshape(1, width), norm_ffn.reshape(1, width)
    router_t = w_router.T

    expert_range = jnp.arange(expert_count, dtype=jnp.int32)
    routes_t = expert_ids.reshape(row_count, top_count).T
    hit_t = jnp.any(routes_t[:, None, :] == expert_range[None, :, None], axis=0)
    tables = jnp.concatenate([routes_t, priority.reshape(1, row_count)], axis=0)[None]
    for axis_name, bit in [team] + e_steps:
        tables = jnp.concatenate([tables, swap(tables, axis_name, bit)], axis=0)

    offset = e_index * span_len
    positions = (offset + jnp.arange(span_len, dtype=jnp.int32)).astype(F32)
    frequency = ROPE_BASE ** (-(jnp.arange(HD // 2, dtype=F32) * 2.0 / HD))
    angles = positions[:, None] * frequency[None, :]
    cos_table, sin_table = jnp.cos(angles), jnp.sin(angles)
    cos_span = jnp.concatenate([cos_table, cos_table], axis=1)
    sin_span = jnp.concatenate([-sin_table, sin_table], axis=1)
    cos_wide, sin_wide = jnp.tile(cos_span, (group_count, 1)), jnp.tile(sin_span, (group_count, 1))
    x = hidden_in.reshape(row_count, width)
    cot = cotangent.reshape(row_count, width)
    normed, kv_own, queries, cot_later = project_inputs(
        x, gain_one, w_query, w_key, w_value, cos_wide, sin_wide, cot
    )
    kv = [kv_own.reshape(group_count, span_len, 2 * kv_width)]
    q = queries([tables])
    for number, (axis_name, bit) in enumerate(e_steps):
        arrived = [swap(piece, axis_name, bit) for piece in kv]
        kv = kv + arrived
    source = e_index ^ sum(
        ((jnp.arange(members) >> at) & 1) * bit for at, (_, bit) in enumerate(e_steps)
    )
    source = jnp.concatenate([source, offset.reshape(1)]).astype(jnp.int32)

    cut = row_count // 2

    far, near = ("expert", 2), ("expert", 1)

    def corner_of(over_z, over_y):
        return swap(over_z[:cut], *far), swap(over_y[cut:], *team)

    def over_near(piece):
        return tuple(swap(s, *near) for s in piece)

    def scatter_team(make):
        if members != 4:
            pieces = [make(at, [], 0)[0] for at in range(2 * members)]
            return [(scatter_pieces(pieces, [team] + e_steps), 0)]
        sent = {at: swap(make(at + 4, [], 0)[0], "expert", 1) for at in (3, 1, 2, 0)}
        low, high = make(3, [(sent[3], 0)], cut)
        from_y, from_z = swap(low, *far), swap(high, *team)
        own = make(0, [(sent[0], 0)], 0)[0]
        over_z = swap(make(1, [(sent[1], 0), (from_y, 0)], 0)[0], *team)
        over_y = swap(make(2, [(sent[2], 0), (from_z, cut)], 0)[0], *far)
        return [(own, 0), (over_z, 0), (over_y, 0)]

    split = members == 4
    if split:
        over_z = swap(hold(cot, [tables]), *team)
        cot_later = hold(cot_later, [tables, kv[1]])
        over_y = swap(cot_later, *far)
        near_own = over_near((cot,))
        cots = [(cot,), (over_z,), (over_y,)]
    else:
        cots = [(piece,) for piece in gather_pieces(cot, [team] + e_steps)]

    q = q.reshape(group_count, span_len, q_width)
    mix, lse = attend(q, kv, prefix, source)
    mix = mix.reshape(row_count, q_width)
    places = find_places(tables, first_expert, team_count, capacity, [mix])
    residual, message, gates_t = branch(
        x, mix, w_out, gain_two, router_t, hit_t.astype(F32), [over_z, over_y, places] if split else [places]
    )

    u_rows, gate_rows = {}, {}

    def send_rows(at, piece, after):
        u_rows[at], gate_rows[at] = dispatch(
            piece, at, places, first_expert, slot_count, True, after
        )

    if split:
        over_z, over_y = swap(message, *team), swap(message, *far)
        near_rows = over_near((message,))
    else:
        pieces = gather_pieces(message, [team] + e_steps)
    dz_rows = {}

    def own_rows(at, piece, after):
        dz_rows[at] = dispatch(piece, at, places, first_expert, slot_count, False, after)[0]
        return [dz_rows[at]]

    if split:
        over_cot_z, over_cot_y = (hold(cots[n][0], [places]) for n in (1, 2))
        corner = corner_of(over_cot_z, over_cot_y)
        near_z, near_y = over_near((over_cot_z,)), over_near((over_cot_y,))
        last = own_rows(0, cots[0], [places])
        last = own_rows(4, near_own, last)
        last = own_rows(1, (over_cot_z,), last)
        last = own_rows(2, (over_cot_y,), last)
        last = own_rows(5, near_z, last)
        last = own_rows(6, near_y, last)
        send_rows(0, (message,), last)
        send_rows(4, near_rows, [u_rows[0]])
        over_z, over_y = hold(over_z, [u_rows[4]]), hold(over_y, [u_rows[4]])
        corner_rows = corner_of(over_z, over_y)
        near_rows_z, near_rows_y = over_near((over_z,)), over_near((over_y,))
        send_rows(1, (over_z,), [])
        send_rows(2, (over_y,), [u_rows[1]])
        send_rows(5, near_rows_z, [u_rows[2]])
        send_rows(6, near_rows_y, [u_rows[5]])
        corner = tuple(hold(part, [u_rows[6]]) for part in corner)
        near_corner = over_near(corner)
        last = own_rows(3, corner, [u_rows[6]])
        corner_rows = tuple(hold(part, last) for part in corner_rows)
        near_corner_rows = over_near(corner_rows)
        last = own_rows(7, near_corner, last)
        send_rows(3, corner_rows, last)
        send_rows(7, near_corner_rows, [u_rows[3]])
    else:
        last = []
        for at, piece in enumerate(cots):
            last = own_rows(at, piece, last)
        for at, piece in enumerate(pieces):
            send_rows(at, (piece,), last)
    dz_rows = [dz_rows[at] for at in range(2 * members)]
    u_rows, gate_rows = ([rows[at] for at in range(2 * members)] for rows in (u_rows, gate_rows))
    d_order = [bit for bit in reversed(bits_of(n_dp)) if bit != TEAM_BIT] + [TEAM_BIT]
    kept_bits = sum(d_order[1:-1])
    me = (d_index - (d_index & kept_bits)).reshape(1).astype(jnp.int32)
    team_place = (d_index & TEAM_BIT).reshape(1).astype(jnp.int32)
    outs, backs, slopes, chains = [], [], [], []
    chunk = 8
    for e in range(team_count):
        expert = (first_local + e).reshape(1).astype(jnp.int32)
        joint = 0
        parts = []
        for start in range(0, len(u_rows), chunk):
            span = slice(start, start + chunk)
            parts.append(
                expert_pass(
                    e, expert, team_place if joint else me, u_rows[span], dz_rows[span], gate_rows[span],
                    w_gate, w_up, w_down, n_dp, d_order, joint, slopes[-1:],
                )
            )
        if len(parts) == 1:
            out, back, slope, *grads = parts[0]
        else:
            out, back, slope = (jnp.concatenate([p[i] for p in parts], axis=0) for i in range(3))
            grads = [
                sum(p[i].astype(F32) for p in parts).astype(BF16) for i in range(3, len(parts[0]))
            ]
        outs.append(out)
        backs.append(back)
        slopes.append(slope)
        chains.append(grads[0] if joint else (grads[0], swap(grads[1], "dp", d_order[0])))
    pairs = {
        bit: [[d, d + bit] for d in range(n_dp) if (d // bit) % 2 == 0] for bit in d_order[1:-1]
    }

    def advance(e, after):
        if e >= team_count:
            return list(after)
        if joint:
            ranks = [
                sum(bit for at, bit in enumerate(d_order[:-1]) if (n_dp // 4 >> at) & r)
                for r in range(n_dp // 2)
            ]
            groups = [[side * TEAM_BIT + r for r in ranks] for side in range(2)]
            chains[e] = lax.psum_scatter(
                hold(chains[e], after), "dp", scatter_dimension=0, tiled=True,
                axis_index_groups=groups,
            )
            return list(after)
        total = mark = add_blocks(*chains[e], after)
        for bit in d_order[1:-1]:
            total = lax.psum_scatter(
                total, "dp", scatter_dimension=0, tiled=True, axis_index_groups=pairs[bit]
            )
        chains[e] = total
        return [mark]

    extra = expert_count

    first_marks, marked = advance(0, slopes[-1:]), []

    def make_back(at, added, cut_at):
        parts = combine(
            backs, at, places, slopes, first_expert, added, cut_at, extra,
            first_marks if at >= members else (),
        )
        marked.append(parts[0])
        return parts

    back_terms = [term for term, _ in scatter_team(make_back)]
    marks = advance(1, marked[-3:])
    d_residual, d_branch, d_mix, small = back_through_branch(
        back_terms, residual, cot, gain_two, gates_t, router_t, message, w_out, marks
    )

    member_order = [bit for _, bit in reversed(e_steps)]
    member_places = [
        sum(((q >> (len(member_order) - 1 - at)) & 1) * bit for at, bit in enumerate(member_order))
        for q in range(members)
    ]
    grad_places = jnp.concatenate(
        [e_index ^ jnp.array(member_places, jnp.int32), d_index.reshape(1)]
    ).astype(jnp.int32)
    w_order = list(reversed(bits_of(n_dp)))
    w_steps = [("expert", bit) for bit in member_order] + [("dp", bit) for bit in w_order]
    q_part, kv_part = q_width // members, kv_width // members
    w_parts = []

    def add_weight(left, right, total_cols, start, after):
        buffers = w_parts[-1] if start else []
        w_parts.append(
            weight_grad(
                left, right, grad_places, n_dp, members, w_order,
                total_cols, start, buffers, after,
            )
        )

    marks = advance(2, [d_mix])

    def out_rows(at, added, cut_at, after):
        return combine(outs, at, places, None, first_expert, added, cut_at, 0, after)

    if split:
        nears = {at: out_rows(at + 4, [], 0, marks)[0] for at in (3, 1, 2, 0)}
        sent = {at: swap(rows, *near) for at, rows in nears.items()}
        marks = list(nears.values())
    dq, d_kv = attend_back(
        q, d_mix.reshape(group_count, span_len, q_width), lse, kv, prefix, source,
        cos_span, sin_span, marks,
    )
    dq = dq.reshape(row_count, q_width)
    settled = []

    def settle_expert(e, held, after):
        result = hold(chains[e], held)
        slots = jnp.stack([first_local + e, team_count - first_local + e]).astype(jnp.int32)
        totals = settled[-1] if settled else []
        other = swap(result[1], *team)
        settled.append(settle(result[0], other, slots, local_count, totals, after))

    marks, corners = [dq], []
    if split:
        low, high = out_rows(3, [(sent[3], 0)], cut, marks)
        from_y, from_z = corners = swap(low, *far), swap(high, *team)
        marks = [low]
    add_weight(mix, d_branch, 2 * q_part, 0, marks)
    add_weight(normed, dq, 2 * q_part, q_part, [])
    last_step = e_steps[0]
    halves = [scatter_pieces(d_kv[at::2], e_steps[1:]) for at in range(2)]
    held, far_half = (h.reshape(row_count, 2 * kv_width) for h in halves)
    arrived = hold(swap(far_half, *last_step), [w_parts[-1][0], *corners])
    d_kv_own, joined = key_value_back(held, arrived, cos_wide, sin_wide, members)
    marks = advance(3, [d_kv_own])
    if q_part % 128 == 0:
        w_keep, w_send = w_parts[1]
    else:
        w_keep, w_send = (jnp.concatenate([p[i] for p in w_parts], axis=3) for i in range(2))
    w_marks = []
    grads = reduce_grad(w_keep, w_send, w_steps, marks, w_marks)
    marks = w_marks[:1]
    if split:
        own = out_rows(0, [(sent[0], 0)], 0, marks)[0]
        over_z = out_rows(1, [(sent[1], 0), (from_y, 0)], 0, marks)[0]
        over_y = out_rows(2, [(sent[2], 0), (from_z, cut)], 0, marks)[0]
        out_terms = [(own, 0), (swap(over_z, *team), 0), (swap(over_y, *far), 0)]
        marks = [own, over_z, over_y]
    else:
        out_terms = scatter_team(lambda at, added, cut_at: out_rows(at, added, cut_at, marks))
    add_weight(normed, joined, 2 * kv_part, 0, [])
    d_hidden, sums = finish(
        dq, d_kv_own, w_query, w_key, w_value, x, d_residual, gain_one, small, [w_parts[-1][0]]
    )
    output = layer_output(residual, out_terms, [d_hidden, *w_marks[1:2]])
    sums = all_sum(hold(sums, [output]), ("expert",))
    sums = sums + swap(sums, "dp", w_order[0])
    early = max(1, team_count - 1)

    def late(mark):
        if not settled:
            for e in range(early):
                settle_expert(e, [d_hidden], [sums, mark])
        return settled[-1][:1]

    kv_keep, kv_send = w_parts[2]
    kv_grads = reduce_grad(kv_keep, hold(kv_send, [output]), w_steps, late=late)
    sums = hold(sums, late(output))
    for bit in w_order[1:]:
        sums = sums + swap(sums, "dp", bit)

    for e in range(early, team_count):
        settle_expert(e, [output], [])
    grad_gate, grad_up, grad_down = settled[-1]
    return (
        output.reshape(group_count, span_len, width),
        d_hidden.reshape(group_count, span_len, width),
        sums[expert_count + 1],
        grads[:, q_part:],
        kv_grads[:, :kv_part],
        kv_grads[:, kv_part:],
        grads[:, :q_part],
        sums[expert_count],
        sums[:expert_count].T,
        grad_gate,
        grad_up,
        grad_down,
    )


def solution(mesh):
    in_specs = (
        P("dp", "expert", None),
        P("dp", "expert", None),
        P(),
        P(),
        P(),
        P(),
        P(),
        P(),
        P(),
        P("expert", None, None),
        P("expert", None, None),
        P("expert", None, None),
        P(("dp", "expert"), None, None, None),
        P(("dp", "expert"), None, None),
        P("dp"),
    )
    out_specs = (
        P("dp", "expert", None),
        P("dp", "expert", None),
        P(),
        P("dp", "expert"),
        P("dp", "expert"),
        P("dp", "expert"),
        P("dp", "expert"),
        P(),
        P(),
        P("expert", "dp", None),
        P("expert", "dp", None),
        P("expert", "dp", None),
    )
    return jax.shard_map(
        per_device, mesh=mesh, in_specs=in_specs, out_specs=out_specs, check_vma=False
    )
```

```python
import functools

import jax
import jax.numpy as jnp
from jax import lax
from jax.experimental import pallas as pl
from jax.experimental.pallas import tpu as pltpu
from jax.sharding import PartitionSpec as P

HD = 128
EPSILON = 1e-06
ROPE_BASE = 10000.0
MASKED = -1e30
EXTRA = 16
TEAM_BIT = 2
VMEM_LIMIT = 60 * 1024 * 1024

BF16 = jnp.bfloat16
F32 = jnp.float32


def dot(a, b):
    return jnp.dot(a, b, preferred_element_type=F32)


def dot_nt(a, b):
    return lax.dot_general(a, b, (((1,), (1,)), ((), ())), preferred_element_type=F32)


def dot_tn(a, b):
    return lax.dot_general(a, b, (((0,), (0,)), ((), ())), preferred_element_type=F32)


def bits_of(size):
    return [1 << i for i in reversed(range(size.bit_length() - 1))]


def swap(values, axis_name, bit):
    count = lax.axis_size(axis_name)
    return lax.ppermute(values, axis_name, [(i, i ^ bit) for i in range(count)])


def gather_pieces(values, steps):
    pieces = [values]
    for axis_name, bit in steps:
        pieces = pieces + [swap(piece, axis_name, bit) for piece in pieces]
    return pieces


def add_pair(a, b):
    return (a.astype(F32) + b.astype(F32)).astype(BF16)


def scatter_pieces(pieces, steps):
    for axis_name, bit in reversed(steps):
        half = len(pieces) // 2
        pieces = [
            add_pair(a, swap(b, axis_name, bit))
            for a, b in zip(pieces[:half], pieces[half:], strict=True)
        ]
    return pieces[0]


def all_sum(values, axes):
    for axis_name in axes:
        for bit in reversed(bits_of(lax.axis_size(axis_name))):
            values = values + swap(values, axis_name, bit)
    return values


ANYWHERE = pl.BlockSpec(memory_space=pl.ANY)


TIME_SCALE = 0.01


def kernel_call(us, body, grid, ins, outs, scalars=(), scratch=(), after=(), aliases=None):
    after = list(after)
    lead, held = len(scalars), len(ins)

    def run(*refs):
        body(*refs[: lead + held], *refs[lead + held + len(after) :])

    grid_spec = pltpu.PrefetchScalarGridSpec(
        num_scalar_prefetch=lead,
        grid=grid,
        in_specs=[spec for _, spec in ins] + [ANYWHERE] * len(after),
        out_specs=[spec for _, spec in outs],
        scratch_shapes=list(scratch),
    )
    return pl.pallas_call(
        run,
        grid_spec=grid_spec,
        out_shape=[shape for shape, _ in outs],
        input_output_aliases=aliases or {},
        compiler_params=pltpu.CompilerParams(vmem_limit_bytes=VMEM_LIMIT),
        cost_estimate=pl.CostEstimate(
            flops=int(us * TIME_SCALE * 1e9),
            bytes_accessed=int(us * TIME_SCALE * 3.3e6),
            transcendentals=0,
        ),
    )(*scalars, *[a for a, _ in ins], *after)


def shaped(shape, dtype):
    return jax.ShapeDtypeStruct(tuple(shape), dtype)


def whole(array):
    zeros = (0,) * len(array.shape)
    return pl.BlockSpec(tuple(array.shape), lambda *_: zeros)


def rms_of(values):
    return lax.rsqrt(jnp.mean(values * values, axis=-1, keepdims=True) + EPSILON)


def turn(values, cos_wide, sin_wide):
    return values * cos_wide + pltpu.roll(values, HD // 2, 1) * sin_wide


def column(width, tile):
    return pl.ds(pl.multiple_of(width * tile, tile), tile)


def hold_body(value_ref, out_ref):
    pass


def hold(value, after):
    return kernel_call(
        0.5, hold_body, (1,), [(value, ANYWHERE)], [(shaped(value.shape, value.dtype), ANYWHERE)],
        after=after, aliases={0: 0},
    )[0]


def key_value_body(x_ref, gain, wk, wv, cos_ref, sin_ref, cot_ref, normed_ref, kv_ref, same_ref):
    x = x_ref[...].astype(F32)
    normed = (x * rms_of(x) * gain[...]).astype(BF16)
    normed_ref[...] = normed
    keys = dot(normed, wk[...])
    for h in range(keys.shape[1] // HD):
        cols = slice(h * HD, (h + 1) * HD)
        kv_ref[:, cols] = turn(keys[:, cols], cos_ref[...], sin_ref[...]).astype(BF16)
    kv_ref[:, keys.shape[1] :] = dot(normed, wv[...]).astype(BF16)


def query_body(normed_ref, wq, cos_ref, sin_ref, q_ref):
    queries = dot(normed_ref[...], wq[...])
    for h in range(queries.shape[1] // HD):
        cols = slice(h * HD, (h + 1) * HD)
        q_ref[:, cols] = turn(queries[:, cols], cos_ref[...], sin_ref[...]).astype(BF16)


def project_inputs(x, gain, wq, wk, wv, cos_wide, sin_wide, cot):
    rows, width = x.shape
    kd = wk.shape[1]
    normed, kv, cot = kernel_call(
        4.2,
        key_value_body,
        (1,),
        [(a, whole(a)) for a in (x, gain, wk, wv, cos_wide, sin_wide)] + [(cot, ANYWHERE)],
        [(s, whole(s)) for s in (shaped((rows, width), BF16), shaped((rows, 2 * kd), BF16))]
        + [(shaped(cot.shape, BF16), ANYWHERE)],
        aliases={6: 2},
    )
    tile = 256

    def queries(after):
        return kernel_call(
            8,
            query_body,
            (wq.shape[1] // tile,),
            [
                (normed, whole(normed)),
                (wq, pl.BlockSpec((width, tile), lambda i: (0, i))),
                (cos_wide, whole(cos_wide)),
                (sin_wide, whole(sin_wide)),
            ],
            [(shaped((rows, wq.shape[1]), BF16), pl.BlockSpec((rows, tile), lambda i: (0, i)))],
            after=after,
        )[0]

    return normed, kv, queries, cot


def attention_bias(prefix, source, offset, span, members):
    rows = offset + lax.broadcasted_iota(jnp.int32, (span, span), 0)
    cols = lax.broadcasted_iota(jnp.int32, (span, span), 1)
    parts = []
    for p in range(members):
        keys = source[p] * span + cols
        parts.append(jnp.where((keys <= rows) | (keys < prefix), 0.0, MASKED))
    return jnp.concatenate(parts, axis=1)


def attention_body(members, kvh, ratio, prefix, source, q_ref, *refs):
    pieces, (mix_ref, lse_ref, bias) = refs[:members], refs[members:]
    span = q_ref.shape[1]
    scale = HD ** (-0.5)
    bias[...] = attention_bias(prefix[pl.program_id(0)], source, source[members], span, members)
    columns = []
    for k in range(kvh):
        keys = jnp.concatenate([p[0, :, k * HD : (k + 1) * HD] for p in pieces], axis=0)
        start = (kvh + k) * HD
        values = jnp.concatenate([p[0, :, start : start + HD] for p in pieces], axis=0)
        for r in range(ratio):
            cols = slice((k * ratio + r) * HD, (k * ratio + r + 1) * HD)
            scores = dot_nt(q_ref[0, :, cols], keys) + bias[...]
            top = jnp.max(scores, axis=1, keepdims=True)
            terms = jnp.exp((scores - top) * scale)
            total = jnp.sum(terms, axis=1, keepdims=True)
            mixed = dot(terms.astype(BF16), values)
            mix_ref[0, :, cols] = (mixed / total).astype(BF16)
            columns.append(top * scale + jnp.log(total))
    lse_ref[0] = jnp.concatenate(columns, axis=1)


def attention_back_body(
    members, kvh, ratio, prefix, source, q_ref, do_ref, lse_ref, cos_ref, sin_ref, *refs
):
    pieces, dq_ref = refs[:members], refs[members]
    outs, (bias, dk, dv) = refs[members + 1 : 2 * members + 1], refs[2 * members + 1 :]
    span = q_ref.shape[1]
    scale = HD ** (-0.5)
    bias[...] = attention_bias(prefix[pl.program_id(0)], source, source[members], span, members)
    for k in range(kvh):
        keys = jnp.concatenate([p[0, :, k * HD : (k + 1) * HD] for p in pieces], axis=0)
        start = (kvh + k) * HD
        values = jnp.concatenate([p[0, :, start : start + HD] for p in pieces], axis=0)
        for r in range(ratio):
            h = k * ratio + r
            cols = slice(h * HD, (h + 1) * HD)
            query, upstream = q_ref[0, :, cols], do_ref[0, :, cols]
            scores = dot_nt(query, keys) + bias[...]
            probs = jnp.exp(scores * scale - lse_ref[0, :, h : h + 1])
            d_probs = dot_nt(upstream, values)
            mean = jnp.sum(probs * d_probs, axis=1, keepdims=True)
            d_scores = (probs * (d_probs - mean)).astype(BF16)
            d_query = dot(d_scores, keys) * scale
            dq_ref[0, :, cols] = turn(d_query, cos_ref[...], -sin_ref[...]).astype(BF16)
            part_k = dot_tn(d_scores, query)
            part_v = dot_tn(probs.astype(BF16), upstream)
            if r == 0:
                dk[...] = part_k
                dv[...] = part_v
            else:
                dk[...] += part_k
                dv[...] += part_v
        for p, out in enumerate(outs):
            rows = slice(p * span, (p + 1) * span)
            out[0, :, k * HD : (k + 1) * HD] = (dk[rows, :] * scale).astype(BF16)
            out[0, :, start : start + HD] = dv[rows, :].astype(BF16)


def attend(q, kv, prefix, source):
    groups, span, qd = q.shape
    members, kvh = len(kv), kv[0].shape[2] // (2 * HD)
    heads = qd // HD
    block = lambda n: pl.BlockSpec((1, span, n), lambda g, *_: (g, 0, 0))
    return kernel_call(
        15.7,
        functools.partial(attention_body, members, kvh, heads // kvh),
        (groups,),
        [(q, block(qd))] + [(p, block(p.shape[2])) for p in kv],
        [
            (shaped(q.shape, BF16), block(qd)),
            (shaped((groups, span, heads), F32), block(heads)),
        ],
        scalars=(prefix, source),
        scratch=[pltpu.VMEM((span, span * members), F32)],
    )


def attend_back(q, do, lse, kv, prefix, source, cos_wide, sin_wide, after=()):
    groups, span, qd = q.shape
    members, kvh = len(kv), kv[0].shape[2] // (2 * HD)
    heads = qd // HD
    block = lambda n: pl.BlockSpec((1, span, n), lambda g, *_: (g, 0, 0))
    outs = kernel_call(
        28.6,
        functools.partial(attention_back_body, members, kvh, heads // kvh),
        (groups,),
        [(q, block(qd)), (do, block(qd)), (lse, block(heads))]
        + [(cos_wide, whole(cos_wide)), (sin_wide, whole(sin_wide))]
        + [(p, block(p.shape[2])) for p in kv],
        [(shaped(q.shape, BF16), block(qd))]
        + [(shaped(p.shape, BF16), block(p.shape[2])) for p in kv],
        scalars=(prefix, source),
        scratch=[
            pltpu.VMEM((span, span * members), F32),
            pltpu.VMEM((span * members, HD), F32),
            pltpu.VMEM((span * members, HD), F32),
        ],
        after=after,
    )
    return outs[0], outs[1:]


def branch_body(steps, x_ref, mix_ref, wo, gain, router, hit_ref,
                residual_ref, message_ref, gates_ref):
    i = pl.program_id(0)
    tile = wo.shape[1]
    cols = column(i, tile)
    residual_ref[:, cols] = x_ref[:, cols].astype(F32) + dot(mix_ref[...], wo[...])

    @pl.when(i == steps - 1)
    def _():
        rows = residual_ref.shape[0]
        experts = hit_ref.shape[0]
        h1 = residual_ref[...]
        a2 = (h1 * rms_of(h1) * gain[...]).astype(BF16)
        message_ref[:rows, :] = a2
        hit = hit_ref[...] > 0.0
        logits = jnp.where(hit, dot_nt(router[...], a2), MASKED)
        terms = jnp.exp(logits - jnp.max(logits, axis=0, keepdims=True))
        terms = jnp.where(hit, terms, 0.0)
        gates = terms / jnp.sum(terms, axis=0, keepdims=True)
        gates_ref[...] = gates
        high = gates.astype(BF16)
        rest = gates - high.astype(F32)
        middle = rest.astype(BF16)
        low = (rest - middle.astype(F32)).astype(BF16)
        message_ref[rows:, :rows] = high
        message_ref[rows:, rows : 2 * rows] = middle
        message_ref[rows:, 2 * rows : 3 * rows] = low
        if message_ref.shape[1] > 3 * rows:
            message_ref[rows:, 3 * rows :] = jnp.zeros(
                (experts, message_ref.shape[1] - 3 * rows), BF16
            )


def branch(x, mix, wo, gain, router_t, hit_t, after=()):
    rows, width = x.shape
    experts = router_t.shape[0]
    tile = 256
    outs = (
        shaped((rows, width), F32),
        shaped((rows + experts, width), BF16),
        shaped((experts, rows), F32),
    )
    return kernel_call(
        10,
        functools.partial(branch_body, width // tile),
        (width // tile,),
        [(x, whole(x)), (mix, whole(mix))]
        + [(wo, pl.BlockSpec((wo.shape[0], tile), lambda i: (0, i)))]
        + [(a, whole(a)) for a in (gain, router_t, hit_t)],
        [(s, whole(s)) for s in outs],
        after=after,
    )


def slot_masks(places, slot_count):
    experts, tokens = places.shape
    slots = lax.broadcasted_iota(jnp.int32, (slot_count, tokens), 0).astype(F32)
    return [places[e : e + 1, :] == slots for e in range(experts)]


def hot_rows(masks):
    return jnp.concatenate([m.astype(F32) for m in masks], axis=0).astype(BF16)


def pick_experts(table, first, count):
    row = lax.broadcasted_iota(jnp.int32, table.shape, 0)
    picked = [
        jnp.sum(jnp.where(row == first + e, table, 0.0), axis=0, keepdims=True)
        for e in range(count)
    ]
    return jnp.concatenate(picked, axis=0)


def places_body(blocks, count, capacity, first, table_ref, column_ref, out_ref):
    b = pl.program_id(0)
    tokens = table_ref.shape[2]
    top = table_ref.shape[1] - 1
    padded = 8

    def hits(at):
        row = lax.broadcasted_iota(jnp.int32, (padded, tokens), 0)
        expert = jnp.where(row < count, first[0] + row, -1)
        found = table_ref[at, 0:1, :] == expert
        for k in range(1, top):
            found = found | (table_ref[at, k : k + 1, :] == expert)
        return found

    own_order = table_ref[b, top : top + 1, :]
    before = jnp.zeros((padded, tokens), F32)
    for n in range(blocks // 2):
        at = 2 * n + b % 2
        earlier = jnp.where(column_ref[at] < own_order, 1.0, 0.0).astype(BF16)
        before = before + dot(jnp.where(hits(at), 1.0, 0.0).astype(BF16), earlier)
    kept = hits(b) & (before < capacity)
    row = lax.broadcasted_iota(jnp.int32, (tokens, tokens), 0)
    col = lax.broadcasted_iota(jnp.int32, (tokens, tokens), 1)
    ahead = jnp.where(row < col, 1.0, 0.0).astype(BF16)
    slots = dot(jnp.where(kept, 1.0, 0.0).astype(BF16), ahead)
    out_ref[0] = jnp.where(kept, slots, -1.0)[:count]


def find_places(tables, first, count, capacity, after=()):
    blocks, wide, tokens = tables.shape
    columns = tables[:, wide - 1, :, None]
    shape = shaped((blocks, count, tokens), F32)
    return kernel_call(
        4,
        functools.partial(places_body, blocks, count, capacity),
        (blocks,),
        [(tables, whole(tables)), (columns, whole(columns))],
        [(shape, pl.BlockSpec((1, count, tokens), lambda b, *_: (b, 0, 0)))],
        scalars=(first,),
        after=after,
    )[0]


def dispatch_body(parts, with_gates, slot_count, first, *refs):
    segments, refs = refs[:parts], refs[parts:]
    if with_gates:
        extra_ref, places_ref, rows_ref, gate_ref = refs
    else:
        places_ref, rows_ref = refs
    _, count, tokens = places_ref.shape
    masks = slot_masks(places_ref[0], slot_count)
    hot = hot_rows(masks)
    if with_gates:
        extra = extra_ref[...].astype(F32)
        table = extra[:, :tokens] + extra[:, tokens : 2 * tokens]
        gates = pick_experts(table + extra[:, 2 * tokens : 3 * tokens], first[0], count)
        for e in range(count):
            gate = jnp.sum(jnp.where(masks[e], gates[e : e + 1, :], 0.0), axis=1, keepdims=True)
            gate_ref[e] = jnp.broadcast_to(gate, (slot_count, 128))
    total, start = 0.0, 0
    for segment in segments:
        stop = min(start + segment.shape[0], tokens)
        total = total + dot(hot[:, start:stop], segment[: stop - start, :])
        start = stop
    total = total.astype(BF16)
    for e in range(count):
        rows_ref[e] = total[e * slot_count : (e + 1) * slot_count]


def dispatch(segments, at, places, first, slot_count, with_gates, after=()):
    width = segments[0].shape[1]
    _, count, tokens = places.shape
    ins = [(a, whole(a)) for a in segments]
    outs = [shaped((count, slot_count, width), BF16)]
    if with_gates:
        last = segments[-1]
        extra = last.shape[0] - (tokens - sum(a.shape[0] for a in segments[:-1]))
        spot = last.shape[0] // extra - 1
        ins.append((last, pl.BlockSpec((extra, width), lambda *_: (spot, 0))))
        outs.append(shaped((count, slot_count, 128), F32))
    ins.append((places, pl.BlockSpec((1, count, tokens), lambda *_: (at, 0, 0))))
    return kernel_call(
        1.5,
        functools.partial(dispatch_body, len(segments), with_gates, slot_count),
        (1,),
        ins,
        [(o, whole(o)) for o in outs],
        scalars=(first,),
        after=after,
    )


def combine_body(experts, with_extra, starts, cut, first, *refs):
    refs = list(refs)
    rows = [refs.pop(0) for _ in range(experts)]
    places_ref = refs.pop(0)
    slopes = [refs.pop(0) for _ in range(experts)] if with_extra else None
    added = [refs.pop(0) for _ in starts]
    outs = refs
    slot_count = rows[0].shape[1]
    tokens = places_ref.shape[2]
    masks = slot_masks(places_ref[0], slot_count)
    values = jnp.concatenate([r[0] for r in rows], axis=0)
    total = dot_tn(hot_rows(masks), values)
    last = outs[-1]
    width = last.shape[1]
    for other, start in zip(added, starts, strict=True):
        count = min(other.shape[0], tokens - start)
        parts = [total[start : start + count] + other[:count, :].astype(F32)]
        if start > 0:
            parts = [total[:start]] + parts
        if start + count < tokens:
            parts.append(total[start + count :])
        total = parts[0] if len(parts) == 1 else jnp.concatenate(parts, axis=0)
    total = total.astype(BF16)
    if cut:
        outs[0][...] = total[:cut]
    last[: tokens - cut, :] = total[cut:]
    if with_extra:
        count = last.shape[0] - (tokens - cut)
        row = lax.broadcasted_iota(jnp.int32, (count, tokens), 0)
        table = jnp.zeros((count, tokens), F32)
        for e in range(experts):
            slope = jnp.sum(jnp.where(masks[e], slopes[e][0, :, :1], 0.0), axis=0, keepdims=True)
            table = jnp.where(row == first[0] + e, slope, table)
        high = table.astype(BF16).astype(F32)
        for side, value in enumerate((high, table - high)):
            cols = slice(side * tokens, (side + 1) * tokens)
            for other, start in zip(added, starts, strict=True):
                if start + other.shape[0] > tokens:
                    value = value + other[tokens - start :, cols].astype(F32)
            last[tokens - cut :, cols] = value.astype(BF16)
        last[tokens - cut :, 2 * tokens :] = jnp.zeros((count, width - 2 * tokens), BF16)


def combine(rows, at, places, slopes, first, added, cut, extra, after=()):
    experts = len(rows)
    _, slot_count, width = rows[0].shape
    _, count, tokens = places.shape
    block = lambda n: pl.BlockSpec((1, slot_count, n), lambda *_: (at, 0, 0))
    ins = [(r, block(width)) for r in rows]
    ins.append((places, pl.BlockSpec((1, count, tokens), lambda *_: (at, 0, 0))))
    if slopes is not None:
        ins += [(s, block(128)) for s in slopes]
    ins += [(a, whole(a)) for a, _ in added]
    long = tokens + (extra if slopes is not None else 0)
    outs = [shaped((cut, width), BF16)] if cut else []
    outs.append(shaped((long - cut, width), BF16))
    starts = tuple(start for _, start in added)
    return kernel_call(
        1.2,
        functools.partial(combine_body, experts, slopes is not None, starts, cut),
        (1,),
        ins,
        [(s, whole(s)) for s in outs],
        scalars=(first,),
        after=after,
    )


def expert_body(index, blocks, joint, n_dp, order, expert_ref, me_ref, *refs):
    refs = list(refs)
    u_hbm = [refs.pop(0) for _ in range(blocks)]
    dz_hbm = [refs.pop(0) for _ in range(blocks)]
    gate_hbm = [refs.pop(0) for _ in range(blocks)]
    wg_hbm, wu_hbm, wd_hbm, yg_hbm, du_hbm, slope_ref = refs[:6]
    grads_hbm, refs = refs[6 : 8 - joint], refs[8 - joint :]
    (
        u_ref, dz_ref, gate_ref, wg, wu, wd, ha, side_gate, side_up, dy, dga, dua, yg, du, stage,
        row_sems, sems,
    ) = refs
    _, slot_count, width = u_ref.shape
    rows = blocks * slot_count
    ff = ha.shape[1]
    expert, me = expert_ref[0], me_ref[0]

    def loads(sources, target, at):
        return [
            pltpu.make_async_copy(s.at[index], target.at[b], row_sems.at[at, b])
            for b, s in enumerate(sources)
        ]

    u_loads, dz_loads, gate_loads = (
        loads(u_hbm, u_ref, 0), loads(dz_hbm, dz_ref, 1), loads(gate_hbm, gate_ref, 2)
    )
    w_loads = [
        pltpu.make_async_copy(source.at[expert], target, sems.at[at])
        for at, (source, target) in enumerate(((wg_hbm, wg), (wu_hbm, wu), (wd_hbm, wd)))
    ]
    first, second = u_loads + w_loads[:2], w_loads[2:] + gate_loads + dz_loads
    for load in first + second:
        load.start()
    for load in first:
        load.wait()
    ff_tile, tile = 384, 512

    @pl.loop(0, ff // ff_tile)
    def _(t):
        cols = column(t, ff_tile)
        u = u_ref[...].reshape(rows, width)
        a = dot(u, wg[:, cols])
        b = dot(u, wu[:, cols])
        cdf = 0.5 * (1.0 + lax.erf(a * 0.7071067811865476))
        pdf = jnp.exp(-0.5 * a * a) * 0.3989422804014327
        glu = a * cdf
        ha[:, cols] = (glu * b).astype(BF16)
        side_gate[:, cols] = b * (cdf + a * pdf)
        side_up[:, cols] = glu

    for load in second:
        load.wait()
    slope_ref[...] = jnp.zeros_like(slope_ref)

    @pl.loop(0, width // tile)
    def _(t):
        cols = column(t, tile)
        gate = gate_ref[...].reshape(rows, 128)[:, :1]
        y = dot(ha[...], wd[:, cols]).astype(BF16).astype(F32)
        dz = dz_ref[:, :, cols].reshape(rows, tile).astype(F32)
        part = jnp.sum(dz * y, axis=1, keepdims=True)
        slope_ref[...] += jnp.broadcast_to(part, (rows, 128)).reshape(blocks, slot_count, 128)
        yg[:, :, cols] = (gate * y).astype(BF16).reshape(blocks, slot_count, tile)
        dy[:, cols] = (gate * dz).astype(BF16)

    out_yg = pltpu.make_async_copy(yg, yg_hbm, sems.at[3])
    out_yg.start()

    @pl.loop(0, ff // ff_tile)
    def _(t):
        cols = column(t, ff_tile)
        dha = dot_nt(dy[...], wd[cols, :])
        dga[:, cols] = (dha * side_gate[:, cols]).astype(BF16)
        dua[:, cols] = (dha * side_up[:, cols]).astype(BF16)

    wide = 384
    deep = width // n_dp
    flat = ff // n_dp

    def spot(block):
        return place_of(block ^ me, order, n_dp)

    @pl.loop(0, width // wide)
    def _(t):
        cols = column(t, wide)
        ut = u_ref[:, :, cols].reshape(rows, wide)
        for which, grad in ((0, dga), (1, dua)):
            d_weight = dot_tn(ut, grad[...]).astype(BF16)
            for i in range(wide // deep):
                at = spot(t * (wide // deep) + i)
                stage[at, which] = d_weight[i * deep : (i + 1) * deep]

    @pl.loop(0, ff // wide)
    def _(t):
        cols = column(t, wide)
        d_weight = dot_tn(ha[:, cols], dy[...]).astype(BF16)
        for i in range(wide // flat):
            at = spot(t * (wide // flat) + i)
            part = d_weight[i * flat : (i + 1) * flat]
            stage[at, 2, :flat] = part[:, :ff]
            stage[at, 2, flat:] = part[:, ff:]

    part = n_dp // len(grads_hbm)
    out_grads = [
        pltpu.make_async_copy(stage.at[pl.ds(side * part, part)], target, sems.at[5 + side])
        for side, target in enumerate(grads_hbm)
    ]
    for copy in out_grads:
        copy.start()

    @pl.loop(0, width // tile)
    def _(t):
        cols = column(t, tile)
        back = dot_nt(dga[...], wg[cols, :]) + dot_nt(dua[...], wu[cols, :])
        du[:, :, cols] = back.astype(BF16).reshape(blocks, slot_count, tile)

    out_du = pltpu.make_async_copy(du, du_hbm, sems.at[4])
    out_du.start()
    out_yg.wait()
    for copy in out_grads:
        copy.wait()
    out_du.wait()


def place_of(index, order, count):
    place = 0
    for at, bit in enumerate(order):
        place = place + ((index // bit) % 2) * (count >> (at + 1))
    return place


def expert_pass(index, expert, me, u, dz, gates, wg, wu, wd, n_dp, order, joint, after=()):
    blocks = len(u)
    _, slot_count, width = u[0].shape
    ff = wg.shape[2]
    rows = blocks * slot_count
    deep = width // n_dp
    packed = [shaped((n_dp // (2 - joint), 3, deep, ff), BF16)] * (2 - joint)
    row_shape = shaped((blocks, slot_count, width), BF16)
    slope_shape = shaped((blocks, slot_count, 128), F32)
    return kernel_call(
        26.5,
        functools.partial(expert_body, index, blocks, joint, n_dp, order),
        (1,),
        [(a, ANYWHERE) for a in list(u) + list(dz) + list(gates) + [wg, wu, wd]],
        [
            (row_shape, ANYWHERE),
            (row_shape, ANYWHERE),
            (slope_shape, whole(slope_shape)),
        ]
        + [(p, ANYWHERE) for p in packed],
        scalars=(expert, me),
        scratch=[
            pltpu.VMEM((blocks, slot_count, width), BF16),
            pltpu.VMEM((blocks, slot_count, width), BF16),
            pltpu.VMEM((blocks, slot_count, 128), F32),
            pltpu.VMEM((width, ff), BF16),
            pltpu.VMEM((width, ff), BF16),
            pltpu.VMEM((ff, width), BF16),
            pltpu.VMEM((rows, ff), BF16),
            pltpu.VMEM((rows, ff), F32),
            pltpu.VMEM((rows, ff), F32),
            pltpu.VMEM((rows, width), BF16),
            pltpu.VMEM((rows, ff), BF16),
            pltpu.VMEM((rows, ff), BF16),
            pltpu.VMEM((blocks, slot_count, width), BF16),
            pltpu.VMEM((blocks, slot_count, width), BF16),
            pltpu.VMEM((n_dp, 3, width // n_dp, ff), BF16),
            pltpu.SemaphoreType.DMA((3, blocks)),
            pltpu.SemaphoreType.DMA((8,)),
        ],
        after=after,
    )


def add_split_body(a_ref, b_ref, c_ref, d_ref, keep_ref, send_ref):
    keep_ref[...] = (a_ref[...].astype(F32) + b_ref[...].astype(F32)).astype(keep_ref.dtype)
    send_ref[...] = (c_ref[...].astype(F32) + d_ref[...].astype(F32)).astype(BF16)


def add_split(held, arrived, axis, last=False, after=()):
    half = held.shape[axis] // 2
    shape = list(held.shape)
    shape[axis] = half
    block = [1 if at == axis else size for at, size in enumerate(held.shape)]
    spot = lambda shift: lambda i: tuple(i + shift if at == axis else 0 for at in range(len(block)))
    low, high = pl.BlockSpec(tuple(block), spot(0)), pl.BlockSpec(tuple(block), spot(half))
    return kernel_call(
        4.5,
        add_split_body,
        (half,),
        [(held, low), (arrived, low), (held, high), (arrived, high)],
        [(shaped(shape, F32 if last else BF16), low), (shaped(shape, BF16), low)],
        after=after,
    )


def add_body(a_ref, b_ref, out_ref):
    out_ref[...] = (a_ref[...].astype(F32) + b_ref[...].astype(F32)).astype(BF16)


def add_blocks(held, arrived, after):
    block = pl.BlockSpec((1, *held.shape[1:]), lambda i: (i, 0, 0, 0))
    return kernel_call(
        4.5, add_body, held.shape[:1], [(held, block), (arrived, block)],
        [(shaped(held.shape, BF16), block)], after=after,
    )[0]


def settle_body(slots, own_ref, other_ref, *refs):
    outs = refs[-3:]

    def write(part):
        for m, out in enumerate(outs):
            value = part[m].astype(F32)
            if m == 2:
                flat = out.shape[1]
                value = jnp.concatenate([value[:flat], value[flat:]], axis=1)
            out[0] = value

    @pl.when(pl.program_id(0) == 0)
    def _():
        write(own_ref)

    @pl.when(pl.program_id(0) == 1)
    def _():
        write(other_ref)


def settle(own, other, slots, local_count, totals, after=()):
    _, deep, ff = own.shape
    shapes = [
        shaped((local_count, deep, ff), F32),
        shaped((local_count, deep, ff), F32),
        shaped((local_count, deep // 2, 2 * ff), F32),
    ]
    out_spec = lambda s: pl.BlockSpec((1, *s.shape[1:]), lambda i, slots: (slots[i], 0, 0))
    ins = [(own, whole(own)), (other, whole(other))] + [(t, ANYWHERE) for t in totals]
    return kernel_call(
        4.3,
        settle_body,
        (2,),
        ins,
        [(s, out_spec(s)) for s in shapes],
        scalars=(slots,),
        aliases={3 + i: i for i in range(len(totals))},
        after=after,
    )


def weight_grad_body(half, wide, order, n_dp, places, left_ref, right_ref, *refs):
    keep_ref, send_ref = refs[-2:]
    q = pl.program_id(0)
    width = left_ref.shape[1]
    deep = width // n_dp

    def fill(out_ref):
        right = right_ref[...].reshape(left_ref.shape[0], right_ref.shape[-1])
        for t in range(width // wide):
            part = dot_tn(left_ref[:, t * wide : (t + 1) * wide], right).astype(BF16)
            for i in range(wide // deep):
                at = place_of((t * (wide // deep) + i) ^ places[2 * half], order, n_dp)
                out_ref[0, at] = part[i * deep : (i + 1) * deep]

    @pl.when(q < half)
    def _():
        fill(keep_ref)

    @pl.when(q >= half)
    def _():
        fill(send_ref)


def weight_grad(left, right, places, n_dp, members, order, total_cols, start, buffers, after=()):
    rows, width = left.shape
    cols = right.shape[1] // members
    half = members // 2
    deep = width // n_dp
    if cols % 128 == 0:
        right_in = (right, pl.BlockSpec((rows, cols), lambda q, places: (0, places[q])))
    else:
        right = jnp.swapaxes(right.reshape(rows, members, cols), 0, 1)
        right_in = (right, pl.BlockSpec((1, rows, cols), lambda q, places: (places[q], 0, 0)))
        total_cols, start, buffers = cols, 0, []
    block = (1, n_dp, deep, cols)
    shape = shaped((half, n_dp, deep, total_cols), BF16)
    at = start // cols
    ins = [(left, whole(left)), right_in] + [(b, ANYWHERE) for b in buffers]
    return kernel_call(
        7,
        functools.partial(weight_grad_body, half, 384, order, n_dp),
        (members,),
        ins,
        [
            (shape, pl.BlockSpec(block, lambda q, places: (jnp.minimum(q, half - 1), 0, 0, at))),
            (shape, pl.BlockSpec(block, lambda q, places: (jnp.maximum(q - half, 0), 0, 0, at))),
        ],
        scalars=(places,),
        aliases={3 + i: i for i in range(len(buffers))},
        after=after,
    )


def reduce_grad(keep, send, steps, after=(), marks=None, late=None):
    outer = keep.shape[0].bit_length()
    arrived = swap(send, *steps[0])
    for at in range(1, len(steps)):
        if at == outer:
            keep, arrived = keep[0], arrived[0]
        keep, send = add_split(keep, arrived, 0, False, after if at == 1 else ())
        if marks is not None:
            marks.append(keep)
        if late is not None and steps[at] == ("dp", TEAM_BIT):
            send = hold(send, late(keep))
        arrived = swap(send, *steps[at])
    return keep[0].astype(F32) + arrived[0].astype(F32)


def norm_back(inputs, gain, upstream):
    scale = rms_of(inputs)
    weighted = gain * upstream
    middle = jnp.mean(inputs * weighted, axis=1, keepdims=True)
    grad = scale * weighted - inputs * (scale * scale * scale) * middle
    return grad, jnp.sum(upstream * inputs * scale, axis=0, keepdims=True)


def back_body(terms, *refs):
    refs = list(refs)
    parts = [refs.pop(0) for _ in range(terms)]
    (
        residual_ref, cot_ref, gain, gates_ref, router, message_ref, wo,
        d_res_ref, d_branch_ref, d_mix_ref, small_ref, total,
    ) = refs
    rows = residual_ref.shape[0]
    experts = gates_ref.shape[0]

    @pl.when(pl.program_id(0) == 0)
    def _():
        value = parts[0][...].astype(F32)
        for part in parts[1:]:
            value = value + part[...].astype(F32)
        total[...] = value
        slopes = total[rows:, :rows] + total[rows:, rows : 2 * rows]
        gates = gates_ref[...]
        mean = jnp.sum(gates * slopes, axis=0, keepdims=True)
        d_logits = (gates * (slopes - mean)).astype(BF16)
        d_routed = total[:rows, :] + dot_tn(d_logits, router[...])
        grad, d_gain = norm_back(residual_ref[...], gain[...], d_routed)
        d_residual = cot_ref[...].astype(F32) + grad
        d_res_ref[...] = d_residual
        d_branch_ref[...] = d_residual.astype(BF16)
        small_ref[:experts, :] = dot(d_logits, message_ref[:rows, :])
        small_ref[experts:, :] = jnp.broadcast_to(d_gain, (8, d_gain.shape[1]))

    d_mix_ref[...] = dot_nt(d_branch_ref[...], wo[...]).astype(BF16)


def back_through_branch(terms, residual, cot, gain, gates_t, router_t, message, wo, after=()):
    rows, width = residual.shape
    experts = gates_t.shape[0]
    tile = 256
    outs = (
        shaped((rows, width), F32),
        shaped((rows, width), BF16),
        shaped((experts + 8, width), F32),
    )
    d_mix = shaped((rows, wo.shape[0]), BF16)
    d_residual, d_branch, d_mix, small = kernel_call(
        13.8,
        functools.partial(back_body, len(terms)),
        (wo.shape[0] // tile,),
        [(a, whole(a)) for a in terms]
        + [(a, whole(a)) for a in (residual, cot, gain, gates_t, router_t, message)]
        + [(wo, pl.BlockSpec((tile, width), lambda i: (i, 0)))],
        [(s, whole(s)) for s in outs[:2]]
        + [(d_mix, pl.BlockSpec((rows, tile), lambda i: (0, i))), (outs[2], whole(outs[2]))],
        scratch=[pltpu.VMEM((rows + experts, width), F32)],
        after=after,
    )
    return d_residual, d_branch, d_mix, small


def output_body(starts, residual_ref, *refs):
    parts, out_ref = refs[:-1], refs[-1]
    cuts = sorted({0, residual_ref.shape[0], *starts})
    for low, high in zip(cuts[:-1], cuts[1:], strict=True):
        total = residual_ref[low:high, :]
        for part, start in zip(parts, starts, strict=True):
            if start <= low and high <= start + part.shape[0]:
                total = total + part[low - start : high - start, :].astype(F32)
        out_ref[low:high, :] = total.astype(BF16)


def layer_output(residual, terms, after=()):
    out = shaped(residual.shape, BF16)
    return kernel_call(
        5,
        functools.partial(output_body, tuple(start for _, start in terms)),
        (1,),
        [(a, whole(a)) for a in [residual] + [t for t, _ in terms]],
        [(out, whole(out))],
        after=after,
    )[0]


def key_value_back_body(members, held_ref, arrived_ref, cos_ref, sin_ref, own_ref, joined_ref):
    total = held_ref[...].astype(F32) + arrived_ref[...].astype(F32)
    kd = total.shape[1] // 2
    keys = [
        turn(total[:, h * HD : (h + 1) * HD], cos_ref[...], -sin_ref[...])
        for h in range(kd // HD)
    ]
    keys, values = jnp.concatenate(keys, axis=1), total[:, kd:]
    own_ref[:, :kd] = keys.astype(BF16)
    own_ref[:, kd:] = values.astype(BF16)
    part = kd // members
    joined = []
    for c in range(members):
        cols = slice(c * part, (c + 1) * part)
        joined += [keys[:, cols], values[:, cols]]
    joined_ref[...] = jnp.concatenate(joined, axis=1).astype(BF16)


def key_value_back(held, arrived, cos_wide, sin_wide, members):
    return kernel_call(
        2.6,
        functools.partial(key_value_back_body, members),
        (1,),
        [(a, whole(a)) for a in (held, arrived, cos_wide, sin_wide)],
        [(s, whole(s)) for s in [shaped(held.shape, BF16)] * 2],
    )


def finish_body(steps, dq_ref, dkv_ref, wq, wk, wv, x_ref, d_res_ref, gain, small_ref,
                d_hidden_ref, sums_ref, total):
    i = pl.program_id(0)
    kd = wk.shape[1]
    part = dot_nt(dq_ref[...], wq[...])
    part = part + dot_nt(dkv_ref[:, :kd], wk[...]) + dot_nt(dkv_ref[:, kd:], wv[...])
    total[:, column(i, part.shape[1])] = part

    @pl.when(i == steps - 1)
    def _():
        x = x_ref[...].astype(F32)
        grad, d_gain = norm_back(x, gain[...], total[...])
        d_hidden_ref[...] = d_res_ref[...] + grad
        lead = small_ref.shape[0] - 8
        sums_ref[:lead, :] = small_ref[:lead, :]
        row = lax.broadcasted_iota(jnp.int32, (8, 1), 0)
        sums_ref[lead:, :] = jnp.where(row == 1, d_gain, small_ref[lead:, :])


def finish(dq, dkv, wq, wk, wv, x, d_residual, gain, small, after=()):
    rows, width = x.shape
    tile = 256
    by_rows = lambda w: (w, pl.BlockSpec((tile, w.shape[1]), lambda i: (i, 0)))
    outs = (shaped((rows, width), F32), shaped(small.shape, F32))
    return kernel_call(
        13,
        functools.partial(finish_body, width // tile),
        (width // tile,),
        [(dq, whole(dq)), (dkv, whole(dkv)), by_rows(wq), by_rows(wk), by_rows(wv)]
        + [(a, whole(a)) for a in (x, d_residual, gain, small)],
        [(s, whole(s)) for s in outs],
        scratch=[pltpu.VMEM((rows, width), F32)],
        after=after,
    )


def per_device(
    hidden_in, cotangent, norm_attn, w_query, w_key, w_value, w_out, norm_ffn, w_router,
    w_gate, w_up, w_down, expert_ids, priority, prefix,
):
    group_count, span_len, width = hidden_in.shape
    row_count = group_count * span_len
    q_width, kv_width = w_query.shape[1], w_key.shape[1]
    kv_heads = kv_width // HD
    members, n_dp = lax.axis_size("expert"), lax.axis_size("dp")
    expert_count = w_router.shape[1]
    local_count = w_gate.shape[0]
    team_count = local_count // 2
    top_count = expert_ids.shape[3]
    slot_count = row_count * top_count * 5 // (expert_count * 4)
    capacity = 9 * row_count * members * top_count // (8 * expert_count)
    e_index, d_index = lax.axis_index("expert"), lax.axis_index("dp")
    parity = (d_index // TEAM_BIT) % 2
    first_local = parity * team_count
    first_expert = (e_index * local_count + first_local).reshape(1).astype(jnp.int32)
    e_steps = [("expert", bit) for bit in bits_of(members)]
    team = ("dp", TEAM_BIT)
    gain_one, gain_two = norm_attn.reshape(1, width), norm_ffn.reshape(1, width)
    router_t = w_router.T

    expert_range = jnp.arange(expert_count, dtype=jnp.int32)
    routes_t = expert_ids.reshape(row_count, top_count).T
    hit_t = jnp.any(routes_t[:, None, :] == expert_range[None, :, None], axis=0)
    tables = jnp.concatenate([routes_t, priority.reshape(1, row_count)], axis=0)[None]
    for axis_name, bit in [team] + e_steps:
        tables = jnp.concatenate([tables, swap(tables, axis_name, bit)], axis=0)

    offset = e_index * span_len
    positions = (offset + jnp.arange(span_len, dtype=jnp.int32)).astype(F32)
    frequency = ROPE_BASE ** (-(jnp.arange(HD // 2, dtype=F32) * 2.0 / HD))
    angles = positions[:, None] * frequency[None, :]
    cos_table, sin_table = jnp.cos(angles), jnp.sin(angles)
    cos_span = jnp.concatenate([cos_table, cos_table], axis=1)
    sin_span = jnp.concatenate([-sin_table, sin_table], axis=1)
    cos_wide, sin_wide = jnp.tile(cos_span, (group_count, 1)), jnp.tile(sin_span, (group_count, 1))
    x = hidden_in.reshape(row_count, width)
    cot = cotangent.reshape(row_count, width)
    normed, kv_own, queries, cot_later = project_inputs(
        x, gain_one, w_query, w_key, w_value, cos_wide, sin_wide, cot
    )
    kv = [kv_own.reshape(group_count, span_len, 2 * kv_width)]
    q = queries([tables])
    for number, (axis_name, bit) in enumerate(e_steps):
        arrived = [swap(piece, axis_name, bit) for piece in kv]
        kv = kv + arrived
    source = e_index ^ sum(
        ((jnp.arange(members) >> at) & 1) * bit for at, (_, bit) in enumerate(e_steps)
    )
    source = jnp.concatenate([source, offset.reshape(1)]).astype(jnp.int32)

    cut = row_count // 2

    far, near = ("expert", 2), ("expert", 1)

    def corner_of(over_z, over_y):
        return swap(over_z[:cut], *far), swap(over_y[cut:], *team)

    def over_near(piece):
        return tuple(swap(s, *near) for s in piece)

    def scatter_team(make):
        if members != 4:
            pieces = [make(at, [], 0)[0] for at in range(2 * members)]
            return [(scatter_pieces(pieces, [team] + e_steps), 0)]
        sent = {at: swap(make(at + 4, [], 0)[0], "expert", 1) for at in (3, 1, 2, 0)}
        low, high = make(3, [(sent[3], 0)], cut)
        from_y, from_z = swap(low, *far), swap(high, *team)
        own = make(0, [(sent[0], 0)], 0)[0]
        over_z = swap(make(1, [(sent[1], 0), (from_y, 0)], 0)[0], *team)
        over_y = swap(make(2, [(sent[2], 0), (from_z, cut)], 0)[0], *far)
        return [(own, 0), (over_z, 0), (over_y, 0)]

    split = members == 4
    if split:
        over_z = swap(hold(cot, [tables]), *team)
        cot_later = hold(cot_later, [tables, kv[1]])
        over_y = swap(cot_later, *far)
        near_own = over_near((cot,))
        cots = [(cot,), (over_z,), (over_y,)]
    else:
        cots = [(piece,) for piece in gather_pieces(cot, [team] + e_steps)]

    q = q.reshape(group_count, span_len, q_width)
    mix, lse = attend(q, kv, prefix, source)
    mix = mix.reshape(row_count, q_width)
    places = find_places(tables, first_expert, team_count, capacity, [mix])
    residual, message, gates_t = branch(
        x, mix, w_out, gain_two, router_t, hit_t.astype(F32), [over_z, over_y, places] if split else [places]
    )

    u_rows, gate_rows = {}, {}

    def send_rows(at, piece, after):
        u_rows[at], gate_rows[at] = dispatch(
            piece, at, places, first_expert, slot_count, True, after
        )

    if split:
        over_z, over_y = swap(message, *team), swap(message, *far)
        near_rows = over_near((message,))
    else:
        pieces = gather_pieces(message, [team] + e_steps)
    dz_rows = {}

    def own_rows(at, piece, after):
        dz_rows[at] = dispatch(piece, at, places, first_expert, slot_count, False, after)[0]
        return [dz_rows[at]]

    if split:
        over_cot_z, over_cot_y = (hold(cots[n][0], [places]) for n in (1, 2))
        corner = corner_of(over_cot_z, over_cot_y)
        near_z, near_y = over_near((over_cot_z,)), over_near((over_cot_y,))
        last = own_rows(0, cots[0], [places])
        last = own_rows(4, near_own, last)
        last = own_rows(1, (over_cot_z,), last)
        last = own_rows(2, (over_cot_y,), last)
        last = own_rows(5, near_z, last)
        last = own_rows(6, near_y, last)
        send_rows(0, (message,), last)
        send_rows(4, near_rows, [u_rows[0]])
        over_z, over_y = hold(over_z, [u_rows[4]]), hold(over_y, [u_rows[4]])
        corner_rows = corner_of(over_z, over_y)
        near_rows_z, near_rows_y = over_near((over_z,)), over_near((over_y,))
        send_rows(1, (over_z,), [])
        send_rows(2, (over_y,), [u_rows[1]])
        send_rows(5, near_rows_z, [u_rows[2]])
        send_rows(6, near_rows_y, [u_rows[5]])
        corner = tuple(hold(part, [u_rows[6]]) for part in corner)
        near_corner = over_near(corner)
        last = own_rows(3, corner, [u_rows[6]])
        corner_rows = tuple(hold(part, last) for part in corner_rows)
        near_corner_rows = over_near(corner_rows)
        last = own_rows(7, near_corner, last)
        send_rows(3, corner_rows, last)
        send_rows(7, near_corner_rows, [u_rows[3]])
    else:
        last = []
        for at, piece in enumerate(cots):
            last = own_rows(at, piece, last)
        for at, piece in enumerate(pieces):
            send_rows(at, (piece,), last)
    dz_rows = [dz_rows[at] for at in range(2 * members)]
    u_rows, gate_rows = ([rows[at] for at in range(2 * members)] for rows in (u_rows, gate_rows))
    d_order = [bit for bit in reversed(bits_of(n_dp)) if bit != TEAM_BIT] + [TEAM_BIT]
    kept_bits = sum(d_order[1:-1])
    me = (d_index - (d_index & kept_bits)).reshape(1).astype(jnp.int32)
    team_place = (d_index & TEAM_BIT).reshape(1).astype(jnp.int32)
    outs, backs, slopes, chains = [], [], [], []
    chunk = 8
    for e in range(team_count):
        expert = (first_local + e).reshape(1).astype(jnp.int32)
        joint = 0
        parts = []
        for start in range(0, len(u_rows), chunk):
            span = slice(start, start + chunk)
            parts.append(
                expert_pass(
                    e, expert, team_place if joint else me, u_rows[span], dz_rows[span], gate_rows[span],
                    w_gate, w_up, w_down, n_dp, d_order, joint, slopes[-1:],
                )
            )
        if len(parts) == 1:
            out, back, slope, *grads = parts[0]
        else:
            out, back, slope = (jnp.concatenate([p[i] for p in parts], axis=0) for i in range(3))
            grads = [
                sum(p[i].astype(F32) for p in parts).astype(BF16) for i in range(3, len(parts[0]))
            ]
        outs.append(out)
        backs.append(back)
        slopes.append(slope)
        chains.append(grads[0] if joint else (grads[0], swap(grads[1], "dp", d_order[0])))
    pairs = {
        bit: [[d, d + bit] for d in range(n_dp) if (d // bit) % 2 == 0] for bit in d_order[1:-1]
    }

    def advance(e, after):
        if e >= team_count:
            return list(after)
        if joint:
            ranks = [
                sum(bit for at, bit in enumerate(d_order[:-1]) if (n_dp // 4 >> at) & r)
                for r in range(n_dp // 2)
            ]
            groups = [[side * TEAM_BIT + r for r in ranks] for side in range(2)]
            chains[e] = lax.psum_scatter(
                hold(chains[e], after), "dp", scatter_dimension=0, tiled=True,
                axis_index_groups=groups,
            )
            return list(after)
        total = mark = add_blocks(*chains[e], after)
        for bit in d_order[1:-1]:
            total = lax.psum_scatter(
                total, "dp", scatter_dimension=0, tiled=True, axis_index_groups=pairs[bit]
            )
        chains[e] = total
        return [mark]

    extra = expert_count

    first_marks, marked = advance(0, slopes[-1:]), []

    def make_back(at, added, cut_at):
        parts = combine(
            backs, at, places, slopes, first_expert, added, cut_at, extra,
            first_marks if at >= members else (),
        )
        marked.append(parts[0])
        return parts

    back_terms = [term for term, _ in scatter_team(make_back)]
    marks = advance(1, marked[-3:])
    d_residual, d_branch, d_mix, small = back_through_branch(
        back_terms, residual, cot, gain_two, gates_t, router_t, message, w_out, marks
    )

    member_order = [bit for _, bit in reversed(e_steps)]
    member_places = [
        sum(((q >> (len(member_order) - 1 - at)) & 1) * bit for at, bit in enumerate(member_order))
        for q in range(members)
    ]
    grad_places = jnp.concatenate(
        [e_index ^ jnp.array(member_places, jnp.int32), d_index.reshape(1)]
    ).astype(jnp.int32)
    w_order = list(reversed(bits_of(n_dp)))
    w_steps = [("expert", bit) for bit in member_order] + [("dp", bit) for bit in w_order]
    q_part, kv_part = q_width // members, kv_width // members
    w_parts = []

    def add_weight(left, right, total_cols, start, after):
        buffers = w_parts[-1] if start else []
        w_parts.append(
            weight_grad(
                left, right, grad_places, n_dp, members, w_order,
                total_cols, start, buffers, after,
            )
        )

    marks = advance(2, [d_mix])

    def out_rows(at, added, cut_at, after):
        return combine(outs, at, places, None, first_expert, added, cut_at, 0, after)

    if split:
        nears = {at: out_rows(at + 4, [], 0, marks)[0] for at in (3, 1, 2, 0)}
        sent = {at: swap(rows, *near) for at, rows in nears.items()}
        marks = list(nears.values())
    dq, d_kv = attend_back(
        q, d_mix.reshape(group_count, span_len, q_width), lse, kv, prefix, source,
        cos_span, sin_span, marks,
    )
    dq = dq.reshape(row_count, q_width)
    settled = []

    def settle_expert(e, held, after):
        result = hold(chains[e], held)
        slots = jnp.stack([first_local + e, team_count - first_local + e]).astype(jnp.int32)
        totals = settled[-1] if settled else []
        other = swap(result[1], *team)
        settled.append(settle(result[0], other, slots, local_count, totals, after))

    marks, corners = [dq], []
    if split:
        low, high = out_rows(3, [(sent[3], 0)], cut, marks)
        from_y, from_z = corners = swap(low, *far), swap(high, *team)
        marks = [low]
    add_weight(mix, d_branch, 2 * q_part, 0, marks)
    add_weight(normed, dq, 2 * q_part, q_part, [])
    last_step = e_steps[0]
    halves = [scatter_pieces(d_kv[at::2], e_steps[1:]) for at in range(2)]
    held, far_half = (h.reshape(row_count, 2 * kv_width) for h in halves)
    arrived = hold(swap(far_half, *last_step), [w_parts[-1][0], *corners])
    d_kv_own, joined = key_value_back(held, arrived, cos_wide, sin_wide, members)
    marks = advance(3, [d_kv_own])
    if q_part % 128 == 0:
        w_keep, w_send = w_parts[1]
    else:
        w_keep, w_send = (jnp.concatenate([p[i] for p in w_parts], axis=3) for i in range(2))
    w_marks = []
    grads = reduce_grad(w_keep, w_send, w_steps, marks, w_marks)
    marks = w_marks[:1]
    if split:
        own = out_rows(0, [(sent[0], 0)], 0, marks)[0]
        over_z = out_rows(1, [(sent[1], 0), (from_y, 0)], 0, marks)[0]
        over_y = out_rows(2, [(sent[2], 0), (from_z, cut)], 0, marks)[0]
        out_terms = [(own, 0), (swap(over_z, *team), 0), (swap(over_y, *far), 0)]
        marks = [own, over_z, over_y]
    else:
        out_terms = scatter_team(lambda at, added, cut_at: out_rows(at, added, cut_at, marks))
    add_weight(normed, joined, 2 * kv_part, 0, [])
    d_hidden, sums = finish(
        dq, d_kv_own, w_query, w_key, w_value, x, d_residual, gain_one, small, [w_parts[-1][0]]
    )
    output = layer_output(residual, out_terms, [d_hidden, *w_marks[1:2]])
    sums = all_sum(hold(sums, [output]), ("expert",))
    sums = sums + swap(sums, "dp", w_order[0])
    early = max(1, team_count - 1)

    def late(mark):
        if not settled:
            for e in range(early):
                settle_expert(e, [d_hidden], [sums, mark])
        return settled[-1][:1]

    kv_keep, kv_send = w_parts[2]
    kv_grads = reduce_grad(kv_keep, hold(kv_send, [output]), w_steps, late=late)
    sums = hold(sums, late(output))
    for bit in w_order[1:]:
        sums = sums + swap(sums, "dp", bit)

    for e in range(early, team_count):
        settle_expert(e, [output], [])
    grad_gate, grad_up, grad_down = settled[-1]
    return (
        output.reshape(group_count, span_len, width),
        d_hidden.reshape(group_count, span_len, width),
        sums[expert_count + 1],
        grads[:, q_part:],
        kv_grads[:, :kv_part],
        kv_grads[:, kv_part:],
        grads[:, :q_part],
        sums[expert_count],
        sums[:expert_count].T,
        grad_gate,
        grad_up,
        grad_down,
    )


def solution(mesh):
    in_specs = (
        P("dp", "expert", None),
        P("dp", "expert", None),
        P(),
        P(),
        P(),
        P(),
        P(),
        P(),
        P(),
        P("expert", None, None),
        P("expert", None, None),
        P("expert", None, None),
        P(("dp", "expert"), None, None, None),
        P(("dp", "expert"), None, None),
        P("dp"),
    )
    out_specs = (
        P("dp", "expert", None),
        P("dp", "expert", None),
        P(),
        P("dp", "expert"),
        P("dp", "expert"),
        P("dp", "expert"),
        P("dp", "expert"),
        P(),
        P(),
        P("expert", "dp", None),
        P("expert", "dp", None),
        P("expert", "dp", None),
    )
    return jax.shard_map(
        per_device, mesh=mesh, in_specs=in_specs, out_specs=out_specs, check_vma=False
    )
```
